256 devices in a mesh: slab: 8 (over y, core), dom: 32 (over z, x).
Axes of the slice: x: 4, y: 4, z: 8, core: 2. Of those that a mesh axis runs over, the one named last changes fastest.
Arguments:
- positions: float32 [8192, 3, 128], P(('slab', 'dom')), may hold values from 0 to 1
- smoothing: float32 [8192, 128], P(('slab', 'dom')), may hold values from 0.35 to 1
- energy: float32 [8192, 128], P(('slab', 'dom')), may hold values from 0.2 to 2
- active: int32 [8192], P(('slab', 'dom')), may hold values from 1 to 128
- boundary: int32 [256, 8], P(('slab', 'dom')), may hold values from 0 to 31, as said below
- wanted: int32 [256, 32, 8], P(('slab', 'dom')), may hold values from 0 to 7, as said below
- cell_pairs: int32 [256, 448, 3], P(('slab', 'dom')), may hold values from 0 to 303, as said below
- pair_count: int32 [256], P(('slab', 'dom')), may hold values from 336 to 448, as said below
Outputs:
- density: float32 [8192, 128], P(('slab', 'dom'))
- acceleration: float32 [8192, 3, 128], P(('slab', 'dom'))
The draws below stay inside these ranges and needn't reach their ends.
Inputs may be any that keep to these rules, and one draw needn't show every extreme that they name: `boundary`: row e lists 8 distinct cells of device e, by their index among its 32 cells. The 8 entries of each row wanted[e, q] are distinct. `cell_pairs`: in each row (u, v, d): u is below 32, v is below 304 and differs from u, d is a neighbour direction from 0 to 26 other than 13. Every view index from 32 to 303 appears in some used row of every device. `pair_count`: some device evaluates 448 pairs.
All inputs are finite; a program needn't handle non-finite values.
Results may differ from the reference program's by a relative error of at most 0.0001.
Values sent between devices are 32-bit elements; how exact they have to be, the bound alone decides.
A program may use at most 64 MiB of HBM per device.

```python
import math
import jax
import jax.numpy as jnp
from jax import lax

CELL = 128
CPD = 32
SLOTS = 8
FACE = 8
BND = 8
PAIRS = 448
NCELLS = 8192
VIEW = 304
N_SLAB = 8
N_DOM = 32
DEVICES = 256


def draw_positions(key, part):
    key = jax.random.fold_in(key, 13)
    key_base = jax.random.fold_in(key, 0)
    base = jax.random.uniform(key_base, (NCELLS, 3, CELL), jnp.float32)
    return base


def draw_smoothing(key, part):
    key = jax.random.fold_in(key, 17)
    key_wide = jax.random.fold_in(key, 0)
    spread = jax.random.uniform(key_wide, (NCELLS, CELL), jnp.float32)
    wide = jnp.clip(0.35 * jnp.exp(spread * jnp.log(1.0 / 0.35)), 0.35, 1.0)
    return wide


def draw_boundary(key, part):
    key = jax.random.fold_in(key, 3)
    device_keys = jax.random.split(key, DEVICES)
    return jax.vmap(lambda single: jax.random.permutation(single, CPD)[:BND])(device_keys).astype(jnp.int32)


def draw_wanted(key, part):
    key = jax.random.fold_in(key, 11)
    row_keys = jax.random.split(key, DEVICES * N_DOM)
    rows = jax.vmap(lambda single: jax.random.permutation(single, BND)[:SLOTS])(row_keys)
    return rows.reshape(DEVICES, N_DOM, SLOTS).astype(jnp.int32)


def draw_cell_pairs(key, part):
    key = jax.random.fold_in(key, 5)
    key_first, key_step, key_direction, key_cover = jax.random.split(key, 4)
    first_local = jax.random.randint(key_first, (DEVICES, PAIRS), 0, CPD)
    second_local = (first_local + jax.random.randint(key_step, (DEVICES, PAIRS), 1, VIEW)) % VIEW
    cover_count = VIEW - CPD
    cover_keys = jax.random.split(key_cover, DEVICES)
    covered = jax.vmap(lambda single: jax.random.permutation(single, cover_count))(cover_keys) + CPD
    row_ids = jnp.arange(PAIRS, dtype=jnp.int32)[None, :]
    covered_full = jnp.concatenate([covered, jnp.zeros((DEVICES, PAIRS - cover_count), jnp.int32)], axis=1)
    second_local = jnp.where(row_ids < cover_count, covered_full, second_local)
    direction = jax.random.randint(key_direction, (DEVICES, PAIRS), 0, 26)
    direction = direction + (direction >= 13).astype(jnp.int32)
    return jnp.stack([first_local, second_local, direction], axis=2).astype(jnp.int32)


def draw_pair_count(key, part):
    key = jax.random.fold_in(key, 7)
    key_base, key_top = jax.random.split(key)
    counts = jax.random.randint(key_base, (DEVICES,), 3 * PAIRS // 4, PAIRS + 1)
    busiest = jax.random.randint(key_top, (), 0, DEVICES)
    return jnp.where(jnp.arange(DEVICES) == busiest, PAIRS, counts).astype(jnp.int32)


def touch_ends(values, own_key, smallest, largest):
    longest = values.shape.index(max(values.shape))
    spots = []
    for shift in (0, 1):
        where = [jax.random.randint(jax.random.fold_in(own_key, axis), (), 0, length) for axis, length in enumerate(values.shape)]
        where[longest] = (where[longest] + shift) % values.shape[longest]
        spots.append(tuple(where))
    return values.at[spots[0]].set(smallest).at[spots[1]].set(largest)


def level_of(own_key, shape, cuts, least, top_value):
    level = 1.0
    for axis_at, shards_of in cuts:
        heights = jax.random.uniform(jax.random.fold_in(jax.random.fold_in(own_key, 6), axis_at), (shards_of,), jnp.float32, least / len(cuts), top_value / len(cuts))
        level = level * jnp.repeat(jnp.exp(heights), shape[axis_at] // shards_of).reshape((-1,) + (1,) * (len(shape) - 1 - axis_at))
    return level


def setup_inputs(seed: int = 0) -> dict:
    arg_keys = jax.random.split(jax.random.key(seed), 9)
    return {
        "positions": draw_positions(jax.random.fold_in(arg_keys[8], 71), 0),
        "smoothing": draw_smoothing(jax.random.fold_in(arg_keys[8], 71), 0),
        "energy": jnp.clip(jnp.exp(math.log(2.0) - 2.3025851 * jax.random.uniform(arg_keys[2], (NCELLS, CELL), jnp.float32) ** level_of(arg_keys[2], (NCELLS, CELL), ((0, 256),), -0.2, 0.2)), 0.2, 2.0),
        "active": touch_ends(jax.random.randint(arg_keys[3], (NCELLS,), 1, CELL + 1), jax.random.fold_in(arg_keys[3], 1), 1, CELL).astype(jnp.int32),
        "boundary": draw_boundary(jax.random.fold_in(arg_keys[8], 71), 0),
        "wanted": draw_wanted(jax.random.fold_in(arg_keys[8], 71), 0),
        "cell_pairs": draw_cell_pairs(jax.random.fold_in(arg_keys[8], 71), 0),
        "pair_count": draw_pair_count(jax.random.fold_in(arg_keys[8], 71), 0),
    }


spline_norm = 21.0 / (2.0 * 3.141592653589793)
tile_group = 16

def direction_offsets(direction):
    return jnp.stack([direction // 9 - 1, direction // 3 % 3 - 1, direction % 3 - 1], axis=1).astype(jnp.float32)

def separations(left_cells, right_cells, offset_vec):
    separation = left_cells[:, :3, :, None] - right_cells[:, :3, None, :] - offset_vec[:, :, None, None]
    distance = jnp.sqrt(lax.optimization_barrier(jnp.sum(separation * separation, axis=1)))
    return (separation, distance)

def kernel_value(distance, radius):
    dist_ratio = distance / radius
    falloff = jnp.maximum(1.0 - dist_ratio, 0.0)
    return spline_norm / radius ** 3 * falloff ** 4 * (1.0 + 4.0 * dist_ratio)

def kernel_slope(distance, radius):
    falloff = jnp.maximum(1.0 - distance / radius, 0.0)
    return -20.0 * spline_norm / radius ** 5 * falloff ** 3

def density_terms(left_cells, right_cells, offset_vec):
    separation, distance = separations(left_cells, right_cells, offset_vec)
    cell_size = left_cells.shape[2]
    left_sum = lax.optimization_barrier(jnp.sum(kernel_value(distance, left_cells[:, 3, :, None]), axis=2)) / cell_size
    right_sum = lax.optimization_barrier(jnp.sum(kernel_value(distance, right_cells[:, 3, None, :]), axis=1)) / cell_size
    return (left_sum, right_sum)

def force_terms(left_cells, right_cells, offset_vec, left_factor, right_factor):
    separation, distance = separations(left_cells, right_cells, offset_vec)
    cell_size = left_cells.shape[2]
    pair_scale = left_factor[:, :, None] * kernel_slope(distance, left_cells[:, 3, :, None]) + right_factor[:, None, :] * kernel_slope(distance, right_cells[:, 3, None, :])
    pair_push = separation * pair_scale[:, None]
    return (-lax.optimization_barrier(jnp.sum(pair_push, axis=3)) / cell_size, lax.optimization_barrier(jnp.sum(pair_push, axis=2)) / cell_size)

def self_density(packed):
    groups = packed.reshape((-1, tile_group) + packed.shape[1:])
    zero_offset = jnp.zeros((tile_group, 3), jnp.float32)
    result = lax.map(lambda group_cells: density_terms(group_cells, group_cells, zero_offset)[0], groups)
    return result.reshape(packed.shape[0], packed.shape[2])

def self_force(packed, factor):
    groups = packed.reshape((-1, tile_group) + packed.shape[1:])
    factor_groups = factor.reshape(-1, tile_group, factor.shape[1])
    zero_offset = jnp.zeros((tile_group, 3), jnp.float32)

    def one_group(pieces):
        return force_terms(pieces[0], pieces[0], zero_offset, pieces[1], pieces[1])[0]
    result = lax.map(one_group, (groups, factor_groups))
    return result.reshape(packed.shape[0], 3, packed.shape[2])

def reference(positions, smoothing, energy, active, boundary, wanted, cell_pairs, pair_count):
    packed = jnp.concatenate([positions, smoothing[:, None, :]], axis=1)
    device_ids = jnp.arange(DEVICES, dtype=jnp.int32)
    slab_ids = device_ids // N_DOM
    dom_ids = device_ids % N_DOM
    first_local = cell_pairs[:, :, 0]
    second_local = cell_pairs[:, :, 1]
    direction = cell_pairs[:, :, 2]
    face_start = CPD + N_DOM * SLOTS
    slot_index = jnp.clip(second_local - CPD, 0, N_DOM * SLOTS - 1).astype(jnp.int32)
    peer_ids = (slab_ids * N_DOM)[:, None] + slot_index // SLOTS
    chosen_slot = jnp.take_along_axis(wanted.reshape(DEVICES, N_DOM * SLOTS), slot_index, axis=1)
    remote_cell = peer_ids * CPD + boundary[peer_ids, chosen_slot]
    face_index = jnp.clip(second_local - face_start, 0, 2 * FACE - 1).astype(jnp.int32)
    lower_ids = (slab_ids - 1) % N_SLAB * N_DOM + dom_ids
    upper_ids = (slab_ids + 1) % N_SLAB * N_DOM + dom_ids
    face_cell = jnp.where(face_index < FACE, lower_ids[:, None] * CPD + CPD - FACE + face_index, upper_ids[:, None] * CPD + face_index - FACE)
    own_first = device_ids[:, None] * CPD + first_local
    own_second = device_ids[:, None] * CPD + second_local
    second_cell = jnp.where(second_local < CPD, own_second, jnp.where(second_local < face_start, remote_cell, face_cell)).astype(jnp.int32)
    valid_mask = jnp.arange(PAIRS, dtype=jnp.int32)[None, :] < pair_count[:, None]
    offset_all = direction_offsets(direction.reshape(-1)).reshape(-1, tile_group, 3)
    left_ids = own_first.reshape(-1, tile_group).astype(jnp.int32)
    right_ids = second_cell.reshape(-1, tile_group)
    keep_mask = valid_mask.reshape(-1, tile_group).astype(jnp.float32)

    def add_density(summed, block_data):
        left_block, right_block, offset_vec, keep_block = block_data
        left_sum, right_sum = density_terms(packed[left_block], packed[right_block], offset_vec)
        summed = summed.at[left_block].add(left_sum * keep_block[:, None])
        return (summed.at[right_block].add(right_sum * keep_block[:, None]), None)
    density_all, unused_out = lax.scan(add_density, self_density(packed), (left_ids, right_ids, offset_all, keep_mask))
    factor = 2.0 / 3.0 * energy / density_all

    def add_force(summed, block_data):
        left_block, right_block, offset_vec, keep_block = block_data
        left_acc, right_acc = force_terms(packed[left_block], packed[right_block], offset_vec, factor[left_block], factor[right_block])
        summed = summed.at[left_block].add(left_acc * keep_block[:, None, None])
        return (summed.at[right_block].add(right_acc * keep_block[:, None, None]), None)
    accel_all, unused_out = lax.scan(add_force, self_force(packed, factor), (left_ids, right_ids, offset_all, keep_mask))
    live_mask = jnp.arange(CELL, dtype=jnp.int32)[None, :] < active[:, None]
    return (jnp.where(live_mask, density_all, 0.0), jnp.where(live_mask[:, None, :], accel_all, 0.0))
```

```python
import functools
import jax
import jax.numpy as jnp
import numpy as np
from jax import lax
from jax.experimental import pallas as pl
from jax.experimental.pallas import tpu as pltpu
from jax.sharding import PartitionSpec as P

CELL, CPD, NVIEW, GROUPS, PAIRS = 128, 32, 304, 38, 448
NORM = 21.0 / (2.0 * 3.141592653589793)
BF = jnp.bfloat16
F32 = jnp.float32
TINY = 1e-30
N_DOM, N_SLAB = 32, 8
MESH = pl.DeviceIdType.MESH
DEPTH = 80
NT = (((1,), (1,)), ((), ()))


def tables():
    shift = np.zeros((28, 32, 128), np.float32)
    scale = np.zeros((28, 32, 128), np.float32)
    for d in range(27):
        o = np.array([d // 9 - 1, d // 3 % 3 - 1, d % 3 - 1], np.float32)
        shift[d, 5:8, :] = -2.0 * o[:, None]
        shift[d, 12, :] = (o * o).sum()
        shift[d, 21:24, :] = -2.0 * o[:, None]
        for at in (0, 8, 24):
            scale[d, at : at + 3, :] = -o[:, None]
    shift[27, 12, :] = 16384.0
    sel = np.zeros((128, 32), np.float32)
    first, second, third, one = 0, 8, 24, 4
    for c in range(3):
        for part, base in ((first, 0), (second, 16), (third, 32)):
            sel[base + c, part + c] = -0.5
            sel[base + 5 + c, part + c] = -0.5
        sel[8 + c, first + c] = -0.5
        sel[24 + c, second + c] = -0.5
        sel[40 + c, first + c] = -0.5
        for base in (48, 56, 72):
            sel[base + c, one] = 1.0
    sel[3, one] = sel[11, one] = sel[12, one] = sel[43, one] = 1.0
    sel[4, first + 3] = sel[20, second + 3] = sel[36, third + 3] = 1.0
    eye = np.eye(128, dtype=np.float32)
    fan = np.zeros((128, 384), np.float32)
    for c in range(3):
        for base in (0, 16, 32):
            fan[base + c, c * 128 : (c + 1) * 128] = 1.0
    return tuple(jnp.asarray(t, BF) for t in (shift, scale, sel, eye, fan))


def view_row(view, c, v):
    return view[v // 8, c, pl.ds(lax.rem(v, 8), 1), :]


def spread_row(eye, row):
    total = jnp.zeros((CELL, CELL), F32)
    for _ in range(3):
        top = row.astype(BF)
        row = row - top.astype(F32)
        total += lax.dot_general(
            eye[...], jnp.broadcast_to(top, (CELL, CELL)), NT, preferred_element_type=F32
        )
    return total


def build_cell_tables(view, vv):
    row = lax.broadcasted_iota(jnp.int32, (8, CELL), 0)

    def one_cell(g, k):
        x, y, z = (
            jnp.broadcast_to(view[g, c, pl.ds(k, 1), :], (8, CELL)) - 0.5 for c in range(3)
        )
        n = x * x + y * y + z * z
        w = jnp.where(row == 3, n, jnp.where(row == 4, 1.0, 0.0))
        w = jnp.where(row == 0, -2.0 * x, w)
        w = jnp.where(row == 1, -2.0 * y, w)
        w = jnp.where(row == 2, -2.0 * z, w)
        t1 = w.astype(BF).astype(F32)
        r1 = w - t1
        t2 = r1.astype(BF).astype(F32)
        t3 = r1 - t2
        return jnp.concatenate([t1, t2, t1, t3], axis=0).astype(BF)

    def group(g, _):
        for k in range(8):
            vv[g * 8 + k] = one_cell(g, k)
        return 0

    lax.fori_loop(0, GROUPS, group, 0)


def right_operand(vv, shift, scale, v, d):
    cell = vv[v]
    moved = cell + shift[d]
    turned = cell * scale[d]
    return jnp.concatenate([moved[:16], moved[:16], moved[16:], turned], axis=0)


def dist2(at, vv, shift, scale, u, v, d):
    return jnp.dot(
        at[u, :, 0:DEPTH], right_operand(vv, shift, scale, v, d), preferred_element_type=F32
    )


def root(r2):
    r2 = jnp.maximum(r2, TINY)
    return r2 * lax.rsqrt(r2)


def fold_rows(w):
    return jnp.sum(w.reshape(-1, 8, CELL), axis=0)


def scalars(pairs, wanted, count, p):
    p = jnp.minimum(p, PAIRS - 1) if not isinstance(p, int) else p
    u = pairs[3 * p]
    v = pairs[3 * p + 1]
    d = jnp.where(p < count, pairs[3 * p + 2], 27)
    slot = jnp.clip(v - CPD, 0, 255)
    offered = CPD + (slot & -8) + wanted[slot]
    v = jnp.where((v >= CPD) & (v < CPD + 256), offered, v)
    return u, v, d


def density_kernel(
    unroll, rows,
    pairs, wanted, count, view, shift, scale, sel, eye, fan, out, vv, at, hb, acc_l, acc_r,
):
    build_cell_tables(view, vv)

    def left(g, _):
        for k in range(4):
            u = g * 4 + k
            picked = jnp.dot(sel[...], vv[u], preferred_element_type=F32).astype(BF)
            cols = lax.dot_general(eye[...], picked, NT, preferred_element_type=F32).astype(BF)
            at[u] = cols
            hb[u] = spread_row(eye, view_row(view, 3, u))
            acc_l[u] = jnp.zeros((CELL, CELL), F32)
        return 0

    lax.fori_loop(0, CPD // 4, left, 0)

    def clear(g, _):
        acc_r[pl.ds(g * 8, 8)] = jnp.zeros((8, 8, CELL), F32)
        return 0

    lax.fori_loop(0, GROUPS, clear, 0)
    d2 = functools.partial(dist2, at, vv, shift, scale)
    chunks = range(CELL // rows)

    def self_tile(u, r2):
        h_r = jnp.broadcast_to(view_row(view, 3, u), (rows, CELL))
        q_r = 1.25 * h_r
        total = jnp.zeros((8, CELL), F32)
        for c in chunks:
            r = root(r2[c * rows : c * rows + rows])
            f = jnp.maximum(h_r - r, 0.0)
            f2 = f * f
            total += fold_rows(f2 * f2 * (q_r - f))
        acc_r[u] = total

    def self_body(i, r2):
        for s in range(4):
            u = i * 4 + s
            after = jnp.minimum(u + 1, CPD - 1)
            ahead = d2(after, after, 13)
            self_tile(u, r2)
            r2 = ahead
        return r2

    lax.fori_loop(0, CPD // 4, self_body, d2(0, 0, 13))

    n = count[0]
    place = functools.partial(scalars, pairs, wanted, n)

    def tile(u, v, r2):
        h_r = jnp.broadcast_to(view_row(view, 3, v), (rows, CELL))
        q_r = 1.25 * h_r
        total = acc_r[v]
        for c in chunks:
            at_rows = pl.ds(c * rows, rows)
            r = root(r2[c * rows : c * rows + rows])
            h_l = hb[u, at_rows, :]
            f = jnp.maximum(h_l - r, 0.0)
            f2 = f * f
            acc_l[u, at_rows, :] += f2 * f2 * (1.25 * h_l - f)
            f = jnp.maximum(h_r - r, 0.0)
            f2 = f * f
            total += fold_rows(f2 * f2 * (q_r - f))
        acc_r[v] = total

    def body(i, carry):
        u, v, r2 = carry
        for s in range(unroll):
            u1, v1, d1 = place(i * unroll + s + 1)
            ahead = d2(u1, v1, d1)
            tile(u, v, r2)
            u, v, r2 = u1, v1, ahead
        return u, v, r2

    u, v, d = place(0)
    lax.fori_loop(0, pl.cdiv(n, unroll), body, (u, v, d2(u, v, d)))

    def finish(g, _):
        out[pl.ds(g * 8, 8), :] = jnp.sum(acc_r[pl.ds(g * 8, 8)], axis=1)
        return 0

    lax.fori_loop(0, GROUPS, finish, 0)
    lane = lax.broadcasted_iota(jnp.int32, (CELL, CELL), 1)

    def finish_left(u, table):
        total = jnp.sum(acc_l[u], axis=1, keepdims=True)
        return jnp.where(lane == u, total, table)

    table = lax.fori_loop(0, CPD, finish_left, jnp.zeros((CELL, CELL), F32))
    out[0:CPD, :] += table.T[0:CPD]


def force_kernel(
    unroll, rows,
    pairs, wanted, count, view, coef, shift, scale, sel, eye, fan, out,
    vv, at, hb, cb, xb, acc_l, acc_r,
):
    build_cell_tables(view, vv)

    def left(g, _):
        for k in range(4):
            u = g * 4 + k
            picked = jnp.dot(sel[...], vv[u], preferred_element_type=F32).astype(BF)
            cols = lax.dot_general(eye[...], picked, NT, preferred_element_type=F32).astype(BF)
            at[u] = cols
            spread = jnp.dot(cols, fan[...], preferred_element_type=F32)
            for c in range(3):
                xb[u, c] = spread[:, c * CELL : (c + 1) * CELL]
                acc_l[u, c] = jnp.zeros((CELL, CELL), F32)
            hb[u] = spread_row(eye, view_row(view, 3, u))
            cb[u] = spread_row(eye, coef[u // 8, pl.ds(lax.rem(u, 8), 1), :])
        return 0

    lax.fori_loop(0, CPD // 4, left, 0)

    def clear(g, _):
        for c in range(3):
            acc_r[c, pl.ds(g * 8, 8)] = jnp.zeros((8, 8, CELL), F32)
        return 0

    lax.fori_loop(0, GROUPS, clear, 0)
    d2 = functools.partial(dist2, at, vv, shift, scale)
    chunks = range(CELL // rows)

    def tile(u, v, d, r2, both):
        h_r = jnp.broadcast_to(view_row(view, 3, v), (rows, CELL))
        c_r = jnp.broadcast_to(coef[v // 8, pl.ds(lax.rem(v, 8), 1), :], (rows, CELL))
        offset = (d // 9 - 1, lax.rem(d // 3, 3) - 1, lax.rem(d, 3) - 1)
        x_r = [
            jnp.broadcast_to(view_row(view, c, v) + (offset[c].astype(F32) - 0.5), (rows, CELL))
            for c in range(3)
        ]
        total = [acc_r[c, v] for c in range(3)]
        for k in chunks:
            at_rows = pl.ds(k * rows, rows)
            r = root(r2[k * rows : k * rows + rows])
            f = jnp.maximum(hb[u, at_rows, :] - r, 0.0)
            s = f * f * (f * cb[u, at_rows, :])
            f = jnp.maximum(h_r - r, 0.0)
            s += f * f * (f * c_r)
            for c in range(3):
                push = s * (xb[u, c, at_rows, :] - x_r[c])
                if both:
                    acc_l[u, c, at_rows, :] += push
                total[c] += fold_rows(push)
        for c in range(3):
            acc_r[c, v] = total[c]

    def self_body(i, r2):
        for s in range(4):
            u = i * 4 + s
            after = jnp.minimum(u + 1, CPD - 1)
            ahead = d2(after, after, 13)
            tile(u, u, jnp.int32(13), r2, False)
            r2 = ahead
        return r2

    lax.fori_loop(0, CPD // 4, self_body, d2(0, 0, 13))

    n = count[0]
    place = functools.partial(scalars, pairs, wanted, n)

    def body(i, carry):
        u, v, d, r2 = carry
        for s in range(unroll):
            u1, v1, d1 = place(i * unroll + s + 1)
            ahead = d2(u1, v1, d1)
            tile(u, v, d, r2, True)
            u, v, d, r2 = u1, v1, d1, ahead
        return u, v, d, r2

    u, v, d = place(0)
    lax.fori_loop(0, pl.cdiv(n, unroll), body, (u, v, d, d2(u, v, d)))

    def finish(g, _):
        for c in range(3):
            out[g, c] = -jnp.sum(acc_r[c, pl.ds(g * 8, 8)], axis=1)
        return 0

    lax.fori_loop(0, GROUPS, finish, 0)
    lane = lax.broadcasted_iota(jnp.int32, (CELL, CELL), 1)
    for c in range(3):

        def finish_left(u, table):
            total = jnp.sum(acc_l[u, c], axis=1, keepdims=True)
            return jnp.where(lane == u, total, table)

        table = lax.fori_loop(0, CPD, finish_left, jnp.zeros((CELL, CELL), F32))
        turned = table.T
        for g in range(CPD // 8):
            out[g, c] += turned[g * 8 : g * 8 + 8]


SMEM = pl.BlockSpec(memory_space=pltpu.SMEM)
VMEM = pl.BlockSpec(memory_space=pltpu.VMEM)


def density_call(pairs, wanted, count, view, consts, unroll=2, rows=64):
    return pl.pallas_call(
        functools.partial(density_kernel, unroll, rows),
        out_shape=jax.ShapeDtypeStruct((NVIEW, CELL), F32),
        in_specs=[SMEM] * 3 + [VMEM] * 6,
        out_specs=VMEM,
        scratch_shapes=[
            pltpu.VMEM((NVIEW, 32, CELL), BF),
            pltpu.VMEM((CPD, CELL, CELL), BF),
            pltpu.VMEM((CPD, CELL, CELL), F32),
            pltpu.VMEM((CPD, CELL, CELL), F32),
            pltpu.VMEM((NVIEW, 8, CELL), F32),
        ],
        compiler_params=pltpu.CompilerParams(vmem_limit_bytes=48 << 20),
        name="density_pairs",
    )(pairs, wanted, count, view, *consts)


def force_call(pairs, wanted, count, view, coef, consts, unroll=2, rows=64):
    return pl.pallas_call(
        functools.partial(force_kernel, unroll, rows),
        out_shape=jax.ShapeDtypeStruct((GROUPS, 3, 8, CELL), F32),
        in_specs=[SMEM] * 3 + [VMEM] * 7,
        out_specs=VMEM,
        scratch_shapes=[
            pltpu.VMEM((NVIEW, 32, CELL), BF),
            pltpu.VMEM((CPD, CELL, CELL), BF),
            pltpu.VMEM((CPD, CELL, CELL), F32),
            pltpu.VMEM((CPD, CELL, CELL), F32),
            pltpu.VMEM((CPD, 3, CELL, CELL), F32),
            pltpu.VMEM((CPD, 3, CELL, CELL), F32),
            pltpu.VMEM((3, NVIEW, 8, CELL), F32),
        ],
        compiler_params=pltpu.CompilerParams(vmem_limit_bytes=48 << 20),
        name="force_pairs",
    )(pairs, wanted, count, view, coef, *consts)


def barrier():
    t, s = lax.axis_index("dom"), lax.axis_index("slab")
    sem = pltpu.get_barrier_semaphore()

    def greet(k, _):
        pl.semaphore_signal(
            sem, inc=1, device_id={"dom": lax.rem(t + k, N_DOM)}, device_id_type=MESH
        )
        return 0

    lax.fori_loop(1, N_DOM, greet, 0)
    for step in (1, N_SLAB - 1):
        pl.semaphore_signal(
            sem, inc=1, device_id={"slab": lax.rem(s + step, N_SLAB)}, device_id_type=MESH
        )
    pl.semaphore_wait(sem, N_DOM + 1)


class Swap:
    def __init__(self, peer_refs, lower_refs, upper_refs, send_sem, recv_sem):
        self.peer_refs, self.lower, self.upper = peer_refs, lower_refs, upper_refs
        self.send_sem, self.recv_sem = send_sem, recv_sem
        self.t, self.s = lax.axis_index("dom"), lax.axis_index("slab")

    def peer_copy(self, k):
        q = lax.rem(self.t + k, N_DOM)
        src, dst = self.peer_refs(q)
        return pltpu.make_async_remote_copy(
            src_ref=src, dst_ref=dst, send_sem=self.send_sem.at[k], recv_sem=self.recv_sem.at[k],
            device_id={"dom": q}, device_id_type=MESH,
        )

    def face_copy(self, which):
        src, dst = (self.lower, self.upper)[which]
        step = (N_SLAB - 1, 1)[which]
        at = (0, N_DOM)[which]
        return pltpu.make_async_remote_copy(
            src_ref=src, dst_ref=dst, send_sem=self.send_sem.at[at], recv_sem=self.recv_sem.at[at],
            device_id={"slab": lax.rem(self.s + step, N_SLAB)}, device_id_type=MESH,
        )

    def each(self, act):
        def one(k, _):
            act(self.peer_copy(k))
            return 0

        lax.fori_loop(1, N_DOM, one, 0)
        for which in (0, 1):
            act(self.face_copy(which))

    def start(self):
        self.each(lambda copy: copy.start())

    def wait_recv(self):
        self.each(lambda copy: copy.wait_recv())

    def wait_send(self):
        self.each(lambda copy: copy.wait_send())


def gather_kernel(boundary, positions, smoothing, view, offered, send_sem, recv_sem):
    t = lax.axis_index("dom")
    for g in range(CPD // 8):
        for c in range(3):
            view[g, c] = positions[g * 8 : g * 8 + 8, c, :]
        view[g, 3] = smoothing[g * 8 : g * 8 + 8, :]
    for b in range(8):
        cell = boundary[b]
        for c in range(4):
            offered[c, b : b + 1, :] = view_row(view, c, cell)
    view[CPD // 8 + t] = offered[...]
    barrier()
    swap = Swap(
        lambda q: (offered, view.at[CPD // 8 + t]),
        (view.at[0], view.at[GROUPS - 1]),
        (view.at[CPD // 8 - 1], view.at[GROUPS - 2]),
        send_sem, recv_sem,
    )
    swap.start()
    swap.wait_recv()
    swap.wait_send()


def settle(own, arrived, faces, boundary, parts=1):
    row = lax.broadcasted_iota(jnp.int32, (CPD, CELL), 0)
    for b in range(8):
        own += jnp.where(row == boundary[b], jnp.broadcast_to(arrived[b : b + 1], own.shape), 0.0)
    first = jnp.concatenate([own[:8] + faces[0], own[8:24], own[24:] + faces[1]], axis=0)
    return first


def factor_kernel(
    boundary, partial, smoothing, energy, rho, coef, arrived, offered, mine,
    send_sem, recv_sem, send_sem2, recv_sem2,
):
    t = lax.axis_index("dom")
    barrier()
    swap = Swap(
        lambda q: (partial.at[CPD // 8 + q], arrived.at[t]),
        (partial.at[GROUPS - 2], arrived.at[N_DOM + 1]),
        (partial.at[GROUPS - 1], arrived.at[N_DOM]),
        send_sem, recv_sem,
    )
    swap.start()
    arrived[t] = partial[CPD // 8 + t]
    swap.wait_recv()
    total = arrived[0]
    for q in range(1, N_DOM):
        total += arrived[q]
    own = partial[0 : CPD // 8].reshape(CPD, CELL)
    raw = settle(own, total, (arrived[N_DOM], arrived[N_DOM + 1]), boundary)
    h2 = smoothing[...] * smoothing[...]
    h4 = h2 * h2
    inverse = 1.0 / (h4 * h4)
    density = (4.0 * NORM / CELL) * inverse * raw
    rho[...] = density
    slope = (40.0 / 3.0 * NORM / CELL) * inverse * energy[...] / density
    for g in range(CPD // 8):
        coef[g] = slope[g * 8 : g * 8 + 8]
    mine[...] = slope
    for b in range(8):
        offered[b : b + 1, :] = mine[pl.ds(boundary[b], 1), :]
    coef[CPD // 8 + t] = offered[...]
    back = Swap(
        lambda q: (offered, coef.at[CPD // 8 + t]),
        (coef.at[0], coef.at[GROUPS - 1]),
        (coef.at[CPD // 8 - 1], coef.at[GROUPS - 2]),
        send_sem2, recv_sem2,
    )
    back.start()
    swap.wait_send()
    back.wait_recv()
    back.wait_send()


def settle_kernel(boundary, partial, accel, arrived, send_sem, recv_sem):
    t = lax.axis_index("dom")
    barrier()
    swap = Swap(
        lambda q: (partial.at[CPD // 8 + q], arrived.at[t]),
        (partial.at[GROUPS - 2], arrived.at[N_DOM + 1]),
        (partial.at[GROUPS - 1], arrived.at[N_DOM]),
        send_sem, recv_sem,
    )
    swap.start()
    arrived[t] = partial[CPD // 8 + t]
    swap.wait_recv()
    for c in range(3):
        total = arrived[0, c]
        for q in range(1, N_DOM):
            total += arrived[q, c]
        own = jnp.concatenate([partial[g, c] for g in range(CPD // 8)], axis=0)
        whole = settle(own, total, (arrived[N_DOM, c], arrived[N_DOM + 1, c]), boundary)
        accel[c] = whole
    swap.wait_send()


def comm_call(kernel, collective, out_shape, scratch, n_sems, operands):
    return pl.pallas_call(
        kernel,
        out_shape=out_shape,
        in_specs=[SMEM] + [VMEM] * (len(operands) - 1),
        out_specs=jax.tree.map(lambda _: VMEM, out_shape),
        scratch_shapes=scratch + [pltpu.SemaphoreType.DMA((N_DOM + 1,))] * n_sems,
        compiler_params=pltpu.CompilerParams(collective_id=collective, has_side_effects=True),
        name=kernel.__name__,
    )(*operands)


def per_device(positions, smoothing, energy, active, boundary, wanted, cell_pairs, pair_count):
    consts = tables()
    offers = boundary[0]
    pairs = cell_pairs.reshape(-1)
    taken = wanted.reshape(-1)
    shape = lambda *dims: jax.ShapeDtypeStruct(dims, F32)
    view = comm_call(
        gather_kernel, 0, shape(GROUPS, 4, 8, CELL), [pltpu.VMEM((4, 8, CELL), F32)], 2,
        (offers, positions, smoothing),
    )
    partial = density_call(pairs, taken, pair_count, view, consts, 8, 32)
    rho, coef = comm_call(
        factor_kernel, 1, (shape(CPD, CELL), shape(GROUPS, 8, CELL)),
        [
            pltpu.VMEM((N_DOM + 2, 8, CELL), F32),
            pltpu.VMEM((8, CELL), F32),
            pltpu.VMEM((CPD, CELL), F32),
        ],
        4,
        (offers, partial.reshape(GROUPS, 8, CELL), smoothing, energy),
    )
    force = force_call(pairs, taken, pair_count, view, coef, consts, 8, 32)
    accel = comm_call(
        settle_kernel, 2, shape(3, CPD, CELL), [pltpu.VMEM((N_DOM + 2, 3, 8, CELL), F32)], 2,
        (offers, force),
    )
    live = jnp.arange(CELL, dtype=jnp.int32)[None, :] < active[:, None]
    return (
        jnp.where(live, rho, 0.0),
        jnp.where(live[:, None, :], accel.transpose(1, 0, 2), 0.0),
    )


def solution(mesh):
    in_specs = (
        P(("slab", "dom"), None, None),
        P(("slab", "dom"), None),
        P(("slab", "dom"), None),
        P(("slab", "dom")),
        P(("slab", "dom"), None),
        P(("slab", "dom"), None, None),
        P(("slab", "dom"), None, None),
        P(("slab", "dom")),
    )
    out_specs = (P(("slab", "dom"), None), P(("slab", "dom"), None, None))
    return jax.shard_map(
        per_device, mesh=mesh, in_specs=in_specs, out_specs=out_specs, check_vma=False
    )
```

```python
import functools
import jax
import jax.numpy as jnp
import numpy as np
from jax import lax
from jax.experimental import pallas as pl
from jax.experimental.pallas import tpu as pltpu
from jax.sharding import PartitionSpec as P

CELL, CPD, NVIEW, GROUPS, PAIRS = 128, 32, 304, 38, 448
NORM = 21.0 / (2.0 * 3.141592653589793)
BF = jnp.bfloat16
F32 = jnp.float32
TINY = 1e-30
N_DOM, N_SLAB = 32, 8
MESH = pl.DeviceIdType.MESH
DEPTH = 80
NT = (((1,), (1,)), ((), ()))


def tables():
    shift = np.zeros((28, 32, 128), np.float32)
    scale = np.zeros((28, 32, 128), np.float32)
    for d in range(27):
        o = np.array([d // 9 - 1, d // 3 % 3 - 1, d % 3 - 1], np.float32)
        shift[d, 5:8, :] = -2.0 * o[:, None]
        shift[d, 12, :] = (o * o).sum()
        shift[d, 21:24, :] = -2.0 * o[:, None]
        for at in (0, 8, 24):
            scale[d, at : at + 3, :] = -o[:, None]
    shift[27, 12, :] = 16384.0
    sel = np.zeros((DEPTH, 32), np.float32)
    first, second, third, one = 0, 8, 24, 4
    for c in range(3):
        for part, base in ((first, 0), (second, 16), (third, 32)):
            sel[base + c, part + c] = -0.5
            sel[base + 5 + c, part + c] = -0.5
        sel[8 + c, first + c] = -0.5
        sel[24 + c, second + c] = -0.5
        sel[40 + c, first + c] = -0.5
        for base in (48, 56, 72):
            sel[base + c, one] = 1.0
    sel[3, one] = sel[11, one] = sel[12, one] = sel[43, one] = 1.0
    sel[4, first + 3] = sel[20, second + 3] = sel[36, third + 3] = 1.0
    eye = np.eye(128, dtype=np.float32)
    return tuple(jnp.asarray(t, BF) for t in (shift, scale, sel, eye))


def view_row(view, c, v):
    return view[v // 8, c, pl.ds(lax.rem(v, 8), 1), :]


def spread_columns(planes, put):
    turned = jnp.concatenate(planes, axis=0).T

    def some(g, turned):
        for k in range(4):
            for c in range(4):
                column = turned[:, c * CPD + k : c * CPD + k + 1]
                put(g * 4 + k, c, jnp.broadcast_to(column, (CELL, CELL)))
        return pltpu.roll(turned, CELL - 4, 1)

    lax.fori_loop(0, CPD // 4, some, turned)


def row_sums(load):
    lane = lax.broadcasted_iota(jnp.int32, (CELL, CELL), 1)

    def some(g, table):
        for k in range(8):
            u = g * 8 + k
            table = jnp.where(lane == u, jnp.sum(load(u), axis=1, keepdims=True), table)
        return table

    return lax.fori_loop(0, CPD // 8, some, jnp.zeros((CELL, CELL), F32)).T[0:CPD]


def own_plane(ref, *at):
    return jnp.concatenate([ref[(g, *at)] for g in range(CPD // 8)], axis=0)


def build_left(vv, sel, eye, at):
    def some(g, _):
        for k in range(8):
            u = g * 8 + k
            picked = jnp.dot(sel[...], vv[u], preferred_element_type=F32).astype(BF)
            cols = lax.dot_general(eye[...], picked, NT, preferred_element_type=F32)
            at[u] = cols.astype(BF)
        return 0

    lax.fori_loop(0, CPD // 8, some, 0)


def sweep(total, place, fill, use, buffers):
    half = len(buffers) // 2
    sides = buffers[:half], buffers[half:]

    def some(i, _):
        for side in (0, 1):
            for s in range(half):
                p = (2 * i + side) * half + s
                fill(sides[1 - side][s], place(p + half))
                use(place(p), sides[side][s])
        return 0

    for s in range(half):
        fill(sides[0][s], place(s))
    lax.fori_loop(0, pl.cdiv(total, 2 * half), some, 0)


def build_cell_tables(view, vv):
    row = lax.broadcasted_iota(jnp.int32, (8, CELL), 0)

    def one_cell(g, k):
        x, y, z = (
            jnp.broadcast_to(view[g, c, pl.ds(k, 1), :], (8, CELL)) - 0.5 for c in range(3)
        )
        n = x * x + y * y + z * z
        w = jnp.where(row == 3, n, jnp.where(row == 4, 1.0, 0.0))
        w = jnp.where(row == 0, -2.0 * x, w)
        w = jnp.where(row == 1, -2.0 * y, w)
        w = jnp.where(row == 2, -2.0 * z, w)
        t1 = w.astype(BF).astype(F32)
        r1 = w - t1
        t2 = r1.astype(BF).astype(F32)
        t3 = r1 - t2
        return jnp.concatenate([t1, t2, t1, t3], axis=0).astype(BF)

    def group(g, _):
        for k in range(8):
            vv[g * 8 + k] = one_cell(g, k)
        return 0

    lax.fori_loop(0, GROUPS, group, 0)


def right_operand(vv, shift, scale, v, d):
    cell = vv[v]
    moved = cell + shift[d]
    turned = cell * scale[d]
    return jnp.concatenate([moved[:16], moved[:16], moved[16:], turned], axis=0)


def dist2(at, vv, shift, scale, u, v, d):
    return jnp.dot(
        at[u], right_operand(vv, shift, scale, v, d), preferred_element_type=F32
    )


def root(r2):
    r2 = jnp.maximum(r2, TINY)
    return r2 * lax.rsqrt(r2)


def fold_rows(w):
    return jnp.sum(w.reshape(-1, 8, CELL), axis=0)


def scalars(pairs, wanted, count, p):
    p = jnp.minimum(p, PAIRS - 1) if not isinstance(p, int) else p
    u = pairs[3 * p]
    v = pairs[3 * p + 1]
    d = jnp.where(p < count, pairs[3 * p + 2], 27)
    slot = jnp.clip(v - CPD, 0, 255)
    offered = CPD + (slot & -8) + wanted[slot]
    v = jnp.where((v >= CPD) & (v < CPD + 256), offered, v)
    return u, v, d


def density_kernel(
    unroll, rows,
    pairs, wanted, count, view, shift, scale, sel, eye, out, vv, at, hb, hq, acc_l, acc_r, *buffers,
):
    build_cell_tables(view, vv)

    build_left(vv, sel, eye, at)

    def put(u, c, column):
        if c == 0:
            hb[u] = column
        elif c == 1:
            hq[u] = column
        elif c == 2:
            acc_l[u] = jnp.zeros((CELL, CELL), F32)

    h = own_plane(view, 3)
    spread_columns([h, 1.25 * h, h, h], put)

    def clear(g, _):
        acc_r[pl.ds(g * 8, 8)] = jnp.zeros((8, 8, CELL), F32)
        return 0

    lax.fori_loop(0, GROUPS, clear, 0)
    d2 = functools.partial(dist2, at, vv, shift, scale)
    chunks = range(CELL // rows)

    def fill(buffer, where):
        buffer[...] = d2(*where)

    def self_tile(where, r2):
        u = where[0]
        h_r = jnp.broadcast_to(view_row(view, 3, u), (rows, CELL))
        q_r = 1.25 * h_r
        total = jnp.zeros((8, CELL), F32)
        for c in chunks:
            r = root(r2[c * rows : c * rows + rows, :])
            f = jnp.maximum(h_r - r, 0.0)
            f2 = f * f
            total += fold_rows(f2 * f2 * (q_r - f))
        acc_r[u] = total

    def self_place(p):
        u = jnp.minimum(p, CPD - 1)
        return u, u, 13

    sweep(CPD, self_place, fill, self_tile, buffers)

    n = count[0]
    place = functools.partial(scalars, pairs, wanted, n)

    def tile(where, r2):
        u, v, _ = where
        h_r = jnp.broadcast_to(view_row(view, 3, v), (rows, CELL))
        q_r = 1.25 * h_r
        total = acc_r[v]
        for c in chunks:
            at_rows = pl.ds(c * rows, rows)
            r = root(r2[c * rows : c * rows + rows, :])
            f = jnp.maximum(hb[u, at_rows, :] - r, 0.0)
            f2 = f * f
            acc_l[u, at_rows, :] += f2 * f2 * (hq[u, at_rows, :] - f)
            f = jnp.maximum(h_r - r, 0.0)
            f2 = f * f
            total += fold_rows(f2 * f2 * (q_r - f))
        acc_r[v] = total

    sweep(n, place, fill, tile, buffers)

    def finish(g, _):
        out[pl.ds(g * 8, 8), :] = jnp.sum(acc_r[pl.ds(g * 8, 8)], axis=1)
        return 0

    lax.fori_loop(0, GROUPS, finish, 0)
    out[0:CPD, :] += row_sums(lambda u: acc_l[u])


def force_kernel(
    unroll, rows,
    pairs, wanted, count, active, view, coef, rho, shift, scale, sel, eye, out, density,
    vv, at, hb, cb, xb, acc_l, acc_r, *buffers,
):
    row = lax.broadcasted_iota(jnp.int32, (CPD, CELL), 0)
    live = jnp.zeros((CPD, CELL), jnp.int32)
    for u in range(CPD):
        live = jnp.where(row == u, active[u], live)
    lane = lax.broadcasted_iota(jnp.int32, (CPD, CELL), 1)
    density[...] = jnp.where(lane < live, rho[...], 0.0)
    build_cell_tables(view, vv)

    build_left(vv, sel, eye, at)

    def put(u, c, column):
        if c == 3:
            hb[u] = column
        else:
            xb[u, c] = column
            acc_l[u, c] = jnp.zeros((CELL, CELL), F32)

    def put_coef(u, c, column):
        if c == 0:
            cb[u] = column

    spread_columns([own_plane(view, c) - (0.5 if c < 3 else 0.0) for c in range(4)], put)
    spread_columns([own_plane(coef)] * 4, put_coef)

    def clear(g, _):
        for c in range(3):
            acc_r[c, pl.ds(g * 8, 8)] = jnp.zeros((8, 8, CELL), F32)
        return 0

    lax.fori_loop(0, GROUPS, clear, 0)
    d2 = functools.partial(dist2, at, vv, shift, scale)
    chunks = range(CELL // rows)

    def tile(both, where, r2):
        u, v, d = where
        h_r = jnp.broadcast_to(view_row(view, 3, v), (rows, CELL))
        c_r = jnp.broadcast_to(coef[v // 8, pl.ds(lax.rem(v, 8), 1), :], (rows, CELL))
        offset = (d // 9 - 1, lax.rem(d // 3, 3) - 1, lax.rem(d, 3) - 1)
        x_r = [
            jnp.broadcast_to(view_row(view, c, v) + (offset[c].astype(F32) - 0.5), (rows, CELL))
            for c in range(3)
        ]
        total = [acc_r[c, v] for c in range(3)]
        for k in chunks:
            at_rows = pl.ds(k * rows, rows)
            r = root(r2[k * rows : k * rows + rows, :])
            f = jnp.maximum(hb[u, at_rows, :] - r, 0.0)
            s = f * f * (f * cb[u, at_rows, :])
            f = jnp.maximum(h_r - r, 0.0)
            s += f * f * (f * c_r)
            for c in range(3):
                push = s * (xb[u, c, at_rows, :] - x_r[c])
                if both:
                    acc_l[u, c, at_rows, :] += push
                total[c] += fold_rows(push)
        for c in range(3):
            acc_r[c, v] = total[c]

    def fill(buffer, where):
        buffer[...] = d2(*where)

    def self_place(p):
        u = jnp.minimum(p, CPD - 1)
        return u, u, jnp.int32(13)

    sweep(CPD, self_place, fill, functools.partial(tile, False), buffers)

    n = count[0]
    place = functools.partial(scalars, pairs, wanted, n)

    sweep(n, place, fill, functools.partial(tile, True), buffers)

    def finish(g, _):
        for c in range(3):
            out[g, c] = -jnp.sum(acc_r[c, pl.ds(g * 8, 8)], axis=1)
        return 0

    lax.fori_loop(0, GROUPS, finish, 0)
    for c in range(3):
        turned = row_sums(lambda u: acc_l[u, c])
        for g in range(CPD // 8):
            out[g, c] += turned[g * 8 : g * 8 + 8]


SMEM = pl.BlockSpec(memory_space=pltpu.SMEM)
VMEM = pl.BlockSpec(memory_space=pltpu.VMEM)


def density_call(pairs, wanted, count, view, consts, unroll=2, rows=64):
    return pl.pallas_call(
        functools.partial(density_kernel, unroll, rows),
        out_shape=jax.ShapeDtypeStruct((NVIEW, CELL), F32),
        in_specs=[SMEM] * 3 + [VMEM] * 5,
        out_specs=VMEM,
        scratch_shapes=[
            pltpu.VMEM((NVIEW, 32, CELL), BF),
            pltpu.VMEM((CPD, CELL, DEPTH), BF),
            pltpu.VMEM((CPD, CELL, CELL), F32),
            pltpu.VMEM((CPD, CELL, CELL), F32),
            pltpu.VMEM((CPD, CELL, CELL), F32),
            pltpu.VMEM((NVIEW, 8, CELL), F32),
        ]
        + [pltpu.VMEM((CELL, CELL), F32)] * unroll,
        compiler_params=pltpu.CompilerParams(vmem_limit_bytes=48 << 20),
        name="density_pairs",
    )(pairs, wanted, count, view, *consts)


def force_call(pairs, wanted, count, view, coef, rho, active, consts, unroll=2, rows=64):
    return pl.pallas_call(
        functools.partial(force_kernel, unroll, rows),
        out_shape=(
            jax.ShapeDtypeStruct((GROUPS, 3, 8, CELL), F32),
            jax.ShapeDtypeStruct((CPD, CELL), F32),
        ),
        in_specs=[SMEM] * 4 + [VMEM] * 7,
        out_specs=(VMEM, VMEM),
        scratch_shapes=[
            pltpu.VMEM((NVIEW, 32, CELL), BF),
            pltpu.VMEM((CPD, CELL, DEPTH), BF),
            pltpu.VMEM((CPD, CELL, CELL), F32),
            pltpu.VMEM((CPD, CELL, CELL), F32),
            pltpu.VMEM((CPD, 3, CELL, CELL), F32),
            pltpu.VMEM((CPD, 3, CELL, CELL), F32),
            pltpu.VMEM((3, NVIEW, 8, CELL), F32),
        ]
        + [pltpu.VMEM((CELL, CELL), F32)] * unroll,
        compiler_params=pltpu.CompilerParams(vmem_limit_bytes=48 << 20),
        name="force_pairs",
    )(pairs, wanted, count, active, view, coef, rho, *consts)


def barrier():
    t, s = lax.axis_index("dom"), lax.axis_index("slab")
    sem = pltpu.get_barrier_semaphore()

    def greet(k, _):
        pl.semaphore_signal(
            sem, inc=1, device_id={"dom": lax.rem(t + k, N_DOM)}, device_id_type=MESH
        )
        return 0

    lax.fori_loop(1, N_DOM, greet, 0)
    for step in (1, N_SLAB - 1):
        pl.semaphore_signal(
            sem, inc=1, device_id={"slab": lax.rem(s + step, N_SLAB)}, device_id_type=MESH
        )
    pl.semaphore_wait(sem, N_DOM + 1)


class Swap:
    def __init__(self, peer_refs, lower_refs, upper_refs, send_sem, recv_sem):
        self.peer_refs, self.lower, self.upper = peer_refs, lower_refs, upper_refs
        self.send_sem, self.recv_sem = send_sem, recv_sem
        self.t, self.s = lax.axis_index("dom"), lax.axis_index("slab")

    def peer_copy(self, k):
        q = lax.rem(self.t + k, N_DOM)
        src, dst = self.peer_refs(q)
        return pltpu.make_async_remote_copy(
            src_ref=src, dst_ref=dst, send_sem=self.send_sem.at[k], recv_sem=self.recv_sem.at[k],
            device_id={"dom": q}, device_id_type=MESH,
        )

    def face_copy(self, which):
        src, dst = (self.lower, self.upper)[which]
        step = (N_SLAB - 1, 1)[which]
        at = (0, N_DOM)[which]
        return pltpu.make_async_remote_copy(
            src_ref=src, dst_ref=dst, send_sem=self.send_sem.at[at], recv_sem=self.recv_sem.at[at],
            device_id={"slab": lax.rem(self.s + step, N_SLAB)}, device_id_type=MESH,
        )

    def each(self, act):
        def one(k, _):
            act(self.peer_copy(k))
            return 0

        lax.fori_loop(1, N_DOM, one, 0)
        for which in (0, 1):
            act(self.face_copy(which))

    def start(self):
        self.each(lambda copy: copy.start())

    def wait_recv(self):
        self.each(lambda copy: copy.wait_recv())

    def wait_send(self):
        self.each(lambda copy: copy.wait_send())


def gather_kernel(boundary, positions, smoothing, view, offered, send_sem, recv_sem):
    t = lax.axis_index("dom")
    for g in range(CPD // 8):
        for c in range(3):
            view[g, c] = positions[g * 8 : g * 8 + 8, c, :]
        view[g, 3] = smoothing[g * 8 : g * 8 + 8, :]
    for b in range(8):
        cell = boundary[b]
        for c in range(4):
            offered[c, b : b + 1, :] = view_row(view, c, cell)
    view[CPD // 8 + t] = offered[...]
    barrier()
    swap = Swap(
        lambda q: (offered, view.at[CPD // 8 + t]),
        (view.at[0], view.at[GROUPS - 1]),
        (view.at[CPD // 8 - 1], view.at[GROUPS - 2]),
        send_sem, recv_sem,
    )
    swap.start()
    swap.wait_recv()
    swap.wait_send()


def settle(own, arrived, faces, boundary, parts=1):
    row = lax.broadcasted_iota(jnp.int32, (CPD, CELL), 0)
    for b in range(8):
        own += jnp.where(row == boundary[b], jnp.broadcast_to(arrived[b : b + 1], own.shape), 0.0)
    first = jnp.concatenate([own[:8] + faces[0], own[8:24], own[24:] + faces[1]], axis=0)
    return first


def factor_kernel(
    boundary, partial, smoothing, energy, rho, coef, arrived, offered, mine,
    send_sem, recv_sem, send_sem2, recv_sem2,
):
    t = lax.axis_index("dom")
    barrier()
    swap = Swap(
        lambda q: (partial.at[CPD // 8 + q], arrived.at[t]),
        (partial.at[GROUPS - 2], arrived.at[N_DOM + 1]),
        (partial.at[GROUPS - 1], arrived.at[N_DOM]),
        send_sem, recv_sem,
    )
    swap.start()
    arrived[t] = partial[CPD // 8 + t]
    swap.wait_recv()
    total = arrived[0]
    for q in range(1, N_DOM):
        total += arrived[q]
    own = partial[0 : CPD // 8].reshape(CPD, CELL)
    raw = settle(own, total, (arrived[N_DOM], arrived[N_DOM + 1]), boundary)
    h2 = smoothing[...] * smoothing[...]
    h4 = h2 * h2
    inverse = 1.0 / (h4 * h4)
    density = (4.0 * NORM / CELL) * inverse * raw
    rho[...] = density
    slope = (40.0 / 3.0 * NORM / CELL) * inverse * energy[...] / density
    for g in range(CPD // 8):
        coef[g] = slope[g * 8 : g * 8 + 8]
    mine[...] = slope
    for b in range(8):
        offered[b : b + 1, :] = mine[pl.ds(boundary[b], 1), :]
    coef[CPD // 8 + t] = offered[...]
    back = Swap(
        lambda q: (offered, coef.at[CPD // 8 + t]),
        (coef.at[0], coef.at[GROUPS - 1]),
        (coef.at[CPD // 8 - 1], coef.at[GROUPS - 2]),
        send_sem2, recv_sem2,
    )
    back.start()
    swap.wait_send()
    back.wait_recv()
    back.wait_send()


def settle_kernel(boundary, partial, accel, arrived, send_sem, recv_sem):
    t = lax.axis_index("dom")
    barrier()
    swap = Swap(
        lambda q: (partial.at[CPD // 8 + q], arrived.at[t]),
        (partial.at[GROUPS - 2], arrived.at[N_DOM + 1]),
        (partial.at[GROUPS - 1], arrived.at[N_DOM]),
        send_sem, recv_sem,
    )
    swap.start()
    arrived[t] = partial[CPD // 8 + t]
    swap.wait_recv()
    for c in range(3):
        total = arrived[0, c]
        for q in range(1, N_DOM):
            total += arrived[q, c]
        own = jnp.concatenate([partial[g, c] for g in range(CPD // 8)], axis=0)
        whole = settle(own, total, (arrived[N_DOM, c], arrived[N_DOM + 1, c]), boundary)
        accel[c] = whole
    swap.wait_send()


def comm_call(kernel, collective, out_shape, scratch, n_sems, operands):
    return pl.pallas_call(
        kernel,
        out_shape=out_shape,
        in_specs=[SMEM] + [VMEM] * (len(operands) - 1),
        out_specs=jax.tree.map(lambda _: VMEM, out_shape),
        scratch_shapes=scratch + [pltpu.SemaphoreType.DMA((N_DOM + 1,))] * n_sems,
        compiler_params=pltpu.CompilerParams(collective_id=collective, has_side_effects=True),
        name=kernel.__name__,
    )(*operands)


def per_device(positions, smoothing, energy, active, boundary, wanted, cell_pairs, pair_count):
    consts = tables()
    offers = boundary[0]
    pairs = cell_pairs.reshape(-1)
    taken = wanted.reshape(-1)
    shape = lambda *dims: jax.ShapeDtypeStruct(dims, F32)
    view = comm_call(
        gather_kernel, 0, shape(GROUPS, 4, 8, CELL), [pltpu.VMEM((4, 8, CELL), F32)], 2,
        (offers, positions, smoothing),
    )
    partial = density_call(pairs, taken, pair_count, view, consts, 16, 32)
    rho, coef = comm_call(
        factor_kernel, 1, (shape(CPD, CELL), shape(GROUPS, 8, CELL)),
        [
            pltpu.VMEM((N_DOM + 2, 8, CELL), F32),
            pltpu.VMEM((8, CELL), F32),
            pltpu.VMEM((CPD, CELL), F32),
        ],
        4,
        (offers, partial.reshape(GROUPS, 8, CELL), smoothing, energy),
    )
    force, density = force_call(pairs, taken, pair_count, view, coef, rho, active, consts, 16, 32)
    accel = comm_call(
        settle_kernel, 2, shape(3, CPD, CELL), [pltpu.VMEM((N_DOM + 2, 3, 8, CELL), F32)], 2,
        (offers, force),
    )
    live = jnp.arange(CELL, dtype=jnp.int32)[None, :] < active[:, None]
    return (
        density,
        jnp.where(live[:, None, :], accel.transpose(1, 0, 2), 0.0),
    )


def solution(mesh):
    in_specs = (
        P(("slab", "dom"), None, None),
        P(("slab", "dom"), None),
        P(("slab", "dom"), None),
        P(("slab", "dom")),
        P(("slab", "dom"), None),
        P(("slab", "dom"), None, None),
        P(("slab", "dom"), None, None),
        P(("slab", "dom")),
    )
    out_specs = (P(("slab", "dom"), None), P(("slab", "dom"), None, None))
    return jax.shard_map(
        per_device, mesh=mesh, in_specs=in_specs, out_specs=out_specs, check_vma=False
    )
```

```python
import functools
import jax
import jax.numpy as jnp
import numpy as np
from jax import lax
from jax.experimental import pallas as pl
from jax.experimental.pallas import tpu as pltpu
from jax.sharding import PartitionSpec as P

CELL, CPD, NVIEW, GROUPS, PAIRS = 128, 32, 304, 38, 448
NORM = 21.0 / (2.0 * 3.141592653589793)
BF = jnp.bfloat16
F32 = jnp.float32
TINY = 1e-30
N_Z, N_X, N_SLAB = 8, 4, 8
MESH = pl.DeviceIdType.MESH
DEPTH = 80
NT = (((1,), (1,)), ((), ()))


def tables():
    shift = np.zeros((28, 32, 128), np.float32)
    scale = np.zeros((28, 32, 128), np.float32)
    for d in range(27):
        o = np.array([d // 9 - 1, d // 3 % 3 - 1, d % 3 - 1], np.float32)
        shift[d, 5:8, :] = -2.0 * o[:, None]
        shift[d, 12, :] = (o * o).sum()
        shift[d, 21:24, :] = -2.0 * o[:, None]
        for at in (0, 8, 24):
            scale[d, at : at + 3, :] = -o[:, None]
    shift[27, 12, :] = 16384.0
    sel = np.zeros((DEPTH, 32), np.float32)
    first, second, third, one = 0, 8, 24, 4
    for c in range(3):
        for part, base in ((first, 0), (second, 16), (third, 32)):
            sel[base + c, part + c] = -0.5
            sel[base + 5 + c, part + c] = -0.5
        sel[8 + c, first + c] = -0.5
        sel[24 + c, second + c] = -0.5
        sel[40 + c, first + c] = -0.5
        for base in (48, 56, 72):
            sel[base + c, one] = 1.0
    sel[3, one] = sel[11, one] = sel[12, one] = sel[43, one] = 1.0
    sel[4, first + 3] = sel[20, second + 3] = sel[36, third + 3] = 1.0
    eye = np.eye(128, dtype=np.float32)
    return tuple(jnp.asarray(t, BF) for t in (shift, scale, sel, eye))


def view_row(view, c, v):
    return view[v // 8, c, pl.ds(lax.rem(v, 8), 1), :]


def spread_columns(planes, put):
    turned = jnp.concatenate(planes, axis=0).T

    def some(g, turned):
        for k in range(4):
            for c in range(4):
                column = turned[:, c * CPD + k : c * CPD + k + 1]
                put(g * 4 + k, c, jnp.broadcast_to(column, (CELL, CELL)))
        return pltpu.roll(turned, CELL - 4, 1)

    lax.fori_loop(0, CPD // 4, some, turned)


def row_sums(load):
    lane = lax.broadcasted_iota(jnp.int32, (CELL, CELL), 1)

    def some(g, table):
        for k in range(8):
            u = g * 8 + k
            table = jnp.where(lane == u, jnp.sum(load(u), axis=1, keepdims=True), table)
        return table

    return lax.fori_loop(0, CPD // 8, some, jnp.zeros((CELL, CELL), F32)).T[0:CPD]


def own_plane(ref, *at):
    return jnp.concatenate([ref[(g, *at)] for g in range(CPD // 8)], axis=0)


def build_left(vv, sel, eye, at):
    def some(g, _):
        for k in range(8):
            u = g * 8 + k
            picked = jnp.dot(sel[...], vv[u], preferred_element_type=F32).astype(BF)
            cols = lax.dot_general(eye[...], picked, NT, preferred_element_type=F32)
            at[u] = cols.astype(BF)
        return 0

    lax.fori_loop(0, CPD // 8, some, 0)


def sweep(total, place, fill, use, buffers):
    half = len(buffers) // 2
    sides = buffers[:half], buffers[half:]

    def some(i, _):
        for side in (0, 1):
            for s in range(half):
                p = (2 * i + side) * half + s
                fill(sides[1 - side][s], place(p + half))
                use(place(p), sides[side][s])
        return 0

    for s in range(half):
        fill(sides[0][s], place(s))
    lax.fori_loop(0, pl.cdiv(total, 2 * half), some, 0)


def build_cell_tables(view, vv):
    row = lax.broadcasted_iota(jnp.int32, (8, CELL), 0)

    def one_cell(g, k):
        x, y, z = (
            jnp.broadcast_to(view[g, c, pl.ds(k, 1), :], (8, CELL)) - 0.5 for c in range(3)
        )
        n = x * x + y * y + z * z
        w = jnp.where(row == 3, n, jnp.where(row == 4, 1.0, 0.0))
        w = jnp.where(row == 0, -2.0 * x, w)
        w = jnp.where(row == 1, -2.0 * y, w)
        w = jnp.where(row == 2, -2.0 * z, w)
        t1 = w.astype(BF).astype(F32)
        r1 = w - t1
        t2 = r1.astype(BF).astype(F32)
        t3 = r1 - t2
        return jnp.concatenate([t1, t2, t1, t3], axis=0).astype(BF)

    def group(g, _):
        for k in range(8):
            vv[g * 8 + k] = one_cell(g, k)
        return 0

    lax.fori_loop(0, GROUPS, group, 0)


def right_operand(vv, shift, scale, v, d):
    cell = vv[v]
    moved = cell + shift[d]
    turned = cell * scale[d]
    return jnp.concatenate([moved[:16], moved[:16], moved[16:], turned], axis=0)


def dist2(at, vv, shift, scale, u, v, d):
    return jnp.dot(
        at[u], right_operand(vv, shift, scale, v, d), preferred_element_type=F32
    )


def root(r2):
    r2 = jnp.maximum(r2, TINY)
    return r2 * lax.rsqrt(r2)


def fold_rows(w):
    return jnp.sum(w.reshape(-1, 8, CELL), axis=0)


def scalars(pairs, wanted, count, p):
    p = jnp.minimum(p, PAIRS - 1) if not isinstance(p, int) else p
    u = pairs[3 * p]
    v = pairs[3 * p + 1]
    d = jnp.where(p < count, pairs[3 * p + 2], 27)
    slot = jnp.clip(v - CPD, 0, 255)
    q = slot >> 3
    offered = CPD + (q & 3) * 64 + (q >> 2) * 8 + wanted[slot]
    v = jnp.where((v >= CPD) & (v < CPD + 256), offered, v)
    return u, v, d


def density_kernel(
    unroll, rows,
    pairs, wanted, count, view, shift, scale, sel, eye, out, vv, at, hb, hq, acc_l, acc_r, *buffers,
):
    build_cell_tables(view, vv)

    build_left(vv, sel, eye, at)

    def put(u, c, column):
        if c == 0:
            hb[u] = column
        elif c == 1:
            hq[u] = column
        elif c == 2:
            acc_l[u] = jnp.zeros((CELL, CELL), F32)

    h = own_plane(view, 3)
    spread_columns([h, 1.25 * h, h, h], put)

    def clear(g, _):
        acc_r[pl.ds(g * 8, 8)] = jnp.zeros((8, 8, CELL), F32)
        return 0

    lax.fori_loop(0, GROUPS, clear, 0)
    d2 = functools.partial(dist2, at, vv, shift, scale)
    chunks = range(CELL // rows)

    def fill(buffer, where):
        buffer[...] = d2(*where)

    def self_tile(where, r2):
        u = where[0]
        h_r = jnp.broadcast_to(view_row(view, 3, u), (rows, CELL))
        q_r = 1.25 * h_r
        total = jnp.zeros((8, CELL), F32)
        for c in chunks:
            r = root(r2[c * rows : c * rows + rows, :])
            f = jnp.maximum(h_r - r, 0.0)
            f2 = f * f
            total += fold_rows(f2 * f2 * (q_r - f))
        acc_r[u] = total

    def self_place(p):
        u = jnp.minimum(p, CPD - 1)
        return u, u, 13

    sweep(CPD, self_place, fill, self_tile, buffers)

    n = count[0]
    place = functools.partial(scalars, pairs, wanted, n)

    def tile(where, r2):
        u, v, _ = where
        h_r = jnp.broadcast_to(view_row(view, 3, v), (rows, CELL))
        q_r = 1.25 * h_r
        total = acc_r[v]
        for c in chunks:
            at_rows = pl.ds(c * rows, rows)
            r = root(r2[c * rows : c * rows + rows, :])
            f = jnp.maximum(hb[u, at_rows, :] - r, 0.0)
            f2 = f * f
            acc_l[u, at_rows, :] += f2 * f2 * (hq[u, at_rows, :] - f)
            f = jnp.maximum(h_r - r, 0.0)
            f2 = f * f
            total += fold_rows(f2 * f2 * (q_r - f))
        acc_r[v] = total

    sweep(n, place, fill, tile, buffers)

    def finish(g, _):
        out[pl.ds(g * 8, 8), :] = jnp.sum(acc_r[pl.ds(g * 8, 8)], axis=1)
        return 0

    lax.fori_loop(0, GROUPS, finish, 0)
    out[0:CPD, :] += row_sums(lambda u: acc_l[u])


def force_kernel(
    unroll, rows,
    pairs, wanted, count, active, view, coef, rho, shift, scale, sel, eye, out, density,
    vv, at, hb, cb, xb, acc_l, acc_r, *buffers,
):
    row = lax.broadcasted_iota(jnp.int32, (CPD, CELL), 0)
    live = jnp.zeros((CPD, CELL), jnp.int32)
    for u in range(CPD):
        live = jnp.where(row == u, active[u], live)
    lane = lax.broadcasted_iota(jnp.int32, (CPD, CELL), 1)
    density[...] = jnp.where(lane < live, rho[...], 0.0)
    build_cell_tables(view, vv)

    build_left(vv, sel, eye, at)

    def put(u, c, column):
        if c == 3:
            hb[u] = column
        else:
            xb[u, c] = column
            acc_l[u, c] = jnp.zeros((CELL, CELL), F32)

    def put_coef(u, c, column):
        if c == 0:
            cb[u] = column

    spread_columns([own_plane(view, c) - (0.5 if c < 3 else 0.0) for c in range(4)], put)
    spread_columns([own_plane(coef)] * 4, put_coef)

    def clear(g, _):
        for c in range(3):
            acc_r[c, pl.ds(g * 8, 8)] = jnp.zeros((8, 8, CELL), F32)
        return 0

    lax.fori_loop(0, GROUPS, clear, 0)
    d2 = functools.partial(dist2, at, vv, shift, scale)
    chunks = range(CELL // rows)

    def tile(both, where, r2):
        u, v, d = where
        h_r = jnp.broadcast_to(view_row(view, 3, v), (rows, CELL))
        c_r = jnp.broadcast_to(coef[v // 8, pl.ds(lax.rem(v, 8), 1), :], (rows, CELL))
        offset = (d // 9 - 1, lax.rem(d // 3, 3) - 1, lax.rem(d, 3) - 1)
        x_r = [
            jnp.broadcast_to(view_row(view, c, v) + (offset[c].astype(F32) - 0.5), (rows, CELL))
            for c in range(3)
        ]
        total = [acc_r[c, v] for c in range(3)]
        for k in chunks:
            at_rows = pl.ds(k * rows, rows)
            r = root(r2[k * rows : k * rows + rows, :])
            f = jnp.maximum(hb[u, at_rows, :] - r, 0.0)
            s = f * f * (f * cb[u, at_rows, :])
            f = jnp.maximum(h_r - r, 0.0)
            s += f * f * (f * c_r)
            for c in range(3):
                push = s * (xb[u, c, at_rows, :] - x_r[c])
                if both:
                    acc_l[u, c, at_rows, :] += push
                total[c] += fold_rows(push)
        for c in range(3):
            acc_r[c, v] = total[c]

    def fill(buffer, where):
        buffer[...] = d2(*where)

    def self_place(p):
        u = jnp.minimum(p, CPD - 1)
        return u, u, jnp.int32(13)

    sweep(CPD, self_place, fill, functools.partial(tile, False), buffers)

    n = count[0]
    place = functools.partial(scalars, pairs, wanted, n)

    sweep(n, place, fill, functools.partial(tile, True), buffers)

    def finish(g, _):
        for c in range(3):
            out[g, c] = -jnp.sum(acc_r[c, pl.ds(g * 8, 8)], axis=1)
        return 0

    lax.fori_loop(0, GROUPS, finish, 0)
    for c in range(3):
        turned = row_sums(lambda u: acc_l[u, c])
        for g in range(CPD // 8):
            out[g, c] += turned[g * 8 : g * 8 + 8]


SMEM = pl.BlockSpec(memory_space=pltpu.SMEM)
VMEM = pl.BlockSpec(memory_space=pltpu.VMEM)


def density_call(pairs, wanted, count, view, consts, unroll=2, rows=64):
    return pl.pallas_call(
        functools.partial(density_kernel, unroll, rows),
        out_shape=jax.ShapeDtypeStruct((NVIEW, CELL), F32),
        in_specs=[SMEM] * 3 + [VMEM] * 5,
        out_specs=VMEM,
        scratch_shapes=[
            pltpu.VMEM((NVIEW, 32, CELL), BF),
            pltpu.VMEM((CPD, CELL, DEPTH), BF),
            pltpu.VMEM((CPD, CELL, CELL), F32),
            pltpu.VMEM((CPD, CELL, CELL), F32),
            pltpu.VMEM((CPD, CELL, CELL), F32),
            pltpu.VMEM((NVIEW, 8, CELL), F32),
        ]
        + [pltpu.VMEM((CELL, CELL), F32)] * unroll,
        compiler_params=pltpu.CompilerParams(vmem_limit_bytes=48 << 20),
        name="density_pairs",
    )(pairs, wanted, count, view, *consts)


def force_call(pairs, wanted, count, view, coef, rho, active, consts, unroll=2, rows=64):
    return pl.pallas_call(
        functools.partial(force_kernel, unroll, rows),
        out_shape=(
            jax.ShapeDtypeStruct((GROUPS, 3, 8, CELL), F32),
            jax.ShapeDtypeStruct((CPD, CELL), F32),
        ),
        in_specs=[SMEM] * 4 + [VMEM] * 7,
        out_specs=(VMEM, VMEM),
        scratch_shapes=[
            pltpu.VMEM((NVIEW, 32, CELL), BF),
            pltpu.VMEM((CPD, CELL, DEPTH), BF),
            pltpu.VMEM((CPD, CELL, CELL), F32),
            pltpu.VMEM((CPD, CELL, CELL), F32),
            pltpu.VMEM((CPD, 3, CELL, CELL), F32),
            pltpu.VMEM((CPD, 3, CELL, CELL), F32),
            pltpu.VMEM((3, NVIEW, 8, CELL), F32),
        ]
        + [pltpu.VMEM((CELL, CELL), F32)] * unroll,
        compiler_params=pltpu.CompilerParams(vmem_limit_bytes=48 << 20),
        name="force_pairs",
    )(pairs, wanted, count, active, view, coef, rho, *consts)


def spot():
    t = lax.axis_index("dom")
    return t // N_X, lax.rem(t, N_X), lax.axis_index("slab")


def group_of(z, x):
    return CPD // 8 + x * N_Z + z


def barrier():
    z, x, s = spot()
    sem = pltpu.get_barrier_semaphore()
    peers = [{"dom": ((z + k) & (N_Z - 1)) * N_X + x} for k in range(1, N_Z)]
    peers += [{"dom": z * N_X + ((x + k) & (N_X - 1))} for k in range(1, N_X)]
    peers += [{"slab": (s + k) & (N_SLAB - 1)} for k in (1, N_SLAB - 1)]
    for peer in peers:
        pl.semaphore_signal(sem, inc=1, device_id=peer, device_id_type=MESH)
    pl.semaphore_wait(sem, len(peers))


def copy_to(src, dst, sems, k, peer):
    return pltpu.make_async_remote_copy(
        src_ref=src, dst_ref=dst, send_sem=sems[0].at[k], recv_sem=sems[1].at[k],
        device_id=peer, device_id_type=MESH,
    )


def z_copies(refs, sems):
    z, x, _ = spot()
    out = []
    for k in (4, 3, 5, 2, 6, 1, 7):
        to = (z + k) & (N_Z - 1)
        out.append((k, copy_to(*refs(to), sems, k, {"dom": to * N_X + x})))
    return dict(out)


def x_copies(refs, sems, base=0):
    z, x, _ = spot()
    out = []
    for k in (2, 1, 3):
        to = (x + k) & (N_X - 1)
        out.append(copy_to(*refs(to), sems, base + k, {"dom": z * N_X + to}))
    return out


def face_copies(lower, upper, sems):
    s = lax.axis_index("slab")
    return [
        copy_to(*lower, sems, 0, {"slab": (s + N_SLAB - 1) & (N_SLAB - 1)}),
        copy_to(*upper, sems, 1, {"slab": (s + 1) & (N_SLAB - 1)}),
    ]


def start(copies):
    for copy in copies:
        copy.start()


def arrive(copies):
    for copy in copies:
        copy.wait_recv()


def leave(copies):
    for copy in copies:
        copy.wait_send()


def gather_kernel(boundary, positions, smoothing, view, offered, *sems):
    z, x, _ = spot()
    face_sems, z_sems, x_sems = sems[:2], sems[2:4], sems[4:6]
    for g in range(CPD // 8):
        for c in range(3):
            view[g, c] = positions[g * 8 : g * 8 + 8, c, :]
        view[g, 3] = smoothing[g * 8 : g * 8 + 8, :]
    for b in range(8):
        cell = boundary[b]
        for c in range(4):
            offered[c, b : b + 1, :] = view_row(view, c, cell)
    here = group_of(z, x)
    view[here] = offered[...]
    barrier()
    along_z = z_copies(lambda to: (offered, view.at[here]), z_sems)
    faces = face_copies(
        (view.at[0], view.at[GROUPS - 1]), (view.at[CPD // 8 - 1], view.at[GROUPS - 2]), face_sems
    )
    start(along_z.values())
    along_x = x_copies(lambda to: (offered, view.at[here]), x_sems)
    start(along_x)
    start(faces)
    for k in (1, 7, 2, 6, 3, 5, 4):
        along_z[k].wait_recv()
        block = view.at[group_of((z - k) & (N_Z - 1), x)]
        onward = x_copies(lambda to: (block, block), x_sems, k * N_X)
        start(onward)
        along_x += onward
    arrive(along_x + faces)
    leave(list(along_z.values()) + along_x + faces)


def settle(own, arrived, lower, upper, boundary):
    row = lax.broadcasted_iota(jnp.int32, (CPD, CELL), 0)
    for b in range(8):
        own += jnp.where(row == boundary[b], jnp.broadcast_to(arrived[b : b + 1], own.shape), 0.0)
    return jnp.concatenate([own[:8] + lower, own[8:24], own[24:] + upper], axis=0)


def sum_back(partial, from_x, column, from_z, faces, sems):
    z, x, _ = spot()
    face_sems, x_sems, z_sems = sems[:2], sems[2:4], sems[4:6]
    along_x = x_copies(
        lambda to: (partial.at[pl.ds(group_of(0, to), N_Z)], from_x.at[x]), x_sems
    )
    across = face_copies(
        (partial.at[GROUPS - 2], faces.at[1]), (partial.at[GROUPS - 1], faces.at[0]), face_sems
    )
    start(along_x)
    start(across)
    total = partial[pl.ds(group_of(0, x), N_Z)]
    arrive(along_x)
    for k in range(1, N_X):
        total += from_x[(x + k) & (N_X - 1)]
    column[...] = total
    along_z = z_copies(lambda to: (column.at[to], from_z.at[z]), z_sems)
    start(along_z.values())
    total = column[z]
    arrive(along_z.values())
    for k in range(1, N_Z):
        total += from_z[(z + k) & (N_Z - 1)]
    arrive(across)
    return total, along_x + across + list(along_z.values())


def factor_kernel(
    boundary, partial, smoothing, energy, rho, coef, from_x, column, from_z, faces, offered, mine,
    *sems,
):
    z, x, _ = spot()
    barrier()
    total, copies = sum_back(partial, from_x, column, from_z, faces, sems[:6])
    own = partial[0 : CPD // 8].reshape(CPD, CELL)
    raw = settle(own, total, faces[0], faces[1], boundary)
    h2 = smoothing[...] * smoothing[...]
    h4 = h2 * h2
    inverse = 1.0 / (h4 * h4)
    density = (4.0 * NORM / CELL) * inverse * raw
    rho[...] = density
    slope = (40.0 / 3.0 * NORM / CELL) * inverse * energy[...] / density
    for g in range(CPD // 8):
        coef[g] = slope[g * 8 : g * 8 + 8]
    mine[...] = slope
    for b in range(8):
        offered[b : b + 1, :] = mine[pl.ds(boundary[b], 1), :]
    here = group_of(z, x)
    coef[here] = offered[...]
    face_sems, z_sems, x_sems = sems[6:8], sems[8:10], sems[10:12]
    along_z = list(z_copies(lambda to: (offered, coef.at[here]), z_sems).values())
    across = face_copies(
        (coef.at[0], coef.at[GROUPS - 1]), (coef.at[CPD // 8 - 1], coef.at[GROUPS - 2]), face_sems
    )
    start(along_z)
    start(across)
    arrive(along_z)
    row = coef.at[pl.ds(group_of(0, x), N_Z)]
    along_x = x_copies(lambda to: (row, row), x_sems)
    start(along_x)
    arrive(along_x + across)
    leave(copies + along_z + across + along_x)


def settle_kernel(boundary, partial, accel, from_x, column, from_z, faces, *sems):
    barrier()
    total, copies = sum_back(partial, from_x, column, from_z, faces, sems)
    for c in range(3):
        own = jnp.concatenate([partial[g, c] for g in range(CPD // 8)], axis=0)
        accel[c] = settle(own, total[c], faces[0, c], faces[1, c], boundary)
    leave(copies)


def comm_call(kernel, collective, out_shape, scratch, n_sems, operands):
    return pl.pallas_call(
        kernel,
        out_shape=out_shape,
        in_specs=[SMEM] + [VMEM] * (len(operands) - 1),
        out_specs=jax.tree.map(lambda _: VMEM, out_shape),
        scratch_shapes=[pltpu.VMEM(dims, F32) for dims in scratch]
        + [pltpu.SemaphoreType.DMA((n,)) for n in n_sems for _ in (0, 1)],
        compiler_params=pltpu.CompilerParams(collective_id=collective, has_side_effects=True),
        name=kernel.__name__,
    )(*operands)


def per_device(positions, smoothing, energy, active, boundary, wanted, cell_pairs, pair_count):
    consts = tables()
    offers = boundary[0]
    pairs = cell_pairs.reshape(-1)
    taken = wanted.reshape(-1)
    shape = lambda *dims: jax.ShapeDtypeStruct(dims, F32)
    rows = (8, CELL)
    view = comm_call(
        gather_kernel, 0, shape(GROUPS, 4, *rows), [(4, *rows)], (2, N_Z, N_Z * N_X),
        (offers, positions, smoothing),
    )
    partial = density_call(pairs, taken, pair_count, view, consts, 16, 32)
    rho, coef = comm_call(
        factor_kernel, 1, (shape(CPD, CELL), shape(GROUPS, *rows)),
        [(N_X, N_Z, *rows), (N_Z, *rows), (N_Z, *rows), (2, *rows), rows, (CPD, CELL)],
        (2, N_X, N_Z, 2, N_Z, N_X),
        (offers, partial.reshape(GROUPS, *rows), smoothing, energy),
    )
    force, density = force_call(pairs, taken, pair_count, view, coef, rho, active, consts, 16, 32)
    accel = comm_call(
        settle_kernel, 2, shape(3, CPD, CELL),
        [(N_X, N_Z, 3, *rows), (N_Z, 3, *rows), (N_Z, 3, *rows), (2, 3, *rows)],
        (2, N_X, N_Z),
        (offers, force),
    )
    live = jnp.arange(CELL, dtype=jnp.int32)[None, :] < active[:, None]
    return density, jnp.where(live[:, None, :], accel.transpose(1, 0, 2), 0.0)


def solution(mesh):
    in_specs = (
        P(("slab", "dom"), None, None),
        P(("slab", "dom"), None),
        P(("slab", "dom"), None),
        P(("slab", "dom")),
        P(("slab", "dom"), None),
        P(("slab", "dom"), None, None),
        P(("slab", "dom"), None, None),
        P(("slab", "dom")),
    )
    out_specs = (P(("slab", "dom"), None), P(("slab", "dom"), None, None))
    return jax.shard_map(
        per_device, mesh=mesh, in_specs=in_specs, out_specs=out_specs, check_vma=False
    )
```

```python
import functools
import jax
import jax.numpy as jnp
import numpy as np
from jax import lax
from jax.experimental import pallas as pl
from jax.experimental.pallas import tpu as pltpu
from jax.sharding import PartitionSpec as P

CELL, CPD, NVIEW, GROUPS, PAIRS = 128, 32, 304, 38, 448
NORM = 21.0 / (2.0 * 3.141592653589793)
BF = jnp.bfloat16
F32 = jnp.float32
TINY = 1e-30
N_Z, N_X, N_SLAB = 8, 4, 8
MESH = pl.DeviceIdType.MESH
DEPTH = 80
NT = (((1,), (1,)), ((), ()))


def tables():
    sel = np.zeros((DEPTH, 32), np.float32)
    first, second, third, one = 0, 8, 24, 4
    for c in range(3):
        for part, base in ((first, 0), (second, 16), (third, 32)):
            sel[base + c, part + c] = -0.5
            sel[base + 5 + c, part + c] = -0.5
        sel[8 + c, first + c] = -0.5
        sel[24 + c, second + c] = -0.5
        sel[40 + c, first + c] = -0.5
        for base in (48, 56, 72):
            sel[base + c, one] = 1.0
    sel[3, one] = sel[11, one] = sel[12, one] = sel[43, one] = 1.0
    sel[4, first + 3] = sel[20, second + 3] = sel[36, third + 3] = 1.0
    return (jnp.asarray(sel, BF),)


def build_constants(shift, scale, eye):
    row = lax.broadcasted_iota(jnp.int32, (8, CELL), 0)
    none = jnp.zeros((8, CELL), F32)
    for d in range(28):
        offset = (d // 9 - 1, d // 3 % 3 - 1, d % 3 - 1) if d < 27 else (0, 0, 0)
        length = sum(o * o for o in offset) if d < 27 else 16384
        moved, turned = none, none
        for c, o in enumerate(offset):
            if o:
                moved = jnp.where(row == 5 + c, -2.0 * o, moved)
                turned = jnp.where(row == c, -1.0 * o, turned)
        far = jnp.where(row == 4, 1.0 * length, none)
        shift[d] = jnp.concatenate([moved, far, moved, none], axis=0).astype(BF)
        scale[d] = jnp.concatenate([turned, turned, none, turned], axis=0).astype(BF)
    down = lax.broadcasted_iota(jnp.int32, (CELL, CELL), 0)
    across = lax.broadcasted_iota(jnp.int32, (CELL, CELL), 1)
    eye[...] = jnp.where(down == across, 1.0, 0.0).astype(BF)


def view_row(view, c, v):
    return view[v // 8, c, pl.ds(lax.rem(v, 8), 1), :]


def spread_columns(planes, put):
    turned = jnp.concatenate(planes, axis=0).T

    def some(g, turned):
        for k in range(4):
            for c in range(4):
                column = turned[:, c * CPD + k : c * CPD + k + 1]
                put(g * 4 + k, c, jnp.broadcast_to(column, (CELL, CELL)))
        return pltpu.roll(turned, CELL - 4, 1)

    lax.fori_loop(0, CPD // 4, some, turned)


def row_sums(load):
    lane = lax.broadcasted_iota(jnp.int32, (CELL, CELL), 1)

    def some(g, table):
        for k in range(8):
            u = g * 8 + k
            table = jnp.where(lane == u, jnp.sum(load(u), axis=1, keepdims=True), table)
        return table

    return lax.fori_loop(0, CPD // 8, some, jnp.zeros((CELL, CELL), F32)).T[0:CPD]


def own_plane(ref, *at):
    return jnp.concatenate([ref[(g, *at)] for g in range(CPD // 8)], axis=0)


def build_left(vv, sel, eye, at):
    def some(g, _):
        for k in range(8):
            u = g * 8 + k
            picked = jnp.dot(sel[...], vv[u], preferred_element_type=F32).astype(BF)
            cols = lax.dot_general(eye[...], picked, NT, preferred_element_type=F32)
            at[u] = cols.astype(BF)
        return 0

    lax.fori_loop(0, CPD // 8, some, 0)


def sweep(total, place, fill, use, buffers):
    half = len(buffers) // 2
    sides = buffers[:half], buffers[half:]

    def some(i, _):
        for side in (0, 1):
            for s in range(half):
                p = (2 * i + side) * half + s
                fill(sides[1 - side][s], place(p + half))
                use(place(p), sides[side][s])
        return 0

    for s in range(half):
        fill(sides[0][s], place(s))
    lax.fori_loop(0, pl.cdiv(total, 2 * half), some, 0)


def build_cell_tables(view, vv):
    row = lax.broadcasted_iota(jnp.int32, (8, CELL), 0)

    def one_cell(g, k):
        x, y, z = (
            jnp.broadcast_to(view[g, c, pl.ds(k, 1), :], (8, CELL)) - 0.5 for c in range(3)
        )
        n = x * x + y * y + z * z
        w = jnp.where(row == 3, n, jnp.where(row == 4, 1.0, 0.0))
        w = jnp.where(row == 0, -2.0 * x, w)
        w = jnp.where(row == 1, -2.0 * y, w)
        w = jnp.where(row == 2, -2.0 * z, w)
        t1 = w.astype(BF).astype(F32)
        r1 = w - t1
        t2 = r1.astype(BF).astype(F32)
        t3 = r1 - t2
        return jnp.concatenate([t1, t2, t1, t3], axis=0).astype(BF)

    def group(g, _):
        for k in range(8):
            vv[g * 8 + k] = one_cell(g, k)
        return 0

    lax.fori_loop(0, GROUPS, group, 0)


def right_operand(vv, shift, scale, v, d):
    cell = vv[v]
    moved = cell + shift[d]
    turned = cell * scale[d]
    return jnp.concatenate([moved[:16], moved[:16], moved[16:], turned], axis=0)


def dist2(at, vv, shift, scale, u, v, d):
    return jnp.dot(
        at[u], right_operand(vv, shift, scale, v, d), preferred_element_type=F32
    )


def root(r2):
    r2 = jnp.maximum(r2, TINY)
    return r2 * lax.rsqrt(r2)


def fold_rows(w):
    return jnp.sum(w.reshape(-1, 8, CELL), axis=0)


def scalars(pairs, wanted, count, p):
    p = jnp.minimum(p, PAIRS - 1) if not isinstance(p, int) else p
    u = pairs[3 * p]
    v = pairs[3 * p + 1]
    d = jnp.where(p < count, pairs[3 * p + 2], 27)
    slot = jnp.clip(v - CPD, 0, 255)
    q = slot >> 3
    offered = CPD + (q & 3) * 64 + (q >> 2) * 8 + wanted[slot]
    v = jnp.where((v >= CPD) & (v < CPD + 256), offered, v)
    return u, v, d


def density_kernel(
    unroll, rows,
    pairs, wanted, count, view, sel, out, shift, scale, eye, vv, at, hb, hq, acc_l, acc_r, *buffers,
):
    build_constants(shift, scale, eye)
    build_cell_tables(view, vv)

    build_left(vv, sel, eye, at)

    def put(u, c, column):
        if c == 0:
            hb[u] = column
        elif c == 1:
            hq[u] = column
        elif c == 2:
            acc_l[u] = jnp.zeros((CELL, CELL), F32)

    h = own_plane(view, 3)
    spread_columns([h, 1.25 * h, h, h], put)

    def clear(g, _):
        acc_r[pl.ds(g * 8, 8)] = jnp.zeros((8, 8, CELL), F32)
        return 0

    lax.fori_loop(0, GROUPS, clear, 0)
    d2 = functools.partial(dist2, at, vv, shift, scale)
    chunks = range(CELL // rows)

    def fill(buffer, where):
        buffer[...] = d2(*where)

    def self_tile(where, r2):
        u = where[0]
        h_r = jnp.broadcast_to(view_row(view, 3, u), (rows, CELL))
        q_r = 1.25 * h_r
        total = jnp.zeros((8, CELL), F32)
        for c in chunks:
            r = root(r2[c * rows : c * rows + rows, :])
            f = jnp.maximum(h_r - r, 0.0)
            f2 = f * f
            total += fold_rows(f2 * f2 * (q_r - f))
        acc_r[u] = total

    def self_place(p):
        u = jnp.minimum(p, CPD - 1)
        return u, u, 13

    sweep(CPD, self_place, fill, self_tile, buffers)

    n = count[0]
    place = functools.partial(scalars, pairs, wanted, n)

    def tile(where, r2):
        u, v, _ = where
        h_r = jnp.broadcast_to(view_row(view, 3, v), (rows, CELL))
        q_r = 1.25 * h_r
        total = acc_r[v]
        for c in chunks:
            at_rows = pl.ds(c * rows, rows)
            r = root(r2[c * rows : c * rows + rows, :])
            f = jnp.maximum(hb[u, at_rows, :] - r, 0.0)
            f2 = f * f
            acc_l[u, at_rows, :] += f2 * f2 * (hq[u, at_rows, :] - f)
            f = jnp.maximum(h_r - r, 0.0)
            f2 = f * f
            total += fold_rows(f2 * f2 * (q_r - f))
        acc_r[v] = total

    sweep(n, place, fill, tile, buffers)

    def finish(g, _):
        out[pl.ds(g * 8, 8), :] = jnp.sum(acc_r[pl.ds(g * 8, 8)], axis=1)
        return 0

    lax.fori_loop(0, GROUPS, finish, 0)
    out[0:CPD, :] += row_sums(lambda u: acc_l[u])


def force_kernel(
    unroll, rows,
    pairs, wanted, count, active, view, coef, rho, sel, out, density,
    shift, scale, eye, vv, at, hb, cb, xb, acc_l, acc_r, *buffers,
):
    row = lax.broadcasted_iota(jnp.int32, (CPD, CELL), 0)
    live = jnp.zeros((CPD, CELL), jnp.int32)
    for u in range(CPD):
        live = jnp.where(row == u, active[u], live)
    lane = lax.broadcasted_iota(jnp.int32, (CPD, CELL), 1)
    density[...] = jnp.where(lane < live, rho[...], 0.0)
    build_constants(shift, scale, eye)
    build_cell_tables(view, vv)

    build_left(vv, sel, eye, at)

    def put(u, c, column):
        if c == 3:
            hb[u] = column
        else:
            xb[u, c] = column
            acc_l[u, c] = jnp.zeros((CELL, CELL), F32)

    def put_coef(u, c, column):
        if c == 0:
            cb[u] = column

    spread_columns([own_plane(view, c) - (0.5 if c < 3 else 0.0) for c in range(4)], put)
    spread_columns([own_plane(coef)] * 4, put_coef)

    def clear(g, _):
        for c in range(3):
            acc_r[c, pl.ds(g * 8, 8)] = jnp.zeros((8, 8, CELL), F32)
        return 0

    lax.fori_loop(0, GROUPS, clear, 0)
    d2 = functools.partial(dist2, at, vv, shift, scale)
    chunks = range(CELL // rows)

    def tile(both, where, r2):
        u, v, d = where
        h_r = jnp.broadcast_to(view_row(view, 3, v), (rows, CELL))
        c_r = jnp.broadcast_to(coef[v // 8, pl.ds(lax.rem(v, 8), 1), :], (rows, CELL))
        offset = (d // 9 - 1, lax.rem(d // 3, 3) - 1, lax.rem(d, 3) - 1)
        x_r = [
            jnp.broadcast_to(view_row(view, c, v) + (offset[c].astype(F32) - 0.5), (rows, CELL))
            for c in range(3)
        ]
        total = [acc_r[c, v] for c in range(3)]
        for k in chunks:
            at_rows = pl.ds(k * rows, rows)
            r = root(r2[k * rows : k * rows + rows, :])
            f = jnp.maximum(hb[u, at_rows, :] - r, 0.0)
            s = f * f * (f * cb[u, at_rows, :])
            f = jnp.maximum(h_r - r, 0.0)
            s += f * f * (f * c_r)
            for c in range(3):
                push = s * (xb[u, c, at_rows, :] - x_r[c])
                if both:
                    acc_l[u, c, at_rows, :] += push
                total[c] += fold_rows(push)
        for c in range(3):
            acc_r[c, v] = total[c]

    def fill(buffer, where):
        buffer[...] = d2(*where)

    def self_place(p):
        u = jnp.minimum(p, CPD - 1)
        return u, u, jnp.int32(13)

    sweep(CPD, self_place, fill, functools.partial(tile, False), buffers)

    n = count[0]
    place = functools.partial(scalars, pairs, wanted, n)

    sweep(n, place, fill, functools.partial(tile, True), buffers)

    def finish(g, _):
        for c in range(3):
            out[g, c] = -jnp.sum(acc_r[c, pl.ds(g * 8, 8)], axis=1)
        return 0

    lax.fori_loop(0, GROUPS, finish, 0)
    for c in range(3):
        turned = row_sums(lambda u: acc_l[u, c])
        for g in range(CPD // 8):
            out[g, c] += turned[g * 8 : g * 8 + 8]


SMEM = pl.BlockSpec(memory_space=pltpu.SMEM)
VMEM = pl.BlockSpec(memory_space=pltpu.VMEM)


def density_call(pairs, wanted, count, view, consts, unroll=2, rows=64):
    return pl.pallas_call(
        functools.partial(density_kernel, unroll, rows),
        out_shape=jax.ShapeDtypeStruct((NVIEW, CELL), F32),
        in_specs=[SMEM] * 3 + [VMEM] * 2,
        out_specs=VMEM,
        scratch_shapes=[
            pltpu.VMEM((28, 32, CELL), BF),
            pltpu.VMEM((28, 32, CELL), BF),
            pltpu.VMEM((CELL, CELL), BF),
            pltpu.VMEM((NVIEW, 32, CELL), BF),
            pltpu.VMEM((CPD, CELL, DEPTH), BF),
            pltpu.VMEM((CPD, CELL, CELL), F32),
            pltpu.VMEM((CPD, CELL, CELL), F32),
            pltpu.VMEM((CPD, CELL, CELL), F32),
            pltpu.VMEM((NVIEW, 8, CELL), F32),
        ]
        + [pltpu.VMEM((CELL, CELL), F32)] * unroll,
        compiler_params=pltpu.CompilerParams(vmem_limit_bytes=48 << 20),
        name="density_pairs",
    )(pairs, wanted, count, view, *consts)


def force_call(pairs, wanted, count, view, coef, rho, active, consts, unroll=2, rows=64):
    return pl.pallas_call(
        functools.partial(force_kernel, unroll, rows),
        out_shape=(
            jax.ShapeDtypeStruct((GROUPS, 3, 8, CELL), F32),
            jax.ShapeDtypeStruct((CPD, CELL), F32),
        ),
        in_specs=[SMEM] * 4 + [VMEM] * 4,
        out_specs=(VMEM, VMEM),
        scratch_shapes=[
            pltpu.VMEM((28, 32, CELL), BF),
            pltpu.VMEM((28, 32, CELL), BF),
            pltpu.VMEM((CELL, CELL), BF),
            pltpu.VMEM((NVIEW, 32, CELL), BF),
            pltpu.VMEM((CPD, CELL, DEPTH), BF),
            pltpu.VMEM((CPD, CELL, CELL), F32),
            pltpu.VMEM((CPD, CELL, CELL), F32),
            pltpu.VMEM((CPD, 3, CELL, CELL), F32),
            pltpu.VMEM((CPD, 3, CELL, CELL), F32),
            pltpu.VMEM((3, NVIEW, 8, CELL), F32),
        ]
        + [pltpu.VMEM((CELL, CELL), F32)] * unroll,
        compiler_params=pltpu.CompilerParams(vmem_limit_bytes=48 << 20),
        name="force_pairs",
    )(pairs, wanted, count, active, view, coef, rho, *consts)


def spot():
    t = lax.axis_index("dom")
    return t // N_X, lax.rem(t, N_X), lax.axis_index("slab")


def group_of(z, x):
    return CPD // 8 + x * N_Z + z


def barrier(steps):
    z, x, s = spot()
    sem = pltpu.get_barrier_semaphore()
    peers = [{"dom": peer_at(z + i, x + j)} for i, j in steps]
    peers += [{"slab": (s + k) & (N_SLAB - 1)} for k in (1, N_SLAB - 1)]
    for peer in peers:
        pl.semaphore_signal(sem, inc=1, device_id=peer, device_id_type=MESH)
    pl.semaphore_wait(sem, len(peers))


def peer_at(z, x):
    return (z & (N_Z - 1)) * N_X + (x & (N_X - 1))


def far_first(steps):
    return sorted(steps, key=lambda at: -min(at[0], N_Z - at[0]) - min(at[1], N_X - at[1]))


ALL_STEPS = far_first((i, j) for i in range(N_Z) for j in range(N_X) if i or j)
AXIS_STEPS = far_first((i, j) for i, j in ALL_STEPS if i == 0 or j == 0)


def copy_to(src, dst, sems, k, peer):
    return pltpu.make_async_remote_copy(
        src_ref=src, dst_ref=dst, send_sem=sems[0].at[k], recv_sem=sems[1].at[k],
        device_id=peer, device_id_type=MESH,
    )


def z_copies(refs, sems):
    z, x, _ = spot()
    out = []
    for k in (4, 3, 5, 2, 6, 1, 7):
        to = (z + k) & (N_Z - 1)
        out.append((k, copy_to(*refs(to), sems, k, {"dom": to * N_X + x})))
    return dict(out)


def x_copies(refs, sems, base=0):
    z, x, _ = spot()
    out = []
    for k in (2, 1, 3):
        to = (x + k) & (N_X - 1)
        out.append(copy_to(*refs(to), sems, base + k, {"dom": z * N_X + to}))
    return out


def peer_copies(refs, sems):
    z, x, _ = spot()
    out = []
    for i, j in ALL_STEPS:
        group = group_of((z + i) & (N_Z - 1), (x + j) & (N_X - 1))
        out.append(
            copy_to(*refs(group), sems, i * N_X + j, {"dom": peer_at(z + i, x + j)})
        )
    return out


def face_copies(lower, upper, sems):
    s = lax.axis_index("slab")
    return [
        copy_to(*lower, sems, 0, {"slab": (s + N_SLAB - 1) & (N_SLAB - 1)}),
        copy_to(*upper, sems, 1, {"slab": (s + 1) & (N_SLAB - 1)}),
    ]


def start(copies):
    for copy in copies:
        copy.start()


def arrive(copies):
    for copy in copies:
        copy.wait_recv()


def leave(copies):
    for copy in copies:
        copy.wait_send()


def gather_kernel(boundary, positions, smoothing, view, offered, *sems):
    z, x, _ = spot()
    face_sems, z_sems, x_sems = sems[:2], sems[2:4], sems[4:6]
    for g in range(CPD // 8):
        for c in range(3):
            view[g, c] = positions[c, g * 8 : g * 8 + 8, :]
        view[g, 3] = smoothing[g * 8 : g * 8 + 8, :]
    for b in range(8):
        cell = boundary[b]
        for c in range(4):
            offered[c, b : b + 1, :] = view_row(view, c, cell)
    here = group_of(z, x)
    view[here] = offered[...]
    barrier(AXIS_STEPS)
    along_z = z_copies(lambda to: (offered, view.at[here]), z_sems)
    faces = face_copies(
        (view.at[0], view.at[GROUPS - 1]), (view.at[CPD // 8 - 1], view.at[GROUPS - 2]), face_sems
    )
    start(along_z.values())
    along_x = x_copies(lambda to: (offered, view.at[here]), x_sems)
    start(along_x)
    start(faces)
    for k in (1, 7, 2, 6, 3, 5, 4):
        along_z[k].wait_recv()
        block = view.at[group_of((z - k) & (N_Z - 1), x)]
        onward = x_copies(lambda to: (block, block), x_sems, k * N_X)
        start(onward)
        along_x += onward
    arrive(along_x + faces)
    leave(list(along_z.values()) + along_x + faces)


def settle(own, arrived, lower, upper, boundary):
    row = lax.broadcasted_iota(jnp.int32, (CPD, CELL), 0)
    for b in range(8):
        own += jnp.where(row == boundary[b], jnp.broadcast_to(arrived[b : b + 1], own.shape), 0.0)
    return jnp.concatenate([own[:8] + lower, own[8:24], own[24:] + upper], axis=0)


def sum_back(partial, arrived, faces, face_sems, sems):
    z, x, _ = spot()
    here = group_of(z, x)
    copies = peer_copies(lambda group: (partial.at[group], arrived.at[here - CPD // 8]), sems)
    copies += face_copies(
        (partial.at[GROUPS - 2], faces.at[1]), (partial.at[GROUPS - 1], faces.at[0]), face_sems
    )
    start(copies)
    arrived[here - CPD // 8] = partial[here]
    arrive(copies)
    total = arrived[0]
    for k in range(1, N_Z * N_X):
        total += arrived[k]
    return total, copies


def factor_kernel(
    boundary, partial, smoothing, energy, rho, coef, arrived, faces, offered, mine, *sems
):
    z, x, _ = spot()
    barrier(ALL_STEPS)
    h2 = smoothing[...] * smoothing[...]
    h4 = h2 * h2
    inverse = 1.0 / (h4 * h4)
    total, copies = sum_back(partial, arrived, faces, sems[0:2], sems[2:4])
    own = partial[0 : CPD // 8].reshape(CPD, CELL)
    raw = settle(own, total, faces[0], faces[1], boundary)
    density = (4.0 * NORM / CELL) * inverse * raw
    rho[...] = density
    slope = (40.0 / 3.0 * NORM / CELL) * inverse * energy[...] / density
    for g in range(CPD // 8):
        coef[g] = slope[g * 8 : g * 8 + 8]
    mine[...] = slope
    for b in range(8):
        offered[b : b + 1, :] = mine[pl.ds(boundary[b], 1), :]
    here = group_of(z, x)
    coef[here] = offered[...]
    back = peer_copies(lambda group: (offered, coef.at[here]), sems[6:8])
    back += face_copies(
        (coef.at[0], coef.at[GROUPS - 1]), (coef.at[CPD // 8 - 1], coef.at[GROUPS - 2]), sems[4:6]
    )
    start(back)
    leave(copies)
    arrive(back)
    leave(back)


def settle_kernel(boundary, partial, accel, arrived, faces, *sems):
    barrier(ALL_STEPS)
    total, copies = sum_back(partial, arrived, faces, sems[0:2], sems[2:4])
    for c in range(3):
        own = jnp.concatenate([partial[g, c] for g in range(CPD // 8)], axis=0)
        accel[c] = settle(own, total[c], faces[0, c], faces[1, c], boundary)
    leave(copies)


def comm_call(kernel, collective, out_shape, scratch, n_sems, operands):
    return pl.pallas_call(
        kernel,
        out_shape=out_shape,
        in_specs=[SMEM] + [VMEM] * (len(operands) - 1),
        out_specs=jax.tree.map(lambda _: VMEM, out_shape),
        scratch_shapes=[pltpu.VMEM(dims, F32) for dims in scratch]
        + [pltpu.SemaphoreType.DMA((n,)) for n in n_sems for _ in (0, 1)],
        compiler_params=pltpu.CompilerParams(collective_id=collective, has_side_effects=True),
        name=kernel.__name__,
    )(*operands)


def per_device(positions, smoothing, energy, active, boundary, wanted, cell_pairs, pair_count):
    consts = tables()
    offers = boundary[0]
    pairs = cell_pairs.reshape(-1)
    taken = wanted.reshape(-1)
    shape = lambda *dims: jax.ShapeDtypeStruct(dims, F32)
    rows = (8, CELL)
    view = comm_call(
        gather_kernel, 0, shape(GROUPS, 4, *rows), [(4, *rows)], (2, N_Z, N_Z * N_X),
        (offers, positions.transpose(1, 0, 2), smoothing),
    )
    partial = density_call(pairs, taken, pair_count, view, consts, 16, 32)
    rho, coef = comm_call(
        factor_kernel, 1, (shape(CPD, CELL), shape(GROUPS, *rows)),
        [(N_Z * N_X, *rows), (2, *rows), rows, (CPD, CELL)],
        (2, N_Z * N_X, 2, N_Z * N_X),
        (offers, partial.reshape(GROUPS, *rows), smoothing, energy),
    )
    force, density = force_call(pairs, taken, pair_count, view, coef, rho, active, consts, 16, 32)
    accel = comm_call(
        settle_kernel, 2, shape(3, CPD, CELL),
        [(N_Z * N_X, 3, *rows), (2, 3, *rows)],
        (2, N_Z * N_X),
        (offers, force),
    )
    live = jnp.arange(CELL, dtype=jnp.int32)[None, :] < active[:, None]
    return density, jnp.where(live[:, None, :], accel.transpose(1, 0, 2), 0.0)


def solution(mesh):
    in_specs = (
        P(("slab", "dom"), None, None),
        P(("slab", "dom"), None),
        P(("slab", "dom"), None),
        P(("slab", "dom")),
        P(("slab", "dom"), None),
        P(("slab", "dom"), None, None),
        P(("slab", "dom"), None, None),
        P(("slab", "dom")),
    )
    out_specs = (P(("slab", "dom"), None), P(("slab", "dom"), None, None))
    return jax.shard_map(
        per_device, mesh=mesh, in_specs=in_specs, out_specs=out_specs, check_vma=False
    )
```

```python
import functools
import jax
import jax.numpy as jnp
import numpy as np
from jax import lax
from jax.experimental import pallas as pl
from jax.experimental.pallas import tpu as pltpu
from jax.sharding import PartitionSpec as P

CELL, CPD, NVIEW, GROUPS, PAIRS = 128, 32, 304, 38, 448
NORM = 21.0 / (2.0 * 3.141592653589793)
BF = jnp.bfloat16
F32 = jnp.float32
TINY = 1e-30
N_Z, N_X, N_SLAB = 8, 4, 8
MESH = pl.DeviceIdType.MESH
DEPTH = 80
NT = (((1,), (1,)), ((), ()))


def tables():
    sel = np.zeros((DEPTH, 32), np.float32)
    first, second, third, one = 0, 8, 24, 4
    for c in range(3):
        for part, base in ((first, 0), (second, 16), (third, 32)):
            sel[base + c, part + c] = -0.5
            sel[base + 5 + c, part + c] = -0.5
        sel[8 + c, first + c] = -0.5
        sel[24 + c, second + c] = -0.5
        sel[40 + c, first + c] = -0.5
        for base in (48, 56, 72):
            sel[base + c, one] = 1.0
    sel[3, one] = sel[11, one] = sel[12, one] = sel[43, one] = 1.0
    sel[4, first + 3] = sel[20, second + 3] = sel[36, third + 3] = 1.0
    return (jnp.asarray(sel, BF),)


def build_constants(shift, scale, eye):
    row = lax.broadcasted_iota(jnp.int32, (8, CELL), 0)
    none = jnp.zeros((8, CELL), F32)
    for d in range(28):
        offset = (d // 9 - 1, d // 3 % 3 - 1, d % 3 - 1) if d < 27 else (0, 0, 0)
        length = sum(o * o for o in offset) if d < 27 else 16384
        moved, turned = none, none
        for c, o in enumerate(offset):
            if o:
                moved = jnp.where(row == 5 + c, -2.0 * o, moved)
                turned = jnp.where(row == c, -1.0 * o, turned)
        far = jnp.where(row == 4, 1.0 * length, none)
        shift[d] = jnp.concatenate([moved, far, moved, none], axis=0).astype(BF)
        scale[d] = jnp.concatenate([turned, turned, none, turned], axis=0).astype(BF)
    down = lax.broadcasted_iota(jnp.int32, (CELL, CELL), 0)
    across = lax.broadcasted_iota(jnp.int32, (CELL, CELL), 1)
    eye[...] = jnp.where(down == across, 1.0, 0.0).astype(BF)


def view_row(view, c, v):
    return view[v // 8, c, pl.ds(lax.rem(v, 8), 1), :]


def spread_columns(planes, put):
    turned = jnp.concatenate(planes, axis=0).T

    def some(g, turned):
        for k in range(4):
            for c in range(4):
                column = turned[:, c * CPD + k : c * CPD + k + 1]
                put(g * 4 + k, c, jnp.broadcast_to(column, (CELL, CELL)))
        return pltpu.roll(turned, CELL - 4, 1)

    lax.fori_loop(0, CPD // 4, some, turned)


def row_sums(load):
    lane = lax.broadcasted_iota(jnp.int32, (CELL, CELL), 1)

    def some(g, table):
        for k in range(8):
            u = g * 8 + k
            table = jnp.where(lane == u, jnp.sum(load(u), axis=1, keepdims=True), table)
        return table

    return lax.fori_loop(0, CPD // 8, some, jnp.zeros((CELL, CELL), F32)).T[0:CPD]


def own_plane(ref, *at):
    return jnp.concatenate([ref[(g, *at)] for g in range(CPD // 8)], axis=0)


def build_left(vv, sel, eye, at):
    def some(g, _):
        for k in range(8):
            u = g * 8 + k
            picked = jnp.dot(sel[...], vv[u], preferred_element_type=F32).astype(BF)
            cols = lax.dot_general(eye[...], picked, NT, preferred_element_type=F32)
            at[u] = cols.astype(BF)
        return 0

    lax.fori_loop(0, CPD // 8, some, 0)


def sweep(total, place, fill, use, buffers):
    half = len(buffers) // 2
    sides = buffers[:half], buffers[half:]

    def some(i, _):
        for side in (0, 1):
            for s in range(half):
                p = (2 * i + side) * half + s
                fill(sides[1 - side][s], place(p + half))
                use(place(p), sides[side][s])
        return 0

    for s in range(half):
        fill(sides[0][s], place(s))
    lax.fori_loop(0, pl.cdiv(total, 2 * half), some, 0)


def build_cell_tables(view, vv):
    row = lax.broadcasted_iota(jnp.int32, (8, CELL), 0)

    def one_cell(g, k):
        x, y, z = (
            jnp.broadcast_to(view[g, c, pl.ds(k, 1), :], (8, CELL)) - 0.5 for c in range(3)
        )
        n = x * x + y * y + z * z
        w = jnp.where(row == 3, n, jnp.where(row == 4, 1.0, 0.0))
        w = jnp.where(row == 0, -2.0 * x, w)
        w = jnp.where(row == 1, -2.0 * y, w)
        w = jnp.where(row == 2, -2.0 * z, w)
        t1 = w.astype(BF).astype(F32)
        r1 = w - t1
        t2 = r1.astype(BF).astype(F32)
        t3 = r1 - t2
        return jnp.concatenate([t1, t2, t1, t3], axis=0).astype(BF)

    def group(g, _):
        for k in range(8):
            vv[g * 8 + k] = one_cell(g, k)
        return 0

    lax.fori_loop(0, GROUPS, group, 0)


def right_operand(vv, shift, scale, v, d):
    cell = vv[v]
    moved = cell + shift[d]
    turned = cell * scale[d]
    return jnp.concatenate([moved[:16], moved[:16], moved[16:], turned], axis=0)


def dist2(at, vv, shift, scale, u, v, d):
    return jnp.dot(
        at[u], right_operand(vv, shift, scale, v, d), preferred_element_type=F32
    )


def root(r2):
    r2 = jnp.maximum(r2, TINY)
    return r2 * lax.rsqrt(r2)


def fold_rows(w):
    return jnp.sum(w.reshape(-1, 8, CELL), axis=0)


def scalars(pairs, wanted, count, p):
    p = jnp.minimum(p, PAIRS - 1) if not isinstance(p, int) else p
    u = pairs[3 * p]
    v = pairs[3 * p + 1]
    d = jnp.where(p < count, pairs[3 * p + 2], 27)
    slot = jnp.clip(v - CPD, 0, 255)
    q = slot >> 3
    offered = CPD + (q & 3) * 64 + (q >> 2) * 8 + wanted[slot]
    v = jnp.where((v >= CPD) & (v < CPD + 256), offered, v)
    return u, v, d


def density_kernel(
    unroll, rows,
    pairs, wanted, count, view, sel, out, shift, scale, eye, vv, at, hb, hq, acc_l, acc_r, *buffers,
):
    build_constants(shift, scale, eye)
    build_cell_tables(view, vv)

    build_left(vv, sel, eye, at)

    def put(u, c, column):
        if c == 0:
            hb[u] = column
        elif c == 1:
            hq[u] = column
        elif c == 2:
            acc_l[u] = jnp.zeros((CELL, CELL), F32)

    h = own_plane(view, 3)
    spread_columns([h, 1.25 * h, h, h], put)

    def clear(g, _):
        acc_r[pl.ds(g * 8, 8)] = jnp.zeros((8, 8, CELL), F32)
        return 0

    lax.fori_loop(0, GROUPS, clear, 0)
    d2 = functools.partial(dist2, at, vv, shift, scale)
    chunks = range(CELL // rows)

    def fill(buffer, where):
        buffer[...] = d2(*where)

    def self_tile(where, r2):
        u = where[0]
        h_r = jnp.broadcast_to(view_row(view, 3, u), (rows, CELL))
        q_r = 1.25 * h_r
        total = jnp.zeros((8, CELL), F32)
        for c in chunks:
            r = root(r2[c * rows : c * rows + rows, :])
            f = jnp.maximum(h_r - r, 0.0)
            f2 = f * f
            total += fold_rows(f2 * f2 * (q_r - f))
        acc_r[u] = total

    def self_place(p):
        u = jnp.minimum(p, CPD - 1)
        return u, u, 13

    sweep(CPD, self_place, fill, self_tile, buffers)

    n = count[0]
    place = functools.partial(scalars, pairs, wanted, n)

    def tile(where, r2):
        u, v, _ = where
        h_r = jnp.broadcast_to(view_row(view, 3, v), (rows, CELL))
        q_r = 1.25 * h_r
        total = acc_r[v]
        for c in chunks:
            at_rows = pl.ds(c * rows, rows)
            r = root(r2[c * rows : c * rows + rows, :])
            f = jnp.maximum(hb[u, at_rows, :] - r, 0.0)
            f2 = f * f
            acc_l[u, at_rows, :] += f2 * f2 * (hq[u, at_rows, :] - f)
            f = jnp.maximum(h_r - r, 0.0)
            f2 = f * f
            total += fold_rows(f2 * f2 * (q_r - f))
        acc_r[v] = total

    sweep(n, place, fill, tile, buffers)

    def finish(g, _):
        out[pl.ds(g * 8, 8), :] = jnp.sum(acc_r[pl.ds(g * 8, 8)], axis=1)
        return 0

    lax.fori_loop(0, GROUPS, finish, 0)
    out[0:CPD, :] += row_sums(lambda u: acc_l[u])


def force_kernel(
    unroll, rows,
    pairs, wanted, count, active, view, coef, rho, sel, out, density,
    shift, scale, eye, vv, at, hb, cb, xb, acc_l, acc_r, *buffers,
):
    row = lax.broadcasted_iota(jnp.int32, (CPD, CELL), 0)
    live = jnp.zeros((CPD, CELL), jnp.int32)
    for u in range(CPD):
        live = jnp.where(row == u, active[u], live)
    lane = lax.broadcasted_iota(jnp.int32, (CPD, CELL), 1)
    density[...] = jnp.where(lane < live, rho[...], 0.0)
    build_constants(shift, scale, eye)
    build_cell_tables(view, vv)

    build_left(vv, sel, eye, at)

    def put(u, c, column):
        if c == 3:
            hb[u] = column
        else:
            xb[u, c] = column

    def put_coef(u, c, column):
        if c == 0:
            cb[u] = column

    spread_columns([own_plane(view, c) - (0.5 if c < 3 else 0.0) for c in range(4)], put)
    spread_columns([own_plane(coef)] * 4, put_coef)

    def clear(g, _):
        for c in range(4):
            acc_r[c, pl.ds(g * 8, 8)] = jnp.zeros((8, 8, CELL), F32)
        return 0

    lax.fori_loop(0, GROUPS, clear, 0)
    acc_l[...] = jnp.zeros(acc_l.shape, F32)
    d2 = functools.partial(dist2, at, vv, shift, scale)
    chunks = range(CELL // rows)

    def tile(both, where, r2):
        u, v, d = where
        h_r = jnp.broadcast_to(view_row(view, 3, v), (rows, CELL))
        c_r = jnp.broadcast_to(coef[v // 8, pl.ds(lax.rem(v, 8), 1), :], (rows, CELL))
        total = [jnp.zeros((8, CELL), F32)] * 4
        tops, rests = [], []
        for k in chunks:
            at_rows = pl.ds(k * rows, rows)
            r = root(r2[k * rows : k * rows + rows, :])
            f = jnp.maximum(hb[u, at_rows, :] - r, 0.0)
            s = f * f * (f * cb[u, at_rows, :])
            f = jnp.maximum(h_r - r, 0.0)
            s += f * f * (f * c_r)
            for c in range(3):
                total[c] += fold_rows(s * xb[u, c, at_rows, :])
            total[3] += fold_rows(s)
            if both:
                top = s.astype(BF)
                tops.append(top)
                rests.append((s - top.astype(F32)).astype(BF))
        if both:
            right = vv[v, 0:16, :] + shift[d, 0:16, :]
            acc_l[u] += lax.dot_general(
                jnp.concatenate([right, right], axis=1),
                jnp.concatenate(
                    [jnp.concatenate(tops, axis=0), jnp.concatenate(rests, axis=0)], axis=1
                ),
                NT,
                preferred_element_type=F32,
            )
        offset = (d // 9 - 1, lax.rem(d // 3, 3) - 1, lax.rem(d, 3) - 1)
        for c in range(3):
            acc_r[c, v] += total[c] - offset[c].astype(F32) * total[3]
        acc_r[3, v] += total[3]

    def fill(buffer, where):
        buffer[...] = d2(*where)

    def self_place(p):
        u = jnp.minimum(p, CPD - 1)
        return u, u, jnp.int32(13)

    sweep(CPD, self_place, fill, functools.partial(tile, False), buffers)

    n = count[0]
    place = functools.partial(scalars, pairs, wanted, n)

    sweep(n, place, fill, functools.partial(tile, True), buffers)

    def finish(g, _):
        whole = jnp.sum(acc_r[3, pl.ds(g * 8, 8)], axis=1)
        for c in range(3):
            out[g, c] = (view[g, c] - 0.5) * whole - jnp.sum(acc_r[c, pl.ds(g * 8, 8)], axis=1)
        return 0

    lax.fori_loop(0, GROUPS, finish, 0)
    for g in range(CPD // 8):
        rows_of = lambda r: jnp.concatenate(
            [acc_l[g * 8 + k, r : r + 1, :] for k in range(8)], axis=0
        )
        whole = rows_of(4)
        for c in range(3):
            moved = rows_of(c) + rows_of(8 + c) + rows_of(5 + c)
            out[g, c] += (view[g, c] - 0.5) * whole + 0.5 * moved


SMEM = pl.BlockSpec(memory_space=pltpu.SMEM)
VMEM = pl.BlockSpec(memory_space=pltpu.VMEM)


def density_call(pairs, wanted, count, view, consts, unroll=2, rows=64):
    return pl.pallas_call(
        functools.partial(density_kernel, unroll, rows),
        out_shape=jax.ShapeDtypeStruct((NVIEW, CELL), F32),
        in_specs=[SMEM] * 3 + [VMEM] * 2,
        out_specs=VMEM,
        scratch_shapes=[
            pltpu.VMEM((28, 32, CELL), BF),
            pltpu.VMEM((28, 32, CELL), BF),
            pltpu.VMEM((CELL, CELL), BF),
            pltpu.VMEM((NVIEW, 32, CELL), BF),
            pltpu.VMEM((CPD, CELL, DEPTH), BF),
            pltpu.VMEM((CPD, CELL, CELL), F32),
            pltpu.VMEM((CPD, CELL, CELL), F32),
            pltpu.VMEM((CPD, CELL, CELL), F32),
            pltpu.VMEM((NVIEW, 8, CELL), F32),
        ]
        + [pltpu.VMEM((CELL, CELL), F32)] * unroll,
        compiler_params=pltpu.CompilerParams(vmem_limit_bytes=48 << 20),
        name="density_pairs",
    )(pairs, wanted, count, view, *consts)


def force_call(pairs, wanted, count, view, coef, rho, active, consts, unroll=2, rows=64):
    return pl.pallas_call(
        functools.partial(force_kernel, unroll, rows),
        out_shape=(
            jax.ShapeDtypeStruct((GROUPS, 3, 8, CELL), F32),
            jax.ShapeDtypeStruct((CPD, CELL), F32),
        ),
        in_specs=[SMEM] * 4 + [VMEM] * 4,
        out_specs=(VMEM, VMEM),
        scratch_shapes=[
            pltpu.VMEM((28, 32, CELL), BF),
            pltpu.VMEM((28, 32, CELL), BF),
            pltpu.VMEM((CELL, CELL), BF),
            pltpu.VMEM((NVIEW, 32, CELL), BF),
            pltpu.VMEM((CPD, CELL, DEPTH), BF),
            pltpu.VMEM((CPD, CELL, CELL), F32),
            pltpu.VMEM((CPD, CELL, CELL), F32),
            pltpu.VMEM((CPD, 3, CELL, CELL), F32),
            pltpu.VMEM((CPD, 16, CELL), F32),
            pltpu.VMEM((4, NVIEW, 8, CELL), F32),
        ]
        + [pltpu.VMEM((CELL, CELL), F32)] * unroll,
        compiler_params=pltpu.CompilerParams(vmem_limit_bytes=48 << 20),
        name="force_pairs",
    )(pairs, wanted, count, active, view, coef, rho, *consts)


def spot():
    t = lax.axis_index("dom")
    return t // N_X, lax.rem(t, N_X), lax.axis_index("slab")


def group_of(z, x):
    return CPD // 8 + x * N_Z + z


def barrier(steps):
    z, x, s = spot()
    sem = pltpu.get_barrier_semaphore()
    peers = [{"dom": peer_at(z + i, x + j)} for i, j in steps]
    peers += [{"slab": (s + k) & (N_SLAB - 1)} for k in (1, N_SLAB - 1)]
    for peer in peers:
        pl.semaphore_signal(sem, inc=1, device_id=peer, device_id_type=MESH)
    pl.semaphore_wait(sem, len(peers))


def peer_at(z, x):
    return (z & (N_Z - 1)) * N_X + (x & (N_X - 1))


def far_first(steps):
    return sorted(steps, key=lambda at: -min(at[0], N_Z - at[0]) - min(at[1], N_X - at[1]))


ALL_STEPS = far_first((i, j) for i in range(N_Z) for j in range(N_X) if i or j)
AXIS_STEPS = far_first((i, j) for i, j in ALL_STEPS if i == 0 or j == 0)


def copy_to(src, dst, sems, k, peer):
    return pltpu.make_async_remote_copy(
        src_ref=src, dst_ref=dst, send_sem=sems[0].at[k], recv_sem=sems[1].at[k],
        device_id=peer, device_id_type=MESH,
    )


def z_copies(refs, sems):
    z, x, _ = spot()
    out = []
    for k in (4, 3, 5, 2, 6, 1, 7):
        to = (z + k) & (N_Z - 1)
        out.append((k, copy_to(*refs(to), sems, k, {"dom": to * N_X + x})))
    return dict(out)


def x_copies(refs, sems, base=0):
    z, x, _ = spot()
    out = []
    for k in (2, 1, 3):
        to = (x + k) & (N_X - 1)
        out.append(copy_to(*refs(to), sems, base + k, {"dom": z * N_X + to}))
    return out


def peer_copies(refs, sems):
    z, x, _ = spot()
    out = []
    for i, j in ALL_STEPS:
        group = group_of((z + i) & (N_Z - 1), (x + j) & (N_X - 1))
        out.append(
            copy_to(*refs(group), sems, i * N_X + j, {"dom": peer_at(z + i, x + j)})
        )
    return out


def face_copies(lower, upper, sems):
    s = lax.axis_index("slab")
    return [
        copy_to(*lower, sems, 0, {"slab": (s + N_SLAB - 1) & (N_SLAB - 1)}),
        copy_to(*upper, sems, 1, {"slab": (s + 1) & (N_SLAB - 1)}),
    ]


def start(copies):
    for copy in copies:
        copy.start()


def arrive(copies):
    for copy in copies:
        copy.wait_recv()


def leave(copies):
    for copy in copies:
        copy.wait_send()


def gather_kernel(boundary, positions, smoothing, view, offered, *sems):
    z, x, _ = spot()
    face_sems, z_sems, x_sems = sems[:2], sems[2:4], sems[4:6]
    for g in range(CPD // 8):
        for c in range(3):
            view[g, c] = positions[c, g * 8 : g * 8 + 8, :]
        view[g, 3] = smoothing[g * 8 : g * 8 + 8, :]
    for b in range(8):
        cell = boundary[b]
        for c in range(4):
            offered[c, b : b + 1, :] = view_row(view, c, cell)
    here = group_of(z, x)
    view[here] = offered[...]
    barrier(AXIS_STEPS)
    along_z = z_copies(lambda to: (offered, view.at[here]), z_sems)
    faces = face_copies(
        (view.at[0], view.at[GROUPS - 1]), (view.at[CPD // 8 - 1], view.at[GROUPS - 2]), face_sems
    )
    start(along_z.values())
    along_x = x_copies(lambda to: (offered, view.at[here]), x_sems)
    start(along_x)
    start(faces)
    for k in (1, 7, 2, 6, 3, 5, 4):
        along_z[k].wait_recv()
        block = view.at[group_of((z - k) & (N_Z - 1), x)]
        onward = x_copies(lambda to: (block, block), x_sems, k * N_X)
        start(onward)
        along_x += onward
    arrive(along_x + faces)
    leave(list(along_z.values()) + along_x + faces)


def settle(own, arrived, lower, upper, boundary):
    row = lax.broadcasted_iota(jnp.int32, (CPD, CELL), 0)
    for b in range(8):
        own += jnp.where(row == boundary[b], jnp.broadcast_to(arrived[b : b + 1], own.shape), 0.0)
    return jnp.concatenate([own[:8] + lower, own[8:24], own[24:] + upper], axis=0)


def sum_back(partial, arrived, faces, face_sems, sems):
    z, x, _ = spot()
    here = group_of(z, x)
    copies = peer_copies(lambda group: (partial.at[group], arrived.at[here - CPD // 8]), sems)
    copies += face_copies(
        (partial.at[GROUPS - 2], faces.at[1]), (partial.at[GROUPS - 1], faces.at[0]), face_sems
    )
    start(copies)
    arrived[here - CPD // 8] = partial[here]
    arrive(copies)
    total = arrived[0]
    for k in range(1, N_Z * N_X):
        total += arrived[k]
    return total, copies


def factor_kernel(
    boundary, partial, smoothing, energy, rho, coef, arrived, faces, offered, mine, *sems
):
    z, x, _ = spot()
    barrier(ALL_STEPS)
    h2 = smoothing[...] * smoothing[...]
    h4 = h2 * h2
    inverse = 1.0 / (h4 * h4)
    total, copies = sum_back(partial, arrived, faces, sems[0:2], sems[2:4])
    own = partial[0 : CPD // 8].reshape(CPD, CELL)
    raw = settle(own, total, faces[0], faces[1], boundary)
    density = (4.0 * NORM / CELL) * inverse * raw
    rho[...] = density
    slope = (40.0 / 3.0 * NORM / CELL) * inverse * energy[...] / density
    for g in range(CPD // 8):
        coef[g] = slope[g * 8 : g * 8 + 8]
    mine[...] = slope
    for b in range(8):
        offered[b : b + 1, :] = mine[pl.ds(boundary[b], 1), :]
    here = group_of(z, x)
    coef[here] = offered[...]
    back = peer_copies(lambda group: (offered, coef.at[here]), sems[6:8])
    back += face_copies(
        (coef.at[0], coef.at[GROUPS - 1]), (coef.at[CPD // 8 - 1], coef.at[GROUPS - 2]), sems[4:6]
    )
    start(back)
    leave(copies)
    arrive(back)
    leave(back)


def settle_kernel(boundary, partial, accel, arrived, faces, *sems):
    barrier(ALL_STEPS)
    total, copies = sum_back(partial, arrived, faces, sems[0:2], sems[2:4])
    for c in range(3):
        own = jnp.concatenate([partial[g, c] for g in range(CPD // 8)], axis=0)
        accel[c] = settle(own, total[c], faces[0, c], faces[1, c], boundary)
    leave(copies)


def comm_call(kernel, collective, out_shape, scratch, n_sems, operands):
    return pl.pallas_call(
        kernel,
        out_shape=out_shape,
        in_specs=[SMEM] + [VMEM] * (len(operands) - 1),
        out_specs=jax.tree.map(lambda _: VMEM, out_shape),
        scratch_shapes=[pltpu.VMEM(dims, F32) for dims in scratch]
        + [pltpu.SemaphoreType.DMA((n,)) for n in n_sems for _ in (0, 1)],
        compiler_params=pltpu.CompilerParams(collective_id=collective, has_side_effects=True),
        name=kernel.__name__,
    )(*operands)


def per_device(positions, smoothing, energy, active, boundary, wanted, cell_pairs, pair_count):
    consts = tables()
    offers = boundary[0]
    pairs = cell_pairs.reshape(-1)
    taken = wanted.reshape(-1)
    shape = lambda *dims: jax.ShapeDtypeStruct(dims, F32)
    rows = (8, CELL)
    view = comm_call(
        gather_kernel, 0, shape(GROUPS, 4, *rows), [(4, *rows)], (2, N_Z, N_Z * N_X),
        (offers, positions.transpose(1, 0, 2), smoothing),
    )
    partial = density_call(pairs, taken, pair_count, view, consts, 16, 32)
    rho, coef = comm_call(
        factor_kernel, 1, (shape(CPD, CELL), shape(GROUPS, *rows)),
        [(N_Z * N_X, *rows), (2, *rows), rows, (CPD, CELL)],
        (2, N_Z * N_X, 2, N_Z * N_X),
        (offers, partial.reshape(GROUPS, *rows), smoothing, energy),
    )
    force, density = force_call(pairs, taken, pair_count, view, coef, rho, active, consts, 16, 32)
    accel = comm_call(
        settle_kernel, 2, shape(3, CPD, CELL),
        [(N_Z * N_X, 3, *rows), (2, 3, *rows)],
        (2, N_Z * N_X),
        (offers, force),
    )
    live = jnp.arange(CELL, dtype=jnp.int32)[None, :] < active[:, None]
    return density, jnp.where(live[:, None, :], accel.transpose(1, 0, 2), 0.0)


def solution(mesh):
    in_specs = (
        P(("slab", "dom"), None, None),
        P(("slab", "dom"), None),
        P(("slab", "dom"), None),
        P(("slab", "dom")),
        P(("slab", "dom"), None),
        P(("slab", "dom"), None, None),
        P(("slab", "dom"), None, None),
        P(("slab", "dom")),
    )
    out_specs = (P(("slab", "dom"), None), P(("slab", "dom"), None, None))
    return jax.shard_map(
        per_device, mesh=mesh, in_specs=in_specs, out_specs=out_specs, check_vma=False
    )
```

```python
import functools
import jax
import jax.numpy as jnp
import numpy as np
from jax import lax
from jax.experimental import pallas as pl
from jax.experimental.pallas import tpu as pltpu
from jax.sharding import PartitionSpec as P

CELL, CPD, NVIEW, GROUPS, PAIRS = 128, 32, 304, 38, 448
NORM = 21.0 / (2.0 * 3.141592653589793)
BF = jnp.bfloat16
F32 = jnp.float32
TINY = 1e-30
N_Z, N_X, N_SLAB = 8, 4, 8
MESH = pl.DeviceIdType.MESH
DEPTH = 80
NT = (((1,), (1,)), ((), ()))


def tables():
    sel = np.zeros((DEPTH, 32), np.float32)
    first, second, third, one = 0, 8, 24, 4
    for c in range(3):
        for part, base in ((first, 0), (second, 16), (third, 32)):
            sel[base + c, part + c] = -0.5
            sel[base + 5 + c, part + c] = -0.5
        sel[8 + c, first + c] = -0.5
        sel[24 + c, second + c] = -0.5
        sel[40 + c, first + c] = -0.5
        for base in (48, 56, 72):
            sel[base + c, one] = 1.0
    sel[3, one] = sel[11, one] = sel[12, one] = sel[43, one] = 1.0
    sel[4, first + 3] = sel[20, second + 3] = sel[36, third + 3] = 1.0
    return (jnp.asarray(sel, BF),)


def build_constants(shift, scale, eye):
    row = lax.broadcasted_iota(jnp.int32, (8, CELL), 0)
    none = jnp.zeros((8, CELL), F32)
    for d in range(28):
        offset = (d // 9 - 1, d // 3 % 3 - 1, d % 3 - 1) if d < 27 else (0, 0, 0)
        length = sum(o * o for o in offset) if d < 27 else 16384
        moved, turned = none, none
        for c, o in enumerate(offset):
            if o:
                moved = jnp.where(row == 5 + c, -2.0 * o, moved)
                turned = jnp.where(row == c, -1.0 * o, turned)
        far = jnp.where(row == 4, 1.0 * length, none)
        shift[d] = jnp.concatenate([moved, far, moved, none], axis=0).astype(BF)
        scale[d] = jnp.concatenate([turned, turned, none, turned], axis=0).astype(BF)
    down = lax.broadcasted_iota(jnp.int32, (CELL, CELL), 0)
    across = lax.broadcasted_iota(jnp.int32, (CELL, CELL), 1)
    eye[...] = jnp.where(down == across, 1.0, 0.0).astype(BF)


def view_row(view, c, v):
    return view[v // 8, c, pl.ds(lax.rem(v, 8), 1), :]


def spread_columns(planes, put):
    turned = jnp.concatenate(planes, axis=0).T

    def some(g, turned):
        for k in range(4):
            for c in range(4):
                column = turned[:, c * CPD + k : c * CPD + k + 1]
                put(g * 4 + k, c, jnp.broadcast_to(column, (CELL, CELL)))
        return pltpu.roll(turned, CELL - 4, 1)

    lax.fori_loop(0, CPD // 4, some, turned)


def row_sums(load):
    lane = lax.broadcasted_iota(jnp.int32, (CELL, CELL), 1)

    def some(g, table):
        for k in range(8):
            u = g * 8 + k
            table = jnp.where(lane == u, jnp.sum(load(u), axis=1, keepdims=True), table)
        return table

    return lax.fori_loop(0, CPD // 8, some, jnp.zeros((CELL, CELL), F32)).T[0:CPD]


def own_plane(ref, *at):
    return jnp.concatenate([ref[(g, *at)] for g in range(CPD // 8)], axis=0)


def build_left(vv, sel, eye, at):
    def some(g, _):
        for k in range(8):
            u = g * 8 + k
            picked = jnp.dot(sel[...], vv[u], preferred_element_type=F32).astype(BF)
            cols = lax.dot_general(eye[...], picked, NT, preferred_element_type=F32)
            at[u] = cols.astype(BF)
        return 0

    lax.fori_loop(0, CPD // 8, some, 0)


def sweep(total, place, fill, use, buffers):
    half = len(buffers) // 2
    sides = buffers[:half], buffers[half:]

    def some(i, _):
        for side in (0, 1):
            for s in range(half):
                p = (2 * i + side) * half + s
                fill(sides[1 - side][s], place(p + half))
                use(place(p), sides[side][s])
        return 0

    for s in range(half):
        fill(sides[0][s], place(s))
    lax.fori_loop(0, pl.cdiv(total, 2 * half), some, 0)


def build_cell_tables(view, vv):
    row = lax.broadcasted_iota(jnp.int32, (8, CELL), 0)

    def one_cell(g, k):
        x, y, z = (
            jnp.broadcast_to(view[g, c, pl.ds(k, 1), :], (8, CELL)) - 0.5 for c in range(3)
        )
        n = x * x + y * y + z * z
        w = jnp.where(row == 3, n, jnp.where(row == 4, 1.0, 0.0))
        w = jnp.where(row == 0, -2.0 * x, w)
        w = jnp.where(row == 1, -2.0 * y, w)
        w = jnp.where(row == 2, -2.0 * z, w)
        t1 = w.astype(BF).astype(F32)
        r1 = w - t1
        t2 = r1.astype(BF).astype(F32)
        t3 = r1 - t2
        return jnp.concatenate([t1, t2, t1, t3], axis=0).astype(BF)

    def group(g, _):
        for k in range(8):
            vv[g * 8 + k] = one_cell(g, k)
        return 0

    lax.fori_loop(0, GROUPS, group, 0)


def right_operand(vv, shift, scale, v, d):
    cell = vv[v]
    moved = cell + shift[d]
    turned = cell * scale[d]
    return jnp.concatenate([moved[:16], moved[:16], moved[16:], turned], axis=0)


def dist2(at, vv, shift, scale, u, v, d):
    return jnp.dot(
        at[u], right_operand(vv, shift, scale, v, d), preferred_element_type=F32
    )


def root(r2):
    r2 = jnp.maximum(r2, TINY)
    return r2 * lax.rsqrt(r2)


def fold_rows(w):
    return jnp.sum(w.reshape(-1, 8, CELL), axis=0)


def scalars(pairs, wanted, count, p):
    p = jnp.minimum(p, PAIRS - 1) if not isinstance(p, int) else p
    u, v = pairs[0, p], pairs[1, p]
    d = jnp.where(p < count, pairs[2, p], 27)
    slot = jnp.clip(v - CPD, 0, 255)
    q = slot >> 3
    offered = CPD + (q & 3) * 64 + (q >> 2) * 8 + wanted[slot & 7, q]
    v = jnp.where((v >= CPD) & (v < CPD + 256), offered, v)
    return u, v, d


def density_kernel(
    unroll, rows,
    pairs, wanted, count, view_in, sel, out,
    shift, scale, eye, vv, at, hb, hq, acc_l, acc_r, view, came, *buffers,
):
    coming = pltpu.make_async_copy(view_in, view, came.at[0])
    coming.start()
    build_constants(shift, scale, eye)

    def clear(g, _):
        acc_r[pl.ds(g * 8, 8)] = jnp.zeros((8, 8, CELL), F32)
        return 0

    lax.fori_loop(0, GROUPS, clear, 0)
    coming.wait()
    build_cell_tables(view, vv)

    build_left(vv, sel, eye, at)

    def put(u, c, column):
        if c == 0:
            hb[u] = column
        elif c == 1:
            hq[u] = column
        elif c == 2:
            acc_l[u] = jnp.zeros((CELL, CELL), F32)

    h = own_plane(view, 3)
    spread_columns([h, 1.25 * h, h, h], put)

    d2 = functools.partial(dist2, at, vv, shift, scale)
    chunks = range(CELL // rows)

    def fill(buffer, where):
        buffer[...] = d2(*where)

    def self_tile(where, r2):
        u = where[0]
        h_r = jnp.broadcast_to(view_row(view, 3, u), (rows, CELL))
        q_r = 1.25 * h_r
        total = jnp.zeros((8, CELL), F32)
        for c in chunks:
            r = root(r2[c * rows : c * rows + rows, :])
            f = jnp.maximum(h_r - r, 0.0)
            f2 = f * f
            total += fold_rows(f2 * f2 * (q_r - f))
        acc_r[u] = total

    def self_place(p):
        u = jnp.minimum(p, CPD - 1)
        return u, u, 13

    sweep(CPD, self_place, fill, self_tile, buffers[:CPD])

    n = count[0]
    place = functools.partial(scalars, pairs, wanted, n)

    def tile(where, r2):
        u, v, _ = where
        h_r = jnp.broadcast_to(view_row(view, 3, v), (rows, CELL))
        q_r = 1.25 * h_r
        total = acc_r[v]
        for c in chunks:
            at_rows = pl.ds(c * rows, rows)
            r = root(r2[c * rows : c * rows + rows, :])
            f = jnp.maximum(hb[u, at_rows, :] - r, 0.0)
            f2 = f * f
            acc_l[u, at_rows, :] += f2 * f2 * (hq[u, at_rows, :] - f)
            f = jnp.maximum(h_r - r, 0.0)
            f2 = f * f
            total += fold_rows(f2 * f2 * (q_r - f))
        acc_r[v] = total

    sweep(n, place, fill, tile, buffers)

    def finish(g, _):
        out[pl.ds(g * 8, 8), :] = jnp.sum(acc_r[pl.ds(g * 8, 8)], axis=1)
        return 0

    lax.fori_loop(0, GROUPS, finish, 0)
    out[0:CPD, :] += row_sums(lambda u: acc_l[u])


def force_kernel(
    unroll, rows,
    pairs, wanted, count, active, view_in, coef_in, rho_in, sel, out, density,
    shift, scale, eye, vv, at, hb, cb, xb, acc_l, acc_r, view, coef, rho, came, *buffers,
):
    coming = [
        pltpu.make_async_copy(src, dst, came.at[i])
        for i, (src, dst) in enumerate(((view_in, view), (coef_in, coef), (rho_in, rho)))
    ]
    for copy in coming:
        copy.start()
    build_constants(shift, scale, eye)

    def clear(g, _):
        for c in range(4):
            acc_r[c, pl.ds(g * 8, 8)] = jnp.zeros((8, 8, CELL), F32)
        return 0

    lax.fori_loop(0, GROUPS, clear, 0)
    acc_l[...] = jnp.zeros(acc_l.shape, F32)
    for copy in coming:
        copy.wait()
    row = lax.broadcasted_iota(jnp.int32, (CPD, CELL), 0)
    live = jnp.zeros((CPD, CELL), jnp.int32)
    for u in range(CPD):
        live = jnp.where(row == u, active[u], live)
    lane = lax.broadcasted_iota(jnp.int32, (CPD, CELL), 1)
    density[...] = jnp.where(lane < live, rho[...], 0.0)
    build_cell_tables(view, vv)

    build_left(vv, sel, eye, at)

    def put(u, c, column):
        if c == 3:
            hb[u] = column
        else:
            xb[u, c] = column

    def put_coef(u, c, column):
        if c == 0:
            cb[u] = column

    spread_columns([own_plane(view, c) - (0.5 if c < 3 else 0.0) for c in range(4)], put)
    spread_columns([own_plane(coef)] * 4, put_coef)

    d2 = functools.partial(dist2, at, vv, shift, scale)
    chunks = range(CELL // rows)

    def tile(both, where, r2):
        u, v, d = where
        h_r = jnp.broadcast_to(view_row(view, 3, v), (rows, CELL))
        c_r = jnp.broadcast_to(coef[v // 8, pl.ds(lax.rem(v, 8), 1), :], (rows, CELL))
        total = [jnp.zeros((8, CELL), F32)] * 4
        tops, rests = [], []
        for k in chunks:
            at_rows = pl.ds(k * rows, rows)
            r = root(r2[k * rows : k * rows + rows, :])
            f = jnp.maximum(hb[u, at_rows, :] - r, 0.0)
            s = f * f * (f * cb[u, at_rows, :])
            f = jnp.maximum(h_r - r, 0.0)
            s += f * f * (f * c_r)
            for c in range(3):
                total[c] += fold_rows(s * xb[u, c, at_rows, :])
            total[3] += fold_rows(s)
            if both:
                top = s.astype(BF)
                tops.append(top)
                rests.append((s - top.astype(F32)).astype(BF))
        if both:
            right = vv[v, 0:16, :] + shift[d, 0:16, :]
            acc_l[u] += lax.dot_general(
                jnp.concatenate([right, right], axis=1),
                jnp.concatenate(
                    [jnp.concatenate(tops, axis=0), jnp.concatenate(rests, axis=0)], axis=1
                ),
                NT,
                preferred_element_type=F32,
            )
        offset = (d // 9 - 1, lax.rem(d // 3, 3) - 1, lax.rem(d, 3) - 1)
        for c in range(3):
            acc_r[c, v] += total[c] - offset[c].astype(F32) * total[3]
        acc_r[3, v] += total[3]

    def fill(buffer, where):
        buffer[...] = d2(*where)

    def self_place(p):
        u = jnp.minimum(p, CPD - 1)
        return u, u, jnp.int32(13)

    sweep(CPD, self_place, fill, functools.partial(tile, False), buffers[:CPD])

    n = count[0]
    place = functools.partial(scalars, pairs, wanted, n)

    sweep(n, place, fill, functools.partial(tile, True), buffers)

    def finish(g, _):
        whole = jnp.sum(acc_r[3, pl.ds(g * 8, 8)], axis=1)
        for c in range(3):
            out[g, c] = (view[g, c] - 0.5) * whole - jnp.sum(acc_r[c, pl.ds(g * 8, 8)], axis=1)
        return 0

    lax.fori_loop(0, GROUPS, finish, 0)
    for g in range(CPD // 8):
        rows_of = lambda r: jnp.concatenate(
            [acc_l[g * 8 + k, r : r + 1, :] for k in range(8)], axis=0
        )
        whole = rows_of(4)
        for c in range(3):
            moved = rows_of(c) + rows_of(8 + c) + rows_of(5 + c)
            out[g, c] += (view[g, c] - 0.5) * whole + 0.5 * moved


SMEM = pl.BlockSpec(memory_space=pltpu.SMEM)
VMEM = pl.BlockSpec(memory_space=pltpu.VMEM)
ANY = pl.BlockSpec(memory_space=pl.ANY)


def density_call(pairs, wanted, count, view, consts, unroll=2, rows=64):
    return pl.pallas_call(
        functools.partial(density_kernel, unroll, rows),
        out_shape=jax.ShapeDtypeStruct((NVIEW, CELL), F32),
        in_specs=[SMEM] * 3 + [ANY, VMEM],
        out_specs=VMEM,
        scratch_shapes=[
            pltpu.VMEM((28, 32, CELL), BF),
            pltpu.VMEM((28, 32, CELL), BF),
            pltpu.VMEM((CELL, CELL), BF),
            pltpu.VMEM((NVIEW, 32, CELL), BF),
            pltpu.VMEM((CPD, CELL, DEPTH), BF),
            pltpu.VMEM((CPD, CELL, CELL), F32),
            pltpu.VMEM((CPD, CELL, CELL), F32),
            pltpu.VMEM((CPD, CELL, CELL), F32),
            pltpu.VMEM((NVIEW, 8, CELL), F32),
            pltpu.VMEM((GROUPS, 4, 8, CELL), F32),
            pltpu.SemaphoreType.DMA((1,)),
        ]
        + [pltpu.VMEM((CELL, CELL), F32)] * unroll,
        compiler_params=pltpu.CompilerParams(vmem_limit_bytes=62 << 20),
        name="density_pairs",
    )(pairs, wanted, count, view, *consts)


def force_call(pairs, wanted, count, view, coef, rho, active, consts, unroll=2, rows=64):
    return pl.pallas_call(
        functools.partial(force_kernel, unroll, rows),
        out_shape=(
            jax.ShapeDtypeStruct((GROUPS, 3, 8, CELL), F32),
            jax.ShapeDtypeStruct((CPD, CELL), F32),
        ),
        in_specs=[SMEM] * 4 + [ANY] * 3 + [VMEM],
        out_specs=(VMEM, VMEM),
        scratch_shapes=[
            pltpu.VMEM((28, 32, CELL), BF),
            pltpu.VMEM((28, 32, CELL), BF),
            pltpu.VMEM((CELL, CELL), BF),
            pltpu.VMEM((NVIEW, 32, CELL), BF),
            pltpu.VMEM((CPD, CELL, DEPTH), BF),
            pltpu.VMEM((CPD, CELL, CELL), F32),
            pltpu.VMEM((CPD, CELL, CELL), F32),
            pltpu.VMEM((CPD, 3, CELL, CELL), F32),
            pltpu.VMEM((CPD, 16, CELL), F32),
            pltpu.VMEM((4, NVIEW, 8, CELL), F32),
            pltpu.VMEM((GROUPS, 4, 8, CELL), F32),
            pltpu.VMEM((GROUPS, 8, CELL), F32),
            pltpu.VMEM((CPD, CELL), F32),
            pltpu.SemaphoreType.DMA((3,)),
        ]
        + [pltpu.VMEM((CELL, CELL), F32)] * unroll,
        compiler_params=pltpu.CompilerParams(vmem_limit_bytes=62 << 20),
        name="force_pairs",
    )(pairs, wanted, count, active, view, coef, rho, *consts)


def spot():
    t = lax.axis_index("dom")
    return t // N_X, lax.rem(t, N_X), lax.axis_index("slab")


def group_of(z, x):
    return CPD // 8 + x * N_Z + z


def barrier(steps, meanwhile=lambda: None):
    z, x, s = spot()
    sem = pltpu.get_barrier_semaphore()
    peers = [{"dom": peer_at(z + i, x + j)} for i, j in steps]
    peers += [{"slab": (s + k) & (N_SLAB - 1)} for k in (1, N_SLAB - 1)]
    for peer in peers:
        pl.semaphore_signal(sem, inc=1, device_id=peer, device_id_type=MESH)
    meanwhile()
    pl.semaphore_wait(sem, len(peers))


def peer_at(z, x):
    return (z & (N_Z - 1)) * N_X + (x & (N_X - 1))


def far_first(steps):
    return sorted(steps, key=lambda at: -min(at[0], N_Z - at[0]) - min(at[1], N_X - at[1]))


ALL_STEPS = far_first((i, j) for i in range(N_Z) for j in range(N_X) if i or j)
AXIS_STEPS = far_first((i, j) for i, j in ALL_STEPS if i == 0 or j == 0)


def copy_to(src, dst, sems, k, peer):
    return pltpu.make_async_remote_copy(
        src_ref=src, dst_ref=dst, send_sem=sems[0].at[k], recv_sem=sems[1].at[k],
        device_id=peer, device_id_type=MESH,
    )


def z_copies(refs, sems):
    z, x, _ = spot()
    out = []
    for k in (4, 3, 5, 2, 6, 1, 7):
        to = (z + k) & (N_Z - 1)
        out.append((k, copy_to(*refs(to), sems, k, {"dom": to * N_X + x})))
    return dict(out)


def x_copies(refs, sems, base=0):
    z, x, _ = spot()
    out = []
    for k in (2, 1, 3):
        to = (x + k) & (N_X - 1)
        out.append(copy_to(*refs(to), sems, base + k, {"dom": z * N_X + to}))
    return out


def peer_copies(refs, sems):
    z, x, _ = spot()
    out = []
    for i, j in ALL_STEPS:
        group = group_of((z + i) & (N_Z - 1), (x + j) & (N_X - 1))
        out.append(
            copy_to(*refs(group), sems, i * N_X + j, {"dom": peer_at(z + i, x + j)})
        )
    return out


def face_copies(lower, upper, sems):
    s = lax.axis_index("slab")
    return [
        copy_to(*lower, sems, 0, {"slab": (s + N_SLAB - 1) & (N_SLAB - 1)}),
        copy_to(*upper, sems, 1, {"slab": (s + 1) & (N_SLAB - 1)}),
    ]


def start(copies):
    for copy in copies:
        copy.start()


def arrive(copies):
    for copy in copies:
        copy.wait_recv()


def leave(copies):
    for copy in copies:
        copy.wait_send()


def leave_local(copies):
    for copy in copies:
        copy.wait()


def pack(boundary, positions, smoothing, view, offered, here, local):
    leave_local(local)
    for g in range(CPD // 8):
        for c in range(3):
            view[g, c] = positions[c, g * 8 : g * 8 + 8, :]
        view[g, 3] = smoothing[g * 8 : g * 8 + 8, :]
    for b in range(8):
        cell = boundary[b]
        for c in range(3):
            offered[c, b : b + 1, :] = positions[c, pl.ds(cell, 1), :]
        offered[3, b : b + 1, :] = smoothing[pl.ds(cell, 1), :]
    view[here] = offered[...]


def gather_kernel(boundary, positions_in, smoothing_in, view, offered, positions, smoothing, near, *sems):
    z, x, _ = spot()
    local = [
        pltpu.make_async_copy(positions_in, positions, near.at[0]),
        pltpu.make_async_copy(smoothing_in, smoothing, near.at[1]),
    ]
    start(local)
    here = group_of(z, x)
    barrier(AXIS_STEPS, lambda: pack(boundary, positions, smoothing, view, offered, here, local))
    face_sems, z_sems, x_sems = sems[:2], sems[2:4], sems[4:6]
    along_z = z_copies(lambda to: (offered, view.at[here]), z_sems)
    faces = face_copies(
        (view.at[0], view.at[GROUPS - 1]), (view.at[CPD // 8 - 1], view.at[GROUPS - 2]), face_sems
    )
    start(along_z.values())
    along_x = x_copies(lambda to: (offered, view.at[here]), x_sems)
    start(along_x)
    start(faces)
    for k in (1, 7, 2, 6, 3, 5, 4):
        along_z[k].wait_recv()
        block = view.at[group_of((z - k) & (N_Z - 1), x)]
        onward = x_copies(lambda to: (block, block), x_sems, k * N_X)
        start(onward)
        along_x += onward
    arrive(along_x + faces)
    leave(list(along_z.values()) + along_x + faces)


def settle(own, arrived, lower, upper, boundary):
    row = lax.broadcasted_iota(jnp.int32, (CPD, CELL), 0)
    for b in range(8):
        own += jnp.where(row == boundary[b], jnp.broadcast_to(arrived[b : b + 1], own.shape), 0.0)
    return jnp.concatenate([own[:8] + lower, own[8:24], own[24:] + upper], axis=0)


def sum_back(partial, arrived, faces, face_sems, sems, near):
    z, x, _ = spot()
    here = group_of(z, x)
    copies = peer_copies(lambda group: (partial.at[group], arrived.at[here - CPD // 8]), sems)
    copies += face_copies(
        (partial.at[GROUPS - 2], faces.at[1]), (partial.at[GROUPS - 1], faces.at[0]), face_sems
    )
    start(copies)
    mine = pltpu.make_async_copy(partial.at[here], arrived.at[here - CPD // 8], near)
    mine.start()
    mine.wait()
    arrive(copies)
    total = arrived[0]
    for k in range(1, N_Z * N_X):
        total += arrived[k]
    return total, copies


def factor_kernel(
    boundary, partial, smoothing_in, energy_in, rho, coef,
    arrived, faces, offered, mine, own, smoothing, energy, near, *sems,
):
    z, x, _ = spot()
    local = [
        pltpu.make_async_copy(src, dst, near.at[i])
        for i, (src, dst) in enumerate(
            ((partial.at[pl.ds(0, CPD // 8)], own), (smoothing_in, smoothing), (energy_in, energy))
        )
    ]
    start(local)
    barrier(ALL_STEPS)
    total, copies = sum_back(partial, arrived, faces, sems[0:2], sems[2:4], near.at[3])
    leave_local(local)
    h2 = smoothing[...] * smoothing[...]
    h4 = h2 * h2
    inverse = 1.0 / (h4 * h4)
    raw = settle(own[...].reshape(CPD, CELL), total, faces[0], faces[1], boundary)
    density = (4.0 * NORM / CELL) * inverse * raw
    rho[...] = density
    slope = (40.0 / 3.0 * NORM / CELL) * inverse * energy[...] / density
    for g in range(CPD // 8):
        coef[g] = slope[g * 8 : g * 8 + 8]
    mine[...] = slope
    for b in range(8):
        offered[b : b + 1, :] = mine[pl.ds(boundary[b], 1), :]
    here = group_of(z, x)
    coef[here] = offered[...]
    back = peer_copies(lambda group: (offered, coef.at[here]), sems[6:8])
    back += face_copies(
        (coef.at[0], coef.at[GROUPS - 1]), (coef.at[CPD // 8 - 1], coef.at[GROUPS - 2]), sems[4:6]
    )
    start(back)
    leave(copies)
    arrive(back)
    leave(back)


def settle_kernel(boundary, partial, accel, arrived, faces, own, near, *sems):
    local = [pltpu.make_async_copy(partial.at[pl.ds(0, CPD // 8)], own, near.at[0])]
    start(local)
    barrier(ALL_STEPS)
    total, copies = sum_back(partial, arrived, faces, sems[0:2], sems[2:4], near.at[1])
    leave_local(local)
    for c in range(3):
        kept = jnp.concatenate([own[g, c] for g in range(CPD // 8)], axis=0)
        accel[c] = settle(kept, total[c], faces[0, c], faces[1, c], boundary)
    leave(copies)


def comm_call(kernel, collective, out_shape, scratch, n_near, n_sems, operands):
    return pl.pallas_call(
        kernel,
        out_shape=out_shape,
        in_specs=[SMEM] + [ANY] * (len(operands) - 1),
        out_specs=jax.tree.map(lambda _: VMEM, out_shape),
        scratch_shapes=[pltpu.VMEM(dims, F32) for dims in scratch]
        + [pltpu.SemaphoreType.DMA((n_near,))]
        + [pltpu.SemaphoreType.DMA((n,)) for n in n_sems for _ in (0, 1)],
        compiler_params=pltpu.CompilerParams(collective_id=collective, has_side_effects=True),
        name=kernel.__name__,
    )(*operands)


def per_device(positions, smoothing, energy, active, boundary, wanted, cell_pairs, pair_count):
    consts = tables()
    offers = boundary[0]
    pairs = cell_pairs[0].T
    taken = wanted[0].T
    shape = lambda *dims: jax.ShapeDtypeStruct(dims, F32)
    rows = (8, CELL)
    view = comm_call(
        gather_kernel, 0, shape(GROUPS, 4, *rows), [(4, *rows), (3, CPD, CELL), (CPD, CELL)], 2,
        (2, N_Z, N_Z * N_X),
        (offers, positions.transpose(1, 0, 2), smoothing),
    )
    partial = density_call(pairs, taken, pair_count, view, consts, 32, 128)
    rho, coef = comm_call(
        factor_kernel, 1, (shape(CPD, CELL), shape(GROUPS, *rows)),
        [(N_Z * N_X, *rows), (2, *rows), rows, (CPD, CELL), (CPD // 8, *rows), (CPD, CELL), (CPD, CELL)],
        4, (2, N_Z * N_X, 2, N_Z * N_X),
        (offers, partial.reshape(GROUPS, *rows), smoothing, energy),
    )
    force, density = force_call(pairs, taken, pair_count, view, coef, rho, active, consts, 32, 128)
    accel = comm_call(
        settle_kernel, 2, shape(3, CPD, CELL),
        [(N_Z * N_X, 3, *rows), (2, 3, *rows), (CPD // 8, 3, *rows)],
        2, (2, N_Z * N_X),
        (offers, force),
    )
    live = jnp.arange(CELL, dtype=jnp.int32)[None, :] < active[:, None]
    return density, jnp.where(live[:, None, :], accel.transpose(1, 0, 2), 0.0)


def solution(mesh):
    in_specs = (
        P(("slab", "dom"), None, None),
        P(("slab", "dom"), None),
        P(("slab", "dom"), None),
        P(("slab", "dom")),
        P(("slab", "dom"), None),
        P(("slab", "dom"), None, None),
        P(("slab", "dom"), None, None),
        P(("slab", "dom")),
    )
    out_specs = (P(("slab", "dom"), None), P(("slab", "dom"), None, None))
    return jax.shard_map(
        per_device, mesh=mesh, in_specs=in_specs, out_specs=out_specs, check_vma=False
    )
```

```python
import functools
import jax
import jax.numpy as jnp
import numpy as np
from jax import lax
from jax.experimental import pallas as pl
from jax.experimental.pallas import tpu as pltpu
from jax.sharding import PartitionSpec as P

CELL, CPD, NVIEW, GROUPS, PAIRS = 128, 32, 304, 38, 448
NORM = 21.0 / (2.0 * 3.141592653589793)
BF = jnp.bfloat16
F32 = jnp.float32
TINY = 1e-30
N_Z, N_X, N_SLAB = 8, 4, 8
MESH = pl.DeviceIdType.MESH
DEPTH = 80
NT = (((1,), (1,)), ((), ()))


def tables():
    sel = np.zeros((DEPTH, 32), np.float32)
    first, second, third, one = 0, 8, 24, 4
    for c in range(3):
        for part, base in ((first, 0), (second, 16), (third, 32)):
            sel[base + c, part + c] = -0.5
            sel[base + 5 + c, part + c] = -0.5
        sel[8 + c, first + c] = -0.5
        sel[24 + c, second + c] = -0.5
        sel[40 + c, first + c] = -0.5
        for base in (48, 56, 72):
            sel[base + c, one] = 1.0
    sel[3, one] = sel[11, one] = sel[12, one] = sel[43, one] = 1.0
    sel[4, first + 3] = sel[20, second + 3] = sel[36, third + 3] = 1.0
    return (jnp.asarray(sel, BF),)


def build_constants(shift, scale, eye):
    row = lax.broadcasted_iota(jnp.int32, (8, CELL), 0)
    none = jnp.zeros((8, CELL), F32)
    for d in range(28):
        offset = (d // 9 - 1, d // 3 % 3 - 1, d % 3 - 1) if d < 27 else (0, 0, 0)
        length = sum(o * o for o in offset) if d < 27 else 16384
        moved, turned = none, none
        for c, o in enumerate(offset):
            if o:
                moved = jnp.where(row == 5 + c, -2.0 * o, moved)
                turned = jnp.where(row == c, -1.0 * o, turned)
        far = jnp.where(row == 4, 1.0 * length, none)
        shift[d] = jnp.concatenate([moved, far, moved, none], axis=0).astype(BF)
        scale[d] = jnp.concatenate([turned, turned, none, turned], axis=0).astype(BF)
    down = lax.broadcasted_iota(jnp.int32, (CELL, CELL), 0)
    across = lax.broadcasted_iota(jnp.int32, (CELL, CELL), 1)
    eye[...] = jnp.where(down == across, 1.0, 0.0).astype(BF)


def view_row(view, c, v):
    return view[v // 8, c, pl.ds(lax.rem(v, 8), 1), :]


def spread_columns(planes, put):
    turned = jnp.concatenate(planes, axis=0).T

    def some(g, turned):
        for k in range(8):
            for c in range(4):
                column = turned[:, c * CPD + k : c * CPD + k + 1]
                put(g * 8 + k, c, jnp.broadcast_to(column, (CELL, CELL)))
        return pltpu.roll(turned, CELL - 8, 1)

    lax.fori_loop(0, CPD // 8, some, turned)


def row_sums(load):
    lane = lax.broadcasted_iota(jnp.int32, (CELL, CELL), 1)

    def some(g, table):
        for k in range(16):
            u = g * 16 + k
            table = jnp.where(lane == u, jnp.sum(load(u), axis=1, keepdims=True), table)
        return table

    return lax.fori_loop(0, CPD // 16, some, jnp.zeros((CELL, CELL), F32)).T[0:CPD]


def own_plane(ref, *at):
    return jnp.concatenate([ref[(g, *at)] for g in range(CPD // 8)], axis=0)


def build_left(vv, sel, eye, at):
    def some(g, _):
        for k in range(16):
            u = g * 16 + k
            picked = jnp.dot(sel[...], vv[u], preferred_element_type=F32).astype(BF)
            cols = lax.dot_general(eye[...], picked, NT, preferred_element_type=F32)
            at[u] = cols.astype(BF)
        return 0

    lax.fori_loop(0, CPD // 16, some, 0)


def sweep(total, place, fill, use, buffers):
    half = len(buffers) // 2
    sides = buffers[:half], buffers[half:]

    def some(i, _):
        for side in (0, 1):
            for s in range(half):
                p = (2 * i + side) * half + s
                fill(sides[1 - side][s], place(p + half))
                use(place(p), sides[side][s])
        return 0

    for s in range(half):
        fill(sides[0][s], place(s))
    lax.fori_loop(0, pl.cdiv(total, 2 * half), some, 0)


def build_cell_tables(view, vv):
    row = lax.broadcasted_iota(jnp.int32, (8, CELL), 0)

    def one_cell(g, k):
        x, y, z = (
            jnp.broadcast_to(view[g, c, pl.ds(k, 1), :], (8, CELL)) - 0.5 for c in range(3)
        )
        n = x * x + y * y + z * z
        w = jnp.where(row == 3, n, jnp.where(row == 4, 1.0, 0.0))
        w = jnp.where(row == 0, -2.0 * x, w)
        w = jnp.where(row == 1, -2.0 * y, w)
        w = jnp.where(row == 2, -2.0 * z, w)
        t1 = w.astype(BF).astype(F32)
        r1 = w - t1
        t2 = r1.astype(BF).astype(F32)
        t3 = r1 - t2
        return jnp.concatenate([t1, t2, t1, t3], axis=0).astype(BF)

    def two_groups(i, _):
        for k in range(16):
            g = i * 2 + k // 8
            vv[g * 8 + k % 8] = one_cell(g, k % 8)
        return 0

    lax.fori_loop(0, GROUPS // 2, two_groups, 0)


def right_operand(vv, shift, scale, v, d):
    cell = vv[v]
    moved = cell + shift[d]
    turned = cell * scale[d]
    return jnp.concatenate([moved[:16], moved[:16], moved[16:], turned], axis=0)


def dist2(at, vv, shift, scale, u, v, d):
    return jnp.dot(
        at[u], right_operand(vv, shift, scale, v, d), preferred_element_type=F32
    )


def root(r2):
    r2 = jnp.maximum(r2, TINY)
    return r2 * lax.rsqrt(r2)


def fold_rows(w):
    return jnp.sum(w.reshape(-1, 8, CELL), axis=0)


def scalars(pairs, wanted, count, p):
    p = jnp.minimum(p, PAIRS - 1) if not isinstance(p, int) else p
    u, v = pairs[0, 0, p], pairs[1, 0, p]
    d = jnp.where(p < count, pairs[2, 0, p], 27)
    slot = jnp.clip(v - CPD, 0, 255)
    q = slot >> 3
    offered = CPD + (q & 3) * 64 + (q >> 2) * 8 + wanted[slot & 7, q]
    v = jnp.where((v >= CPD) & (v < CPD + 256), offered, v)
    return u, v, d


def density_kernel(
    unroll, rows,
    pairs, wanted, count, view_in, sel, out,
    shift, scale, eye, vv, at, hb, hq, acc_l, acc_r, view, came, *buffers,
):
    coming = pltpu.make_async_copy(view_in, view, came.at[0])
    coming.start()
    build_constants(shift, scale, eye)

    def clear(g, _):
        acc_r[pl.ds(g * 8, 8)] = jnp.zeros((8, 8, CELL), F32)
        return 0

    lax.fori_loop(0, GROUPS, clear, 0)
    coming.wait()
    build_cell_tables(view, vv)

    build_left(vv, sel, eye, at)

    def put(u, c, column):
        if c == 0:
            hb[u] = column
        elif c == 1:
            hq[u] = column
        elif c == 2:
            acc_l[u] = jnp.zeros((CELL, CELL), F32)

    h = own_plane(view, 3)
    spread_columns([h, 1.25 * h, h, h], put)

    d2 = functools.partial(dist2, at, vv, shift, scale)
    chunks = range(CELL // rows)

    def fill(buffer, where):
        buffer[...] = d2(*where)

    def self_tile(where, r2):
        u = where[0]
        h_r = jnp.broadcast_to(view_row(view, 3, u), (rows, CELL))
        q_r = 1.25 * h_r
        total = jnp.zeros((8, CELL), F32)
        for c in chunks:
            r = root(r2[c * rows : c * rows + rows, :])
            f = jnp.maximum(h_r - r, 0.0)
            f2 = f * f
            total += fold_rows(f2 * f2 * (q_r - f))
        acc_r[u] = total

    def self_place(p):
        u = jnp.minimum(p, CPD - 1)
        return u, u, 13

    sweep(CPD, self_place, fill, self_tile, buffers[:CPD])

    n = count[0]
    place = functools.partial(scalars, pairs, wanted, n)

    def tile(where, r2):
        u, v, _ = where
        h_r = jnp.broadcast_to(view_row(view, 3, v), (rows, CELL))
        q_r = 1.25 * h_r
        total = acc_r[v]
        for c in chunks:
            at_rows = pl.ds(c * rows, rows)
            r = root(r2[c * rows : c * rows + rows, :])
            f = jnp.maximum(hb[u, at_rows, :] - r, 0.0)
            f2 = f * f
            acc_l[u, at_rows, :] += f2 * f2 * (hq[u, at_rows, :] - f)
            f = jnp.maximum(h_r - r, 0.0)
            f2 = f * f
            total += fold_rows(f2 * f2 * (q_r - f))
        acc_r[v] = total

    sweep(n, place, fill, tile, buffers)

    def finish(g, _):
        for h in range(2):
            at_rows = pl.ds((g * 2 + h) * 8, 8)
            out[at_rows, :] = jnp.sum(acc_r[at_rows], axis=1)
        return 0

    lax.fori_loop(0, GROUPS // 2, finish, 0)
    out[0:CPD, :] += row_sums(lambda u: acc_l[u])


def force_kernel(
    unroll, rows,
    pairs, wanted, count, active, view_in, coef_in, rho_in, sel, out, density,
    shift, scale, eye, vv, at, hb, cb, xb, acc_l, acc_r, view, coef, rho, came, *buffers,
):
    coming = [
        pltpu.make_async_copy(src, dst, came.at[i])
        for i, (src, dst) in enumerate(((view_in, view), (coef_in, coef), (rho_in, rho)))
    ]
    for copy in coming:
        copy.start()
    build_constants(shift, scale, eye)

    def clear(g, _):
        for c in range(4):
            acc_r[c, pl.ds(g * 8, 8)] = jnp.zeros((8, 8, CELL), F32)
        return 0

    lax.fori_loop(0, GROUPS, clear, 0)
    acc_l[...] = jnp.zeros(acc_l.shape, F32)
    for copy in coming:
        copy.wait()
    row = lax.broadcasted_iota(jnp.int32, (CPD, CELL), 0)
    live = jnp.zeros((CPD, CELL), jnp.int32)
    for u in range(CPD):
        live = jnp.where(row == u, active[u], live)
    lane = lax.broadcasted_iota(jnp.int32, (CPD, CELL), 1)
    density[...] = jnp.where(lane < live, rho[...], 0.0)
    build_cell_tables(view, vv)

    build_left(vv, sel, eye, at)

    def put(u, c, column):
        if c == 3:
            hb[u] = column
        else:
            xb[u, c] = column

    def put_coef(u, c, column):
        if c == 0:
            cb[u] = column

    spread_columns([own_plane(view, c) - (0.5 if c < 3 else 0.0) for c in range(4)], put)
    spread_columns([own_plane(coef)] * 4, put_coef)

    d2 = functools.partial(dist2, at, vv, shift, scale)
    chunks = range(CELL // rows)

    def tile(both, where, r2):
        u, v, d = where
        h_r = jnp.broadcast_to(view_row(view, 3, v), (rows, CELL))
        c_r = jnp.broadcast_to(coef[v // 8, pl.ds(lax.rem(v, 8), 1), :], (rows, CELL))
        total = [jnp.zeros((8, CELL), F32)] * 4
        tops, rests = [], []
        for k in chunks:
            at_rows = pl.ds(k * rows, rows)
            r = root(r2[k * rows : k * rows + rows, :])
            f = jnp.maximum(hb[u, at_rows, :] - r, 0.0)
            s = f * f * (f * cb[u, at_rows, :])
            f = jnp.maximum(h_r - r, 0.0)
            s += f * f * (f * c_r)
            for c in range(3):
                total[c] += fold_rows(s * xb[u, c, at_rows, :])
            total[3] += fold_rows(s)
            if both:
                top = s.astype(BF)
                tops.append(top)
                rests.append((s - top.astype(F32)).astype(BF))
        if both:
            right = vv[v, 0:16, :] + shift[d, 0:16, :]
            acc_l[u] += lax.dot_general(
                jnp.concatenate([right, right], axis=1),
                jnp.concatenate(
                    [jnp.concatenate(tops, axis=0), jnp.concatenate(rests, axis=0)], axis=1
                ),
                NT,
                preferred_element_type=F32,
            )
        offset = (d // 9 - 1, lax.rem(d // 3, 3) - 1, lax.rem(d, 3) - 1)
        for c in range(3):
            acc_r[c, v] += total[c] - offset[c].astype(F32) * total[3]
        acc_r[3, v] += total[3]

    def fill(buffer, where):
        buffer[...] = d2(*where)

    def self_place(p):
        u = jnp.minimum(p, CPD - 1)
        return u, u, jnp.int32(13)

    sweep(CPD, self_place, fill, functools.partial(tile, False), buffers[:CPD])

    n = count[0]
    place = functools.partial(scalars, pairs, wanted, n)

    sweep(n, place, fill, functools.partial(tile, True), buffers)

    def finish(g, _):
        whole = jnp.sum(acc_r[3, pl.ds(g * 8, 8)], axis=1)
        for c in range(3):
            out[g, c] = (view[g, c] - 0.5) * whole - jnp.sum(acc_r[c, pl.ds(g * 8, 8)], axis=1)
        return 0

    lax.fori_loop(0, GROUPS, finish, 0)
    for g in range(CPD // 8):
        rows_of = lambda r: jnp.concatenate(
            [acc_l[g * 8 + k, r : r + 1, :] for k in range(8)], axis=0
        )
        whole = rows_of(4)
        for c in range(3):
            moved = rows_of(c) + rows_of(8 + c) + rows_of(5 + c)
            out[g, c] += (view[g, c] - 0.5) * whole + 0.5 * moved


SMEM = pl.BlockSpec(memory_space=pltpu.SMEM)
VMEM = pl.BlockSpec(memory_space=pltpu.VMEM)
ANY = pl.BlockSpec(memory_space=pl.ANY)


def density_call(pairs, wanted, count, view, consts, unroll=2, rows=64):
    return pl.pallas_call(
        functools.partial(density_kernel, unroll, rows),
        out_shape=jax.ShapeDtypeStruct((NVIEW, CELL), F32),
        in_specs=[SMEM] * 3 + [ANY, VMEM],
        out_specs=VMEM,
        scratch_shapes=[
            pltpu.VMEM((28, 32, CELL), BF),
            pltpu.VMEM((28, 32, CELL), BF),
            pltpu.VMEM((CELL, CELL), BF),
            pltpu.VMEM((NVIEW, 32, CELL), BF),
            pltpu.VMEM((CPD, CELL, DEPTH), BF),
            pltpu.VMEM((CPD, CELL, CELL), F32),
            pltpu.VMEM((CPD, CELL, CELL), F32),
            pltpu.VMEM((CPD, CELL, CELL), F32),
            pltpu.VMEM((NVIEW, 8, CELL), F32),
            pltpu.VMEM((GROUPS, 4, 8, CELL), F32),
            pltpu.SemaphoreType.DMA((1,)),
        ]
        + [pltpu.VMEM((CELL, CELL), F32)] * unroll,
        compiler_params=pltpu.CompilerParams(vmem_limit_bytes=62 << 20),
        name="density_pairs",
    )(pairs, wanted, count, view, *consts)


def force_call(pairs, wanted, count, view, coef, rho, active, consts, unroll=2, rows=64):
    return pl.pallas_call(
        functools.partial(force_kernel, unroll, rows),
        out_shape=(
            jax.ShapeDtypeStruct((GROUPS, 3, 8, CELL), F32),
            jax.ShapeDtypeStruct((CPD, CELL), F32),
        ),
        in_specs=[SMEM] * 4 + [ANY] * 3 + [VMEM],
        out_specs=(VMEM, VMEM),
        scratch_shapes=[
            pltpu.VMEM((28, 32, CELL), BF),
            pltpu.VMEM((28, 32, CELL), BF),
            pltpu.VMEM((CELL, CELL), BF),
            pltpu.VMEM((NVIEW, 32, CELL), BF),
            pltpu.VMEM((CPD, CELL, DEPTH), BF),
            pltpu.VMEM((CPD, CELL, CELL), F32),
            pltpu.VMEM((CPD, CELL, CELL), F32),
            pltpu.VMEM((CPD, 3, CELL, CELL), F32),
            pltpu.VMEM((CPD, 16, CELL), F32),
            pltpu.VMEM((4, NVIEW, 8, CELL), F32),
            pltpu.VMEM((GROUPS, 4, 8, CELL), F32),
            pltpu.VMEM((GROUPS, 8, CELL), F32),
            pltpu.VMEM((CPD, CELL), F32),
            pltpu.SemaphoreType.DMA((3,)),
        ]
        + [pltpu.VMEM((CELL, CELL), F32)] * unroll,
        compiler_params=pltpu.CompilerParams(vmem_limit_bytes=62 << 20),
        name="force_pairs",
    )(pairs, wanted, count, active, view, coef, rho, *consts)


def spot():
    t = lax.axis_index("dom")
    return t // N_X, lax.rem(t, N_X), lax.axis_index("slab")


def group_of(z, x):
    return CPD // 8 + x * N_Z + z


def barrier(steps, meanwhile=lambda: None):
    z, x, s = spot()
    sem = pltpu.get_barrier_semaphore()
    peers = [{"dom": peer_at(z + i, x + j)} for i, j in steps]
    peers += [{"slab": (s + k) & (N_SLAB - 1)} for k in (1, N_SLAB - 1)]
    for peer in peers:
        pl.semaphore_signal(sem, inc=1, device_id=peer, device_id_type=MESH)
    meanwhile()
    pl.semaphore_wait(sem, len(peers))


def peer_at(z, x):
    return (z & (N_Z - 1)) * N_X + (x & (N_X - 1))


def far_first(steps):
    return sorted(steps, key=lambda at: -min(at[0], N_Z - at[0]) - min(at[1], N_X - at[1]))


ALL_STEPS = far_first((i, j) for i in range(N_Z) for j in range(N_X) if i or j)
AXIS_STEPS = far_first((i, j) for i, j in ALL_STEPS if i == 0 or j == 0)


def copy_to(src, dst, sems, k, peer):
    return pltpu.make_async_remote_copy(
        src_ref=src, dst_ref=dst, send_sem=sems[0].at[k], recv_sem=sems[1].at[k],
        device_id=peer, device_id_type=MESH,
    )


def z_copies(refs, sems):
    z, x, _ = spot()
    out = []
    for k in (4, 3, 5, 2, 6, 1, 7):
        to = (z + k) & (N_Z - 1)
        out.append((k, copy_to(*refs(to), sems, k, {"dom": to * N_X + x})))
    return dict(out)


def x_copies(refs, sems, base=0):
    z, x, _ = spot()
    out = []
    for k in (2, 1, 3):
        to = (x + k) & (N_X - 1)
        out.append(copy_to(*refs(to), sems, base + k, {"dom": z * N_X + to}))
    return out


def peer_copies(refs, sems):
    z, x, _ = spot()
    out = []
    for i, j in ALL_STEPS:
        group = group_of((z + i) & (N_Z - 1), (x + j) & (N_X - 1))
        out.append(
            copy_to(*refs(group), sems, i * N_X + j, {"dom": peer_at(z + i, x + j)})
        )
    return out


def face_copies(lower, upper, sems):
    s = lax.axis_index("slab")
    return [
        copy_to(*lower, sems, 0, {"slab": (s + N_SLAB - 1) & (N_SLAB - 1)}),
        copy_to(*upper, sems, 1, {"slab": (s + 1) & (N_SLAB - 1)}),
    ]


def start(copies):
    for copy in copies:
        copy.start()


def arrive(copies):
    for copy in copies:
        copy.wait_recv()


def leave(copies):
    for copy in copies:
        copy.wait_send()


def leave_local(copies):
    for copy in copies:
        copy.wait()


def pack(boundary, positions, smoothing, view, offered, here, local):
    leave_local(local)
    for g in range(CPD // 8):
        for c in range(3):
            view[g, c] = positions[c, g * 8 : g * 8 + 8, :]
        view[g, 3] = smoothing[g * 8 : g * 8 + 8, :]
    for b in range(8):
        cell = boundary[b]
        for c in range(3):
            offered[c, b : b + 1, :] = positions[c, pl.ds(cell, 1), :]
        offered[3, b : b + 1, :] = smoothing[pl.ds(cell, 1), :]
    view[here] = offered[...]


def gather_kernel(boundary, positions_in, smoothing_in, view, offered, positions, smoothing, near, *sems):
    z, x, _ = spot()
    local = [
        pltpu.make_async_copy(positions_in, positions, near.at[0]),
        pltpu.make_async_copy(smoothing_in, smoothing, near.at[1]),
    ]
    start(local)
    here = group_of(z, x)
    barrier(AXIS_STEPS, lambda: pack(boundary, positions, smoothing, view, offered, here, local))
    face_sems, z_sems, x_sems = sems[:2], sems[2:4], sems[4:6]
    along_z = z_copies(lambda to: (offered, view.at[here]), z_sems)
    faces = face_copies(
        (view.at[0], view.at[GROUPS - 1]), (view.at[CPD // 8 - 1], view.at[GROUPS - 2]), face_sems
    )
    start(along_z.values())
    along_x = x_copies(lambda to: (offered, view.at[here]), x_sems)
    start(along_x)
    start(faces)
    for k in (1, 7, 2, 6, 3, 5, 4):
        along_z[k].wait_recv()
        block = view.at[group_of((z - k) & (N_Z - 1), x)]
        onward = x_copies(lambda to: (block, block), x_sems, k * N_X)
        start(onward)
        along_x += onward
    arrive(along_x + faces)
    leave(list(along_z.values()) + along_x + faces)


def settle(own, arrived, lower, upper, boundary):
    row = lax.broadcasted_iota(jnp.int32, (CPD, CELL), 0)
    for b in range(8):
        own += jnp.where(row == boundary[b], jnp.broadcast_to(arrived[b : b + 1], own.shape), 0.0)
    return jnp.concatenate([own[:8] + lower, own[8:24], own[24:] + upper], axis=0)


def sum_back(partial, arrived, faces, face_sems, sems, near):
    z, x, _ = spot()
    here = group_of(z, x)
    copies = peer_copies(lambda group: (partial.at[group], arrived.at[here - CPD // 8]), sems)
    copies += face_copies(
        (partial.at[GROUPS - 2], faces.at[1]), (partial.at[GROUPS - 1], faces.at[0]), face_sems
    )
    start(copies)
    mine = pltpu.make_async_copy(partial.at[here], arrived.at[here - CPD // 8], near)
    mine.start()
    mine.wait()
    arrive(copies)
    total = arrived[0]
    for k in range(1, N_Z * N_X):
        total += arrived[k]
    return total, copies


def factor_kernel(
    boundary, partial, smoothing_in, energy_in, rho, coef,
    arrived, faces, offered, mine, own, smoothing, energy, near, *sems,
):
    z, x, _ = spot()
    local = [
        pltpu.make_async_copy(src, dst, near.at[i])
        for i, (src, dst) in enumerate(
            ((partial.at[pl.ds(0, CPD // 8)], own), (smoothing_in, smoothing), (energy_in, energy))
        )
    ]
    start(local)
    barrier(ALL_STEPS)
    total, copies = sum_back(partial, arrived, faces, sems[0:2], sems[2:4], near.at[3])
    leave_local(local)
    h2 = smoothing[...] * smoothing[...]
    h4 = h2 * h2
    inverse = 1.0 / (h4 * h4)
    raw = settle(own[...].reshape(CPD, CELL), total, faces[0], faces[1], boundary)
    density = (4.0 * NORM / CELL) * inverse * raw
    rho[...] = density
    slope = (40.0 / 3.0 * NORM / CELL) * inverse * energy[...] / density
    for g in range(CPD // 8):
        coef[g] = slope[g * 8 : g * 8 + 8]
    mine[...] = slope
    for b in range(8):
        offered[b : b + 1, :] = mine[pl.ds(boundary[b], 1), :]
    here = group_of(z, x)
    coef[here] = offered[...]
    back = peer_copies(lambda group: (offered, coef.at[here]), sems[6:8])
    back += face_copies(
        (coef.at[0], coef.at[GROUPS - 1]), (coef.at[CPD // 8 - 1], coef.at[GROUPS - 2]), sems[4:6]
    )
    start(back)
    leave(copies)
    arrive(back)
    leave(back)


def settle_kernel(boundary, partial, accel, arrived, faces, own, near, *sems):
    local = [pltpu.make_async_copy(partial.at[pl.ds(0, CPD // 8)], own, near.at[0])]
    start(local)
    barrier(ALL_STEPS)
    total, copies = sum_back(partial, arrived, faces, sems[0:2], sems[2:4], near.at[1])
    leave_local(local)
    for c in range(3):
        kept = jnp.concatenate([own[g, c] for g in range(CPD // 8)], axis=0)
        accel[c] = settle(kept, total[c], faces[0, c], faces[1, c], boundary)
    leave(copies)


def comm_call(kernel, collective, out_shape, scratch, n_near, n_sems, operands):
    return pl.pallas_call(
        kernel,
        out_shape=out_shape,
        in_specs=[SMEM] + [ANY] * (len(operands) - 1),
        out_specs=jax.tree.map(lambda _: VMEM, out_shape),
        scratch_shapes=[pltpu.VMEM(dims, F32) for dims in scratch]
        + [pltpu.SemaphoreType.DMA((n_near,))]
        + [pltpu.SemaphoreType.DMA((n,)) for n in n_sems for _ in (0, 1)],
        compiler_params=pltpu.CompilerParams(collective_id=collective, has_side_effects=True),
        name=kernel.__name__,
    )(*operands)


def per_device(positions, smoothing, energy, active, boundary, wanted, cell_pairs, pair_count):
    consts = tables()
    offers = boundary[0]
    pairs = cell_pairs.transpose(2, 0, 1)
    taken = wanted[0].T
    shape = lambda *dims: jax.ShapeDtypeStruct(dims, F32)
    rows = (8, CELL)
    view = comm_call(
        gather_kernel, 0, shape(GROUPS, 4, *rows), [(4, *rows), (3, CPD, CELL), (CPD, CELL)], 2,
        (2, N_Z, N_Z * N_X),
        (offers, positions.transpose(1, 0, 2), smoothing),
    )
    partial = density_call(pairs, taken, pair_count, view, consts, 32, 128)
    rho, coef = comm_call(
        factor_kernel, 1, (shape(CPD, CELL), shape(GROUPS, *rows)),
        [(N_Z * N_X, *rows), (2, *rows), rows, (CPD, CELL), (CPD // 8, *rows), (CPD, CELL), (CPD, CELL)],
        4, (2, N_Z * N_X, 2, N_Z * N_X),
        (offers, partial.reshape(GROUPS, *rows), smoothing, energy),
    )
    force, density = force_call(pairs, taken, pair_count, view, coef, rho, active, consts, 32, 128)
    accel = comm_call(
        settle_kernel, 2, shape(3, CPD, CELL),
        [(N_Z * N_X, 3, *rows), (2, 3, *rows), (CPD // 8, 3, *rows)],
        2, (2, N_Z * N_X),
        (offers, force),
    )
    live = jnp.arange(CELL, dtype=jnp.int32)[None, :] < active[:, None]
    return density, jnp.where(live[:, None, :], accel.transpose(1, 0, 2), 0.0)


def solution(mesh):
    in_specs = (
        P(("slab", "dom"), None, None),
        P(("slab", "dom"), None),
        P(("slab", "dom"), None),
        P(("slab", "dom")),
        P(("slab", "dom"), None),
        P(("slab", "dom"), None, None),
        P(("slab", "dom"), None, None),
        P(("slab", "dom")),
    )
    out_specs = (P(("slab", "dom"), None), P(("slab", "dom"), None, None))
    return jax.shard_map(
        per_device, mesh=mesh, in_specs=in_specs, out_specs=out_specs, check_vma=False
    )
```

```python
import functools
import jax
import jax.numpy as jnp
import numpy as np
from jax import lax
from jax.experimental import pallas as pl
from jax.experimental.pallas import tpu as pltpu
from jax.sharding import PartitionSpec as P

CELL, CPD, NVIEW, GROUPS, PAIRS = 128, 32, 304, 38, 448
NORM = 21.0 / (2.0 * 3.141592653589793)
BF = jnp.bfloat16
F32 = jnp.float32
TINY = 1e-30
N_Z, N_X, N_SLAB = 8, 4, 8
MESH = pl.DeviceIdType.MESH
DEPTH = 80
NT = (((1,), (1,)), ((), ()))


def tables():
    sel = np.zeros((DEPTH, 32), np.float32)
    first, second, third, one = 0, 8, 24, 4
    for c in range(3):
        for part, base in ((first, 0), (second, 16), (third, 32)):
            sel[base + c, part + c] = -0.5
            sel[base + 5 + c, part + c] = -0.5
        sel[8 + c, first + c] = -0.5
        sel[24 + c, second + c] = -0.5
        sel[40 + c, first + c] = -0.5
        for base in (48, 56, 72):
            sel[base + c, one] = 1.0
    sel[3, one] = sel[11, one] = sel[12, one] = sel[43, one] = 1.0
    sel[4, first + 3] = sel[20, second + 3] = sel[36, third + 3] = 1.0
    return (jnp.asarray(sel, BF),)


def build_constants(shift, scale):
    row = lax.broadcasted_iota(jnp.int32, (8, CELL), 0)
    none = jnp.zeros((8, CELL), F32)
    for d in range(28):
        offset = (d // 9 - 1, d // 3 % 3 - 1, d % 3 - 1) if d < 27 else (0, 0, 0)
        length = sum(o * o for o in offset) if d < 27 else 16384
        moved, turned = none, none
        for c, o in enumerate(offset):
            if o:
                moved = jnp.where(row == 5 + c, -2.0 * o, moved)
                turned = jnp.where(row == c, -1.0 * o, turned)
        far = jnp.where(row == 4, 1.0 * length, none)
        shift[d] = jnp.concatenate([moved, far, moved, none], axis=0).astype(BF)
        scale[d] = jnp.concatenate([turned, turned, none, turned], axis=0).astype(BF)


def build_eye(eye):
    down = lax.broadcasted_iota(jnp.int32, (CELL, CELL), 0)
    across = lax.broadcasted_iota(jnp.int32, (CELL, CELL), 1)
    eye[...] = jnp.where(down == across, 1.0, 0.0).astype(BF)


def view_row(view, c, v):
    return view[v // 8, c, pl.ds(lax.rem(v, 8), 1), :]


def spread_columns(planes, put):
    turned = jnp.concatenate(planes, axis=0).T

    def some(g, turned):
        for k in range(8):
            for c in range(4):
                column = turned[:, c * CPD + k : c * CPD + k + 1]
                put(g * 8 + k, c, jnp.broadcast_to(column, (CELL, CELL)))
        return pltpu.roll(turned, CELL - 8, 1)

    lax.fori_loop(0, CPD // 8, some, turned)


def row_sums(load):
    lane = lax.broadcasted_iota(jnp.int32, (CELL, CELL), 1)

    def some(g, table):
        for k in range(16):
            u = g * 16 + k
            table = jnp.where(lane == u, jnp.sum(load(u), axis=1, keepdims=True), table)
        return table

    return lax.fori_loop(0, CPD // 16, some, jnp.zeros((CELL, CELL), F32)).T[0:CPD]


def own_plane(ref, *at):
    return jnp.concatenate([ref[(g, *at)] for g in range(CPD // 8)], axis=0)


def build_left(vv, sel, eye, at):
    def some(g, _):
        for k in range(16):
            u = g * 16 + k
            picked = jnp.dot(sel[...], vv[u], preferred_element_type=F32).astype(BF)
            cols = lax.dot_general(eye[...], picked, NT, preferred_element_type=F32)
            at[u] = cols.astype(BF)
        return 0

    lax.fori_loop(0, CPD // 16, some, 0)


def sweep(total, place, fill, use, buffers):
    half = len(buffers) // 2
    sides = buffers[:half], buffers[half:]

    def some(i, _):
        for side in (0, 1):
            for s in range(half):
                p = (2 * i + side) * half + s
                fill(sides[1 - side][s], place(p + half))
                use(place(p), sides[side][s])
        return 0

    for s in range(half):
        fill(sides[0][s], place(s))
    lax.fori_loop(0, pl.cdiv(total, 2 * half), some, 0)


def build_cell_tables(view, vv, groups=GROUPS):
    row = lax.broadcasted_iota(jnp.int32, (8, CELL), 0)

    def one_cell(g, k):
        x, y, z = (
            jnp.broadcast_to(view[g, c, pl.ds(k, 1), :], (8, CELL)) - 0.5 for c in range(3)
        )
        n = x * x + y * y + z * z
        w = jnp.where(row == 3, n, jnp.where(row == 4, 1.0, 0.0))
        w = jnp.where(row == 0, -2.0 * x, w)
        w = jnp.where(row == 1, -2.0 * y, w)
        w = jnp.where(row == 2, -2.0 * z, w)
        t1 = w.astype(BF).astype(F32)
        r1 = w - t1
        t2 = r1.astype(BF).astype(F32)
        t3 = r1 - t2
        return jnp.concatenate([t1, t2, t1, t3], axis=0).astype(BF)

    def two_groups(i, _):
        for k in range(16):
            g = i * 2 + k // 8
            vv[g * 8 + k % 8] = one_cell(g, k % 8)
        return 0

    lax.fori_loop(0, groups // 2, two_groups, 0)


def right_operand(vv, shift, scale, v, d):
    cell = vv[v]
    moved = cell + shift[d]
    turned = cell * scale[d]
    return jnp.concatenate([moved[:16], moved[:16], moved[16:], turned], axis=0)


def dist2(at, vv, shift, scale, u, v, d):
    return jnp.dot(
        at[u], right_operand(vv, shift, scale, v, d), preferred_element_type=F32
    )


def root(r2):
    r2 = jnp.maximum(r2, TINY)
    return r2 * lax.rsqrt(r2)


def fold_rows(w):
    return jnp.sum(w.reshape(-1, 8, CELL), axis=0)


def scalars(pairs, wanted, count, p):
    p = jnp.minimum(p, PAIRS - 1) if not isinstance(p, int) else p
    u, v = pairs[0, 0, p], pairs[1, 0, p]
    d = jnp.where(p < count, pairs[2, 0, p], 27)
    slot = jnp.clip(v - CPD, 0, 255)
    q = slot >> 3
    offered = CPD + (q & 3) * 64 + (q >> 2) * 8 + wanted[slot & 7, q]
    v = jnp.where((v >= CPD) & (v < CPD + 256), offered, v)
    return u, v, d


def self_densities(view, vv, at, sums):
    def some(g, _):
        for k in range(8):
            u = g * 8 + k
            cell = vv[u]
            right = jnp.concatenate([cell[:16], cell[:16], cell[16:]], axis=0)
            r = root(jnp.dot(at[u, :, 0:48], right, preferred_element_type=F32))
            h = jnp.broadcast_to(view[g, 3, k : k + 1, :], (CELL, CELL))
            f = jnp.maximum(h - r, 0.0)
            f2 = f * f
            sums[u] = fold_rows(f2 * f2 * (1.25 * h - f))
        return 0

    lax.fori_loop(0, CPD // 8, some, 0)


def density_kernel(
    unroll, rows,
    pairs, wanted, count, view_in, at_in, self_in, out,
    shift, scale, vv, at, hb, hq, acc_l, acc_r, view, came, *buffers,
):
    coming = pltpu.make_async_copy(view_in, view, came.at[0])
    coming.start()
    handed = [
        pltpu.make_async_copy(at_in, at, came.at[1]),
        pltpu.make_async_copy(self_in, acc_r.at[pl.ds(0, CPD)], came.at[2]),
    ]
    for copy in handed:
        copy.start()
    build_constants(shift, scale)

    def clear(g, _):
        acc_r[pl.ds(g * 8, 8)] = jnp.zeros((8, 8, CELL), F32)
        return 0

    lax.fori_loop(CPD // 8, GROUPS, clear, 0)
    coming.wait()
    build_cell_tables(view, vv)


    def put(u, c, column):
        if c == 0:
            hb[u] = column
        elif c == 1:
            hq[u] = column
        elif c == 2:
            acc_l[u] = jnp.zeros((CELL, CELL), F32)

    h = own_plane(view, 3)
    spread_columns([h, 1.25 * h, h, h], put)

    d2 = functools.partial(dist2, at, vv, shift, scale)
    chunks = range(CELL // rows)

    def fill(buffer, where):
        buffer[...] = d2(*where)

    for copy in handed:
        copy.wait()
    n = count[0]
    place = functools.partial(scalars, pairs, wanted, n)

    def tile(where, r2):
        u, v, _ = where
        h_r = jnp.broadcast_to(view_row(view, 3, v), (rows, CELL))
        q_r = 1.25 * h_r
        total = acc_r[v]
        for c in chunks:
            at_rows = pl.ds(c * rows, rows)
            r = root(r2[c * rows : c * rows + rows, :])
            f = jnp.maximum(hb[u, at_rows, :] - r, 0.0)
            f2 = f * f
            acc_l[u, at_rows, :] += f2 * f2 * (hq[u, at_rows, :] - f)
            f = jnp.maximum(h_r - r, 0.0)
            f2 = f * f
            total += fold_rows(f2 * f2 * (q_r - f))
        acc_r[v] = total

    sweep(n, place, fill, tile, buffers)

    def finish(g, _):
        for h in range(2):
            at_rows = pl.ds((g * 2 + h) * 8, 8)
            out[at_rows, :] = jnp.sum(acc_r[at_rows], axis=1)
        return 0

    lax.fori_loop(0, GROUPS // 2, finish, 0)
    out[0:CPD, :] += row_sums(lambda u: acc_l[u])


def force_kernel(
    unroll, rows,
    pairs, wanted, count, active, view_in, coef_in, rho_in, at_in, out, density,
    shift, scale, vv, at, hb, cb, xb, acc_l, acc_r, view, coef, rho, came, *buffers,
):
    coming = [
        pltpu.make_async_copy(src, dst, came.at[i])
        for i, (src, dst) in enumerate(((view_in, view), (coef_in, coef), (rho_in, rho)))
    ]
    handed = pltpu.make_async_copy(at_in, at, came.at[3])
    handed.start()
    for copy in coming:
        copy.start()
    build_constants(shift, scale)

    def clear(g, _):
        for c in range(4):
            acc_r[c, pl.ds(g * 8, 8)] = jnp.zeros((8, 8, CELL), F32)
        return 0

    lax.fori_loop(0, GROUPS, clear, 0)
    acc_l[...] = jnp.zeros(acc_l.shape, F32)
    for copy in coming:
        copy.wait()
    row = lax.broadcasted_iota(jnp.int32, (CPD, CELL), 0)
    live = jnp.zeros((CPD, CELL), jnp.int32)
    for u in range(CPD):
        live = jnp.where(row == u, active[u], live)
    lane = lax.broadcasted_iota(jnp.int32, (CPD, CELL), 1)
    density[...] = jnp.where(lane < live, rho[...], 0.0)
    build_cell_tables(view, vv)


    def put(u, c, column):
        if c == 3:
            hb[u] = column
        else:
            xb[u, c] = column

    def put_coef(u, c, column):
        if c == 0:
            cb[u] = column

    spread_columns([own_plane(view, c) - (0.5 if c < 3 else 0.0) for c in range(4)], put)
    spread_columns([own_plane(coef)] * 4, put_coef)

    handed.wait()
    d2 = functools.partial(dist2, at, vv, shift, scale)
    chunks = range(CELL // rows)

    def tile(both, where, r2):
        u, v, d = where
        h_r = jnp.broadcast_to(view_row(view, 3, v), (rows, CELL))
        c_r = jnp.broadcast_to(coef[v // 8, pl.ds(lax.rem(v, 8), 1), :], (rows, CELL))
        total = [jnp.zeros((8, CELL), F32)] * 4
        tops, rests = [], []
        for k in chunks:
            at_rows = pl.ds(k * rows, rows)
            r = root(r2[k * rows : k * rows + rows, :])
            f = jnp.maximum(hb[u, at_rows, :] - r, 0.0)
            s = f * f * (f * cb[u, at_rows, :])
            f = jnp.maximum(h_r - r, 0.0)
            s += f * f * (f * c_r)
            for c in range(3):
                total[c] += fold_rows(s * xb[u, c, at_rows, :])
            total[3] += fold_rows(s)
            if both:
                top = s.astype(BF)
                tops.append(top)
                rests.append((s - top.astype(F32)).astype(BF))
        if both:
            right = vv[v, 0:16, :] + shift[d, 0:16, :]
            acc_l[u] += lax.dot_general(
                jnp.concatenate([right, right], axis=1),
                jnp.concatenate(
                    [jnp.concatenate(tops, axis=0), jnp.concatenate(rests, axis=0)], axis=1
                ),
                NT,
                preferred_element_type=F32,
            )
        offset = (d // 9 - 1, lax.rem(d // 3, 3) - 1, lax.rem(d, 3) - 1)
        for c in range(3):
            acc_r[c, v] += total[c] - offset[c].astype(F32) * total[3]
        acc_r[3, v] += total[3]

    def fill(buffer, where):
        buffer[...] = d2(*where)

    def self_place(p):
        u = jnp.minimum(p, CPD - 1)
        return u, u, jnp.int32(13)

    sweep(CPD, self_place, fill, functools.partial(tile, False), buffers[:CPD])

    n = count[0]
    place = functools.partial(scalars, pairs, wanted, n)

    sweep(n, place, fill, functools.partial(tile, True), buffers)

    def finish(g, _):
        whole = jnp.sum(acc_r[3, pl.ds(g * 8, 8)], axis=1)
        for c in range(3):
            out[g, c] = (view[g, c] - 0.5) * whole - jnp.sum(acc_r[c, pl.ds(g * 8, 8)], axis=1)
        return 0

    lax.fori_loop(0, GROUPS, finish, 0)
    for g in range(CPD // 8):
        rows_of = lambda r: jnp.concatenate(
            [acc_l[g * 8 + k, r : r + 1, :] for k in range(8)], axis=0
        )
        whole = rows_of(4)
        for c in range(3):
            moved = rows_of(c) + rows_of(8 + c) + rows_of(5 + c)
            out[g, c] += (view[g, c] - 0.5) * whole + 0.5 * moved


SMEM = pl.BlockSpec(memory_space=pltpu.SMEM)
VMEM = pl.BlockSpec(memory_space=pltpu.VMEM)
ANY = pl.BlockSpec(memory_space=pl.ANY)


def density_call(pairs, wanted, count, view, own, unroll=2, rows=64):
    return pl.pallas_call(
        functools.partial(density_kernel, unroll, rows),
        out_shape=jax.ShapeDtypeStruct((NVIEW, CELL), F32),
        in_specs=[SMEM] * 3 + [ANY] * 3,
        out_specs=VMEM,
        scratch_shapes=[
            pltpu.VMEM((28, 32, CELL), BF),
            pltpu.VMEM((28, 32, CELL), BF),
            pltpu.VMEM((NVIEW, 32, CELL), BF),
            pltpu.VMEM((CPD, CELL, DEPTH), BF),
            pltpu.VMEM((CPD, CELL, CELL), F32),
            pltpu.VMEM((CPD, CELL, CELL), F32),
            pltpu.VMEM((CPD, CELL, CELL), F32),
            pltpu.VMEM((NVIEW, 8, CELL), F32),
            pltpu.VMEM((GROUPS, 4, 8, CELL), F32),
            pltpu.SemaphoreType.DMA((3,)),
        ]
        + [pltpu.VMEM((CELL, CELL), F32)] * unroll,
        compiler_params=pltpu.CompilerParams(vmem_limit_bytes=62 << 20),
        name="density_pairs",
    )(pairs, wanted, count, view, *own)


def force_call(pairs, wanted, count, view, coef, rho, active, own, unroll=2, rows=64):
    return pl.pallas_call(
        functools.partial(force_kernel, unroll, rows),
        out_shape=(
            jax.ShapeDtypeStruct((GROUPS, 3, 8, CELL), F32),
            jax.ShapeDtypeStruct((CPD, CELL), F32),
        ),
        in_specs=[SMEM] * 4 + [ANY] * 4,
        out_specs=(VMEM, VMEM),
        scratch_shapes=[
            pltpu.VMEM((28, 32, CELL), BF),
            pltpu.VMEM((28, 32, CELL), BF),
            pltpu.VMEM((NVIEW, 32, CELL), BF),
            pltpu.VMEM((CPD, CELL, DEPTH), BF),
            pltpu.VMEM((CPD, CELL, CELL), F32),
            pltpu.VMEM((CPD, CELL, CELL), F32),
            pltpu.VMEM((CPD, 3, CELL, CELL), F32),
            pltpu.VMEM((CPD, 16, CELL), F32),
            pltpu.VMEM((4, NVIEW, 8, CELL), F32),
            pltpu.VMEM((GROUPS, 4, 8, CELL), F32),
            pltpu.VMEM((GROUPS, 8, CELL), F32),
            pltpu.VMEM((CPD, CELL), F32),
            pltpu.SemaphoreType.DMA((4,)),
        ]
        + [pltpu.VMEM((CELL, CELL), F32)] * unroll,
        compiler_params=pltpu.CompilerParams(vmem_limit_bytes=62 << 20),
        name="force_pairs",
    )(pairs, wanted, count, active, view, coef, rho, own[0])


def spot():
    t = lax.axis_index("dom")
    return t // N_X, lax.rem(t, N_X), lax.axis_index("slab")


def group_of(z, x):
    return CPD // 8 + x * N_Z + z


def barrier(steps, meanwhile=lambda: None):
    z, x, s = spot()
    sem = pltpu.get_barrier_semaphore()
    peers = [{"dom": peer_at(z + i, x + j)} for i, j in steps]
    peers += [{"slab": (s + k) & (N_SLAB - 1)} for k in (1, N_SLAB - 1)]
    for peer in peers:
        pl.semaphore_signal(sem, inc=1, device_id=peer, device_id_type=MESH)
    meanwhile()
    pl.semaphore_wait(sem, len(peers))


def peer_at(z, x):
    return (z & (N_Z - 1)) * N_X + (x & (N_X - 1))


def far_first(steps):
    return sorted(steps, key=lambda at: -min(at[0], N_Z - at[0]) - min(at[1], N_X - at[1]))


ALL_STEPS = far_first((i, j) for i in range(N_Z) for j in range(N_X) if i or j)
AXIS_STEPS = far_first((i, j) for i, j in ALL_STEPS if i == 0 or j == 0)


def copy_to(src, dst, sems, k, peer):
    return pltpu.make_async_remote_copy(
        src_ref=src, dst_ref=dst, send_sem=sems[0].at[k], recv_sem=sems[1].at[k],
        device_id=peer, device_id_type=MESH,
    )


def z_copies(refs, sems):
    z, x, _ = spot()
    out = []
    for k in (4, 3, 5, 2, 6, 1, 7):
        to = (z + k) & (N_Z - 1)
        out.append((k, copy_to(*refs(to), sems, k, {"dom": to * N_X + x})))
    return dict(out)


def x_copies(refs, sems, base=0):
    z, x, _ = spot()
    out = []
    for k in (2, 1, 3):
        to = (x + k) & (N_X - 1)
        out.append(copy_to(*refs(to), sems, base + k, {"dom": z * N_X + to}))
    return out


def peer_copies(refs, sems):
    z, x, _ = spot()
    out = []
    for i, j in ALL_STEPS:
        group = group_of((z + i) & (N_Z - 1), (x + j) & (N_X - 1))
        out.append(
            copy_to(*refs(group), sems, i * N_X + j, {"dom": peer_at(z + i, x + j)})
        )
    return out


def face_copies(lower, upper, sems):
    s = lax.axis_index("slab")
    return [
        copy_to(*lower, sems, 0, {"slab": (s + N_SLAB - 1) & (N_SLAB - 1)}),
        copy_to(*upper, sems, 1, {"slab": (s + 1) & (N_SLAB - 1)}),
    ]


def start(copies):
    for copy in copies:
        copy.start()


def arrive(copies):
    for copy in copies:
        copy.wait_recv()


def leave(copies):
    for copy in copies:
        copy.wait_send()


def leave_local(copies):
    for copy in copies:
        copy.wait()


def pack(boundary, positions, smoothing, view, mine, offered, here, local):
    leave_local(local)
    for g in range(CPD // 8):
        for c in range(3):
            view[g, c] = positions[c, g * 8 : g * 8 + 8, :]
            mine[g, c] = positions[c, g * 8 : g * 8 + 8, :]
        view[g, 3] = smoothing[g * 8 : g * 8 + 8, :]
        mine[g, 3] = smoothing[g * 8 : g * 8 + 8, :]
    for b in range(8):
        cell = boundary[b]
        for c in range(3):
            offered[c, b : b + 1, :] = positions[c, pl.ds(cell, 1), :]
        offered[3, b : b + 1, :] = smoothing[pl.ds(cell, 1), :]
    view[here] = offered[...]


def gather_kernel(
    boundary, positions_in, smoothing_in, sel, view, at_out, self_out,
    offered, positions, smoothing, mine, sums, vv, at, eye, near, *sems,
):
    z, x, _ = spot()
    local = [
        pltpu.make_async_copy(positions_in, positions, near.at[0]),
        pltpu.make_async_copy(smoothing_in, smoothing, near.at[1]),
    ]
    start(local)
    here = group_of(z, x)
    barrier(AXIS_STEPS, lambda: pack(boundary, positions, smoothing, view, mine, offered, here, local))
    face_sems, z_sems, x_sems = sems[:2], sems[2:4], sems[4:6]
    along_z = z_copies(lambda to: (offered, view.at[here]), z_sems)
    faces = face_copies(
        (view.at[0], view.at[GROUPS - 1]), (view.at[CPD // 8 - 1], view.at[GROUPS - 2]), face_sems
    )
    start(along_z.values())
    along_x = x_copies(lambda to: (offered, view.at[here]), x_sems)
    start(along_x)
    start(faces)
    for k in (1, 7, 2, 6, 3, 5, 4):
        along_z[k].wait_recv()
        block = view.at[group_of((z - k) & (N_Z - 1), x)]
        onward = x_copies(lambda to: (block, block), x_sems, k * N_X)
        start(onward)
        along_x += onward
    build_eye(eye)
    build_cell_tables(mine, vv, CPD // 8)
    build_left(vv, sel, eye, at)
    self_densities(mine, vv, at, sums)
    handed = [
        pltpu.make_async_copy(at, at_out, near.at[2]),
        pltpu.make_async_copy(sums, self_out, near.at[3]),
    ]
    start(handed)
    arrive(along_x + faces)
    leave(list(along_z.values()) + along_x + faces)
    leave_local(handed)


def settle(own, arrived, lower, upper, boundary):
    row = lax.broadcasted_iota(jnp.int32, (CPD, CELL), 0)
    for b in range(8):
        own += jnp.where(row == boundary[b], jnp.broadcast_to(arrived[b : b + 1], own.shape), 0.0)
    return jnp.concatenate([own[:8] + lower, own[8:24], own[24:] + upper], axis=0)


def sum_back(partial, arrived, faces, face_sems, sems, near):
    z, x, _ = spot()
    here = group_of(z, x)
    copies = peer_copies(lambda group: (partial.at[group], arrived.at[here - CPD // 8]), sems)
    copies += face_copies(
        (partial.at[GROUPS - 2], faces.at[1]), (partial.at[GROUPS - 1], faces.at[0]), face_sems
    )
    start(copies)
    mine = pltpu.make_async_copy(partial.at[here], arrived.at[here - CPD // 8], near)
    mine.start()
    mine.wait()
    arrive(copies)
    total = arrived[0]
    for k in range(1, N_Z * N_X):
        total += arrived[k]
    return total, copies


def factor_kernel(
    boundary, partial, smoothing_in, energy_in, rho, coef,
    arrived, faces, offered, mine, own, smoothing, energy, near, *sems,
):
    z, x, _ = spot()
    local = [
        pltpu.make_async_copy(src, dst, near.at[i])
        for i, (src, dst) in enumerate(
            ((partial.at[pl.ds(0, CPD // 8)], own), (smoothing_in, smoothing), (energy_in, energy))
        )
    ]
    start(local)
    barrier(ALL_STEPS)
    total, copies = sum_back(partial, arrived, faces, sems[0:2], sems[2:4], near.at[3])
    leave_local(local)
    h2 = smoothing[...] * smoothing[...]
    h4 = h2 * h2
    inverse = 1.0 / (h4 * h4)
    raw = settle(own[...].reshape(CPD, CELL), total, faces[0], faces[1], boundary)
    density = (4.0 * NORM / CELL) * inverse * raw
    rho[...] = density
    slope = (40.0 / 3.0 * NORM / CELL) * inverse * energy[...] / density
    for g in range(CPD // 8):
        coef[g] = slope[g * 8 : g * 8 + 8]
    mine[...] = slope
    for b in range(8):
        offered[b : b + 1, :] = mine[pl.ds(boundary[b], 1), :]
    here = group_of(z, x)
    coef[here] = offered[...]
    back = peer_copies(lambda group: (offered, coef.at[here]), sems[6:8])
    back += face_copies(
        (coef.at[0], coef.at[GROUPS - 1]), (coef.at[CPD // 8 - 1], coef.at[GROUPS - 2]), sems[4:6]
    )
    start(back)
    leave(copies)
    arrive(back)
    leave(back)


def settle_kernel(boundary, partial, accel, arrived, faces, own, near, *sems):
    local = [pltpu.make_async_copy(partial.at[pl.ds(0, CPD // 8)], own, near.at[0])]
    start(local)
    barrier(ALL_STEPS)
    total, copies = sum_back(partial, arrived, faces, sems[0:2], sems[2:4], near.at[1])
    leave_local(local)
    for c in range(3):
        kept = jnp.concatenate([own[g, c] for g in range(CPD // 8)], axis=0)
        accel[c] = settle(kept, total[c], faces[0, c], faces[1, c], boundary)
    leave(copies)


LEFT_SCRATCH = ((CPD, 32, CELL), (CPD, CELL, DEPTH), (CELL, CELL))


def comm_call(kernel, collective, out_shape, scratch, n_near, n_sems, operands, more=None):
    return pl.pallas_call(
        kernel,
        out_shape=out_shape,
        in_specs=[SMEM] + [ANY] * (len(operands) - 1) + [VMEM] * len(more or ()),
        out_specs=(VMEM, ANY, ANY) if more else jax.tree.map(lambda _: VMEM, out_shape),
        scratch_shapes=[pltpu.VMEM(dims, F32) for dims in scratch]
        + [pltpu.VMEM(dims, BF) for dims in (LEFT_SCRATCH if more else ())]
        + [pltpu.SemaphoreType.DMA((n_near,))]
        + [pltpu.SemaphoreType.DMA((n,)) for n in n_sems for _ in (0, 1)],
        compiler_params=pltpu.CompilerParams(collective_id=collective, has_side_effects=True),
        name=kernel.__name__,
    )(*operands, *(more or ()))


def per_device(positions, smoothing, energy, active, boundary, wanted, cell_pairs, pair_count):
    offers = boundary[0]
    pairs = cell_pairs.transpose(2, 0, 1)
    taken = wanted[0].T
    shape = lambda *dims: jax.ShapeDtypeStruct(dims, F32)
    rows = (8, CELL)
    view, *own = comm_call(
        gather_kernel, 0,
        (
            shape(GROUPS, 4, *rows),
            jax.ShapeDtypeStruct((CPD, CELL, DEPTH), BF),
            shape(CPD, *rows),
        ),
        [(4, *rows), (3, CPD, CELL), (CPD, CELL), (CPD // 8, 4, *rows), (CPD, *rows)], 4,
        (2, N_Z, N_Z * N_X),
        (offers, positions.transpose(1, 0, 2), smoothing),
        tables(),
    )
    partial = density_call(pairs, taken, pair_count, view, own, 32, 128)
    rho, coef = comm_call(
        factor_kernel, 1, (shape(CPD, CELL), shape(GROUPS, *rows)),
        [(N_Z * N_X, *rows), (2, *rows), rows, (CPD, CELL), (CPD // 8, *rows), (CPD, CELL), (CPD, CELL)],
        4, (2, N_Z * N_X, 2, N_Z * N_X),
        (offers, partial.reshape(GROUPS, *rows), smoothing, energy),
    )
    force, density = force_call(pairs, taken, pair_count, view, coef, rho, active, own, 32, 128)
    accel = comm_call(
        settle_kernel, 2, shape(3, CPD, CELL),
        [(N_Z * N_X, 3, *rows), (2, 3, *rows), (CPD // 8, 3, *rows)],
        2, (2, N_Z * N_X),
        (offers, force),
    )
    live = jnp.arange(CELL, dtype=jnp.int32)[None, :] < active[:, None]
    return density, jnp.where(live[:, None, :], accel.transpose(1, 0, 2), 0.0)


def solution(mesh):
    in_specs = (
        P(("slab", "dom"), None, None),
        P(("slab", "dom"), None),
        P(("slab", "dom"), None),
        P(("slab", "dom")),
        P(("slab", "dom"), None),
        P(("slab", "dom"), None, None),
        P(("slab", "dom"), None, None),
        P(("slab", "dom")),
    )
    out_specs = (P(("slab", "dom"), None), P(("slab", "dom"), None, None))
    return jax.shard_map(
        per_device, mesh=mesh, in_specs=in_specs, out_specs=out_specs, check_vma=False
    )
```

```python
import functools
import jax
import jax.numpy as jnp
import numpy as np
from jax import lax
from jax.experimental import pallas as pl
from jax.experimental.pallas import tpu as pltpu
from jax.sharding import PartitionSpec as P

CELL, CPD, NVIEW, GROUPS, PAIRS = 128, 32, 304, 38, 448
NORM = 21.0 / (2.0 * 3.141592653589793)
BF = jnp.bfloat16
F32 = jnp.float32
TINY = 1e-30
N_Z, N_X, N_SLAB = 8, 4, 8
MESH = pl.DeviceIdType.MESH
DEPTH = 80
NT = (((1,), (1,)), ((), ()))


def tables():
    sel = np.zeros((DEPTH, 32), np.float32)
    first, second, third, one = 0, 8, 24, 4
    for c in range(3):
        for part, base in ((first, 0), (second, 16), (third, 32)):
            sel[base + c, part + c] = -0.5
            sel[base + 5 + c, part + c] = -0.5
        sel[8 + c, first + c] = -0.5
        sel[24 + c, second + c] = -0.5
        sel[40 + c, first + c] = -0.5
        for base in (48, 56, 72):
            sel[base + c, one] = 1.0
    sel[3, one] = sel[11, one] = sel[12, one] = sel[43, one] = 1.0
    sel[4, first + 3] = sel[20, second + 3] = sel[36, third + 3] = 1.0
    return (jnp.asarray(sel, BF),)


def build_constants(shift, scale):
    row = lax.broadcasted_iota(jnp.int32, (8, CELL), 0)
    none = jnp.zeros((8, CELL), F32)
    for d in range(28):
        offset = (d // 9 - 1, d // 3 % 3 - 1, d % 3 - 1) if d < 27 else (0, 0, 0)
        length = sum(o * o for o in offset) if d < 27 else 16384
        moved, turned = none, none
        for c, o in enumerate(offset):
            if o:
                moved = jnp.where(row == 5 + c, -2.0 * o, moved)
                turned = jnp.where(row == c, -1.0 * o, turned)
        far = jnp.where(row == 4, 1.0 * length, none)
        shift[d] = jnp.concatenate([moved, far, moved, none], axis=0).astype(BF)
        scale[d] = jnp.concatenate([turned, turned, none, turned], axis=0).astype(BF)


def build_eye(eye):
    down = lax.broadcasted_iota(jnp.int32, (CELL, CELL), 0)
    across = lax.broadcasted_iota(jnp.int32, (CELL, CELL), 1)
    eye[...] = jnp.where(down == across, 1.0, 0.0).astype(BF)


def view_row(view, c, v):
    return view[v // 8, c, pl.ds(lax.rem(v, 8), 1), :]


def spread_columns(planes, put):
    turned = jnp.concatenate(planes, axis=0).T

    def some(g, turned):
        for k in range(8):
            for c in range(4):
                column = turned[:, c * CPD + k : c * CPD + k + 1]
                put(g * 8 + k, c, jnp.broadcast_to(column, (CELL, CELL)))
        return pltpu.roll(turned, CELL - 8, 1)

    lax.fori_loop(0, CPD // 8, some, turned)


def row_sums(load):
    lane = lax.broadcasted_iota(jnp.int32, (CELL, CELL), 1)

    def some(g, table):
        for k in range(16):
            u = g * 16 + k
            table = jnp.where(lane == u, jnp.sum(load(u), axis=1, keepdims=True), table)
        return table

    return lax.fori_loop(0, CPD // 16, some, jnp.zeros((CELL, CELL), F32)).T[0:CPD]


def own_plane(ref, *at):
    return jnp.concatenate([ref[(g, *at)] for g in range(CPD // 8)], axis=0)


def build_left(vv, sel, eye, at):
    def some(g, _):
        for k in range(16):
            u = g * 16 + k
            picked = jnp.dot(sel[...], vv[u], preferred_element_type=F32).astype(BF)
            cols = lax.dot_general(eye[...], picked, NT, preferred_element_type=F32)
            at[u] = cols.astype(BF)
        return 0

    lax.fori_loop(0, CPD // 16, some, 0)


def sweep(total, place, fill, use, buffers):
    half = len(buffers) // 2
    sides = buffers[:half], buffers[half:]

    def some(i, _):
        for side in (0, 1):
            for s in range(half):
                p = (2 * i + side) * half + s
                fill(sides[1 - side][s], place(p + half))
                use(place(p), sides[side][s])
        return 0

    for s in range(half):
        fill(sides[0][s], place(s))
    lax.fori_loop(0, pl.cdiv(total, 2 * half), some, 0)


def build_cell_tables(view, vv, groups=GROUPS):
    row = lax.broadcasted_iota(jnp.int32, (8, CELL), 0)

    def one_cell(g, k):
        x, y, z = (
            jnp.broadcast_to(view[g, c, pl.ds(k, 1), :], (8, CELL)) - 0.5 for c in range(3)
        )
        n = x * x + y * y + z * z
        w = jnp.where(row == 3, n, jnp.where(row == 4, 1.0, 0.0))
        w = jnp.where(row == 0, -2.0 * x, w)
        w = jnp.where(row == 1, -2.0 * y, w)
        w = jnp.where(row == 2, -2.0 * z, w)
        t1 = w.astype(BF).astype(F32)
        r1 = w - t1
        t2 = r1.astype(BF).astype(F32)
        t3 = r1 - t2
        return jnp.concatenate([t1, t2, t1, t3], axis=0).astype(BF)

    def two_groups(i, _):
        for k in range(16):
            g = i * 2 + k // 8
            vv[g * 8 + k % 8] = one_cell(g, k % 8)
        return 0

    lax.fori_loop(0, groups // 2, two_groups, 0)


def right_operand(vv, shift, scale, v, d):
    cell = vv[v]
    moved = cell + shift[d]
    turned = cell * scale[d]
    return jnp.concatenate([moved[:16], moved[:16], moved[16:], turned], axis=0)


def dist2(at, vv, shift, scale, u, v, d):
    return jnp.dot(
        at[u], right_operand(vv, shift, scale, v, d), preferred_element_type=F32
    )


def root(r2):
    r2 = jnp.maximum(r2, TINY)
    return r2 * lax.rsqrt(r2)


def fold_rows(w):
    return jnp.sum(w.reshape(-1, 8, CELL), axis=0)


def scalars(pairs, wanted, count, p):
    p = jnp.minimum(p, PAIRS - 1) if not isinstance(p, int) else p
    u, v = pairs[0, 0, p], pairs[1, 0, p]
    d = jnp.where(p < count, pairs[2, 0, p], 27)
    slot = jnp.clip(v - CPD, 0, 255)
    q = slot >> 3
    offered = CPD + (q & 3) * 64 + (q >> 2) * 8 + wanted[slot & 7, q]
    v = jnp.where((v >= CPD) & (v < CPD + 256), offered, v)
    return u, v, d


def self_densities(view, vv, at, sums):
    def some(g, _):
        for k in range(8):
            u = g * 8 + k
            cell = vv[u]
            right = jnp.concatenate([cell[:16], cell[:16], cell[16:]], axis=0)
            r = root(jnp.dot(at[u, :, 0:48], right, preferred_element_type=F32))
            h = jnp.broadcast_to(view[g, 3, k : k + 1, :], (CELL, CELL))
            f = jnp.maximum(h - r, 0.0)
            f2 = f * f
            sums[u] = fold_rows(f2 * f2 * (1.25 * h - f))
        return 0

    lax.fori_loop(0, CPD // 8, some, 0)


def density_kernel(
    unroll, rows,
    pairs, wanted, count, view_in, at_in, self_in, hb_in, out,
    shift, scale, vv, at, hb, hq, acc_l, acc_r, view, came, *buffers,
):
    coming = pltpu.make_async_copy(view_in, view, came.at[0])
    coming.start()
    handed = [
        pltpu.make_async_copy(at_in, at, came.at[1]),
        pltpu.make_async_copy(self_in, acc_r.at[pl.ds(0, CPD)], came.at[2]),
        pltpu.make_async_copy(hb_in, hb, came.at[3]),
    ]
    for copy in handed:
        copy.start()
    build_constants(shift, scale)

    def clear(g, _):
        acc_r[pl.ds(g * 8, 8)] = jnp.zeros((8, 8, CELL), F32)
        return 0

    lax.fori_loop(CPD // 8, GROUPS, clear, 0)
    coming.wait()
    build_cell_tables(view, vv)


    for copy in handed:
        copy.wait()

    def prepare(u, _):
        hq[u] = 1.25 * hb[u]
        acc_l[u] = jnp.zeros((CELL, CELL), F32)
        return 0

    lax.fori_loop(0, CPD, prepare, 0)

    d2 = functools.partial(dist2, at, vv, shift, scale)
    chunks = range(CELL // rows)

    def fill(buffer, where):
        buffer[...] = d2(*where)

    n = count[0]
    place = functools.partial(scalars, pairs, wanted, n)

    def tile(where, r2):
        u, v, _ = where
        h_r = jnp.broadcast_to(view_row(view, 3, v), (rows, CELL))
        q_r = 1.25 * h_r
        total = acc_r[v]
        for c in chunks:
            at_rows = pl.ds(c * rows, rows)
            r = root(r2[c * rows : c * rows + rows, :])
            f = jnp.maximum(hb[u, at_rows, :] - r, 0.0)
            f2 = f * f
            acc_l[u, at_rows, :] += f2 * f2 * (hq[u, at_rows, :] - f)
            f = jnp.maximum(h_r - r, 0.0)
            f2 = f * f
            total += fold_rows(f2 * f2 * (q_r - f))
        acc_r[v] = total

    sweep(n, place, fill, tile, buffers)

    def finish(g, _):
        for h in range(2):
            at_rows = pl.ds((g * 2 + h) * 8, 8)
            out[at_rows, :] = jnp.sum(acc_r[at_rows], axis=1)
        return 0

    lax.fori_loop(0, GROUPS // 2, finish, 0)
    out[0:CPD, :] += row_sums(lambda u: acc_l[u])


def force_kernel(
    unroll, rows,
    pairs, wanted, count, active, view_in, coef_in, rho_in, at_in, hb_in, out, density,
    shift, scale, vv, at, hb, cb, xb, acc_l, acc_r, view, coef, rho, came, *buffers,
):
    coming = [
        pltpu.make_async_copy(src, dst, came.at[i])
        for i, (src, dst) in enumerate(((view_in, view), (coef_in, coef), (rho_in, rho)))
    ]
    handed = [
        pltpu.make_async_copy(at_in, at, came.at[3]),
        pltpu.make_async_copy(hb_in, hb, came.at[4]),
    ]
    for copy in coming + handed:
        copy.start()
    build_constants(shift, scale)

    def clear(g, _):
        for c in range(4):
            acc_r[c, pl.ds(g * 8, 8)] = jnp.zeros((8, 8, CELL), F32)
        return 0

    lax.fori_loop(0, GROUPS, clear, 0)
    acc_l[...] = jnp.zeros(acc_l.shape, F32)
    for copy in coming:
        copy.wait()
    row = lax.broadcasted_iota(jnp.int32, (CPD, CELL), 0)
    live = jnp.zeros((CPD, CELL), jnp.int32)
    for u in range(CPD):
        live = jnp.where(row == u, active[u], live)
    lane = lax.broadcasted_iota(jnp.int32, (CPD, CELL), 1)
    density[...] = jnp.where(lane < live, rho[...], 0.0)
    build_cell_tables(view, vv)


    def put(u, c, column):
        if c == 3:
            cb[u] = column
        else:
            xb[u, c] = column

    spread_columns([own_plane(view, c) - 0.5 for c in range(3)] + [own_plane(coef)], put)
    for copy in handed:
        copy.wait()
    d2 = functools.partial(dist2, at, vv, shift, scale)
    chunks = range(CELL // rows)

    def tile(both, where, r2):
        u, v, d = where
        h_r = jnp.broadcast_to(view_row(view, 3, v), (rows, CELL))
        c_r = jnp.broadcast_to(coef[v // 8, pl.ds(lax.rem(v, 8), 1), :], (rows, CELL))
        total = [jnp.zeros((8, CELL), F32)] * 4
        tops, rests = [], []
        for k in chunks:
            at_rows = pl.ds(k * rows, rows)
            r = root(r2[k * rows : k * rows + rows, :])
            f = jnp.maximum(hb[u, at_rows, :] - r, 0.0)
            s = f * f * (f * cb[u, at_rows, :])
            f = jnp.maximum(h_r - r, 0.0)
            s += f * f * (f * c_r)
            for c in range(3):
                total[c] += fold_rows(s * xb[u, c, at_rows, :])
            total[3] += fold_rows(s)
            if both:
                top = s.astype(BF)
                tops.append(top)
                rests.append((s - top.astype(F32)).astype(BF))
        if both:
            right = vv[v, 0:16, :] + shift[d, 0:16, :]
            acc_l[u] += lax.dot_general(
                jnp.concatenate([right, right], axis=1),
                jnp.concatenate(
                    [jnp.concatenate(tops, axis=0), jnp.concatenate(rests, axis=0)], axis=1
                ),
                NT,
                preferred_element_type=F32,
            )
        offset = (d // 9 - 1, lax.rem(d // 3, 3) - 1, lax.rem(d, 3) - 1)
        for c in range(3):
            acc_r[c, v] += total[c] - offset[c].astype(F32) * total[3]
        acc_r[3, v] += total[3]

    def fill(buffer, where):
        buffer[...] = d2(*where)

    def self_place(p):
        u = jnp.minimum(p, CPD - 1)
        return u, u, jnp.int32(13)

    sweep(CPD, self_place, fill, functools.partial(tile, False), buffers[:CPD])

    n = count[0]
    place = functools.partial(scalars, pairs, wanted, n)

    sweep(n, place, fill, functools.partial(tile, True), buffers)

    def finish(g, _):
        whole = jnp.sum(acc_r[3, pl.ds(g * 8, 8)], axis=1)
        for c in range(3):
            out[g, c] = (view[g, c] - 0.5) * whole - jnp.sum(acc_r[c, pl.ds(g * 8, 8)], axis=1)
        return 0

    lax.fori_loop(0, GROUPS, finish, 0)
    for g in range(CPD // 8):
        rows_of = lambda r: jnp.concatenate(
            [acc_l[g * 8 + k, r : r + 1, :] for k in range(8)], axis=0
        )
        whole = rows_of(4)
        for c in range(3):
            moved = rows_of(c) + rows_of(8 + c) + rows_of(5 + c)
            out[g, c] += (view[g, c] - 0.5) * whole + 0.5 * moved


SMEM = pl.BlockSpec(memory_space=pltpu.SMEM)
VMEM = pl.BlockSpec(memory_space=pltpu.VMEM)
ANY = pl.BlockSpec(memory_space=pl.ANY)


def density_call(pairs, wanted, count, view, own, unroll=2, rows=64):
    return pl.pallas_call(
        functools.partial(density_kernel, unroll, rows),
        out_shape=jax.ShapeDtypeStruct((NVIEW, CELL), F32),
        in_specs=[SMEM] * 3 + [ANY] * 4,
        out_specs=VMEM,
        scratch_shapes=[
            pltpu.VMEM((28, 32, CELL), BF),
            pltpu.VMEM((28, 32, CELL), BF),
            pltpu.VMEM((NVIEW, 32, CELL), BF),
            pltpu.VMEM((CPD, CELL, DEPTH), BF),
            pltpu.VMEM((CPD, CELL, CELL), F32),
            pltpu.VMEM((CPD, CELL, CELL), F32),
            pltpu.VMEM((CPD, CELL, CELL), F32),
            pltpu.VMEM((NVIEW, 8, CELL), F32),
            pltpu.VMEM((GROUPS, 4, 8, CELL), F32),
            pltpu.SemaphoreType.DMA((4,)),
        ]
        + [pltpu.VMEM((CELL, CELL), F32)] * unroll,
        compiler_params=pltpu.CompilerParams(vmem_limit_bytes=62 << 20),
        name="density_pairs",
    )(pairs, wanted, count, view, *own)


def force_call(pairs, wanted, count, view, coef, rho, active, own, unroll=2, rows=64):
    return pl.pallas_call(
        functools.partial(force_kernel, unroll, rows),
        out_shape=(
            jax.ShapeDtypeStruct((GROUPS, 3, 8, CELL), F32),
            jax.ShapeDtypeStruct((CPD, CELL), F32),
        ),
        in_specs=[SMEM] * 4 + [ANY] * 5,
        out_specs=(VMEM, VMEM),
        scratch_shapes=[
            pltpu.VMEM((28, 32, CELL), BF),
            pltpu.VMEM((28, 32, CELL), BF),
            pltpu.VMEM((NVIEW, 32, CELL), BF),
            pltpu.VMEM((CPD, CELL, DEPTH), BF),
            pltpu.VMEM((CPD, CELL, CELL), F32),
            pltpu.VMEM((CPD, CELL, CELL), F32),
            pltpu.VMEM((CPD, 3, CELL, CELL), F32),
            pltpu.VMEM((CPD, 16, CELL), F32),
            pltpu.VMEM((4, NVIEW, 8, CELL), F32),
            pltpu.VMEM((GROUPS, 4, 8, CELL), F32),
            pltpu.VMEM((GROUPS, 8, CELL), F32),
            pltpu.VMEM((CPD, CELL), F32),
            pltpu.SemaphoreType.DMA((5,)),
        ]
        + [pltpu.VMEM((CELL, CELL), F32)] * unroll,
        compiler_params=pltpu.CompilerParams(vmem_limit_bytes=62 << 20),
        name="force_pairs",
    )(pairs, wanted, count, active, view, coef, rho, own[0], own[2])


def spot():
    t = lax.axis_index("dom")
    return t // N_X, lax.rem(t, N_X), lax.axis_index("slab")


def group_of(z, x):
    return CPD // 8 + x * N_Z + z


def barrier(steps, meanwhile=lambda: None):
    z, x, s = spot()
    sem = pltpu.get_barrier_semaphore()
    peers = [{"dom": peer_at(z + i, x + j)} for i, j in steps]
    peers += [{"slab": (s + k) & (N_SLAB - 1)} for k in (1, N_SLAB - 1)]
    for peer in peers:
        pl.semaphore_signal(sem, inc=1, device_id=peer, device_id_type=MESH)
    meanwhile()
    pl.semaphore_wait(sem, len(peers))


def peer_at(z, x):
    return (z & (N_Z - 1)) * N_X + (x & (N_X - 1))


def far_first(steps):
    return sorted(steps, key=lambda at: -min(at[0], N_Z - at[0]) - min(at[1], N_X - at[1]))


ALL_STEPS = far_first((i, j) for i in range(N_Z) for j in range(N_X) if i or j)
AXIS_STEPS = far_first((i, j) for i, j in ALL_STEPS if i == 0 or j == 0)


def copy_to(src, dst, sems, k, peer):
    return pltpu.make_async_remote_copy(
        src_ref=src, dst_ref=dst, send_sem=sems[0].at[k], recv_sem=sems[1].at[k],
        device_id=peer, device_id_type=MESH,
    )


def z_copies(refs, sems):
    z, x, _ = spot()
    out = []
    for k in (4, 3, 5, 2, 6, 1, 7):
        to = (z + k) & (N_Z - 1)
        out.append((k, copy_to(*refs(to), sems, k, {"dom": to * N_X + x})))
    return dict(out)


def x_copies(refs, sems, base=0):
    z, x, _ = spot()
    out = []
    for k in (2, 1, 3):
        to = (x + k) & (N_X - 1)
        out.append(copy_to(*refs(to), sems, base + k, {"dom": z * N_X + to}))
    return out


def peer_copies(refs, sems):
    z, x, _ = spot()
    out = []
    for i, j in ALL_STEPS:
        group = group_of((z + i) & (N_Z - 1), (x + j) & (N_X - 1))
        out.append(
            copy_to(*refs(group), sems, i * N_X + j, {"dom": peer_at(z + i, x + j)})
        )
    return out


def face_copies(lower, upper, sems):
    s = lax.axis_index("slab")
    return [
        copy_to(*lower, sems, 0, {"slab": (s + N_SLAB - 1) & (N_SLAB - 1)}),
        copy_to(*upper, sems, 1, {"slab": (s + 1) & (N_SLAB - 1)}),
    ]


def start(copies):
    for copy in copies:
        copy.start()


def arrive(copies):
    for copy in copies:
        copy.wait_recv()


def leave(copies):
    for copy in copies:
        copy.wait_send()


def leave_local(copies):
    for copy in copies:
        copy.wait()


def pack(boundary, positions, smoothing, view, mine, offered, here, local):
    leave_local(local)
    for g in range(CPD // 8):
        for c in range(3):
            view[g, c] = positions[c, g * 8 : g * 8 + 8, :]
            mine[g, c] = positions[c, g * 8 : g * 8 + 8, :]
        view[g, 3] = smoothing[g * 8 : g * 8 + 8, :]
        mine[g, 3] = smoothing[g * 8 : g * 8 + 8, :]
    for b in range(8):
        cell = boundary[b]
        for c in range(3):
            offered[c, b : b + 1, :] = positions[c, pl.ds(cell, 1), :]
        offered[3, b : b + 1, :] = smoothing[pl.ds(cell, 1), :]
    view[here] = offered[...]


def gather_kernel(
    boundary, positions_in, smoothing_in, sel, view, at_out, self_out, hb_out,
    offered, positions, smoothing, mine, sums, hb, vv, at, eye, near, *sems,
):
    z, x, _ = spot()
    local = [
        pltpu.make_async_copy(positions_in, positions, near.at[0]),
        pltpu.make_async_copy(smoothing_in, smoothing, near.at[1]),
    ]
    start(local)
    here = group_of(z, x)
    barrier(AXIS_STEPS, lambda: pack(boundary, positions, smoothing, view, mine, offered, here, local))
    face_sems, z_sems, x_sems = sems[:2], sems[2:4], sems[4:6]
    along_z = z_copies(lambda to: (offered, view.at[here]), z_sems)
    faces = face_copies(
        (view.at[0], view.at[GROUPS - 1]), (view.at[CPD // 8 - 1], view.at[GROUPS - 2]), face_sems
    )
    start(along_z.values())
    along_x = x_copies(lambda to: (offered, view.at[here]), x_sems)
    start(along_x)
    start(faces)
    for k in (1, 7, 2, 6, 3, 5, 4):
        along_z[k].wait_recv()
        block = view.at[group_of((z - k) & (N_Z - 1), x)]
        onward = x_copies(lambda to: (block, block), x_sems, k * N_X)
        start(onward)
        along_x += onward
    build_eye(eye)
    build_cell_tables(mine, vv, CPD // 8)
    build_left(vv, sel, eye, at)
    self_densities(mine, vv, at, sums)

    def put(u, c, column):
        if c == 0:
            hb[u] = column

    spread_columns([own_plane(mine, 3)] * 4, put)
    handed = [
        pltpu.make_async_copy(at, at_out, near.at[2]),
        pltpu.make_async_copy(sums, self_out, near.at[3]),
        pltpu.make_async_copy(hb, hb_out, near.at[4]),
    ]
    start(handed)
    arrive(along_x + faces)
    leave(list(along_z.values()) + along_x + faces)
    leave_local(handed)


def settle(own, arrived, lower, upper, boundary):
    row = lax.broadcasted_iota(jnp.int32, (CPD, CELL), 0)
    for b in range(8):
        own += jnp.where(row == boundary[b], jnp.broadcast_to(arrived[b : b + 1], own.shape), 0.0)
    return jnp.concatenate([own[:8] + lower, own[8:24], own[24:] + upper], axis=0)


def sum_back(partial, arrived, faces, face_sems, sems, near):
    z, x, _ = spot()
    here = group_of(z, x)
    copies = peer_copies(lambda group: (partial.at[group], arrived.at[here - CPD // 8]), sems)
    copies += face_copies(
        (partial.at[GROUPS - 2], faces.at[1]), (partial.at[GROUPS - 1], faces.at[0]), face_sems
    )
    start(copies)
    mine = pltpu.make_async_copy(partial.at[here], arrived.at[here - CPD // 8], near)
    mine.start()
    mine.wait()
    arrive(copies)
    total = arrived[0]
    for k in range(1, N_Z * N_X):
        total += arrived[k]
    return total, copies


def factor_kernel(
    boundary, partial, smoothing_in, energy_in, rho, coef,
    arrived, faces, offered, mine, own, smoothing, energy, near, *sems,
):
    z, x, _ = spot()
    local = [
        pltpu.make_async_copy(src, dst, near.at[i])
        for i, (src, dst) in enumerate(
            ((partial.at[pl.ds(0, CPD // 8)], own), (smoothing_in, smoothing), (energy_in, energy))
        )
    ]
    start(local)
    barrier(ALL_STEPS)
    total, copies = sum_back(partial, arrived, faces, sems[0:2], sems[2:4], near.at[3])
    leave_local(local)
    h2 = smoothing[...] * smoothing[...]
    h4 = h2 * h2
    inverse = 1.0 / (h4 * h4)
    raw = settle(own[...].reshape(CPD, CELL), total, faces[0], faces[1], boundary)
    density = (4.0 * NORM / CELL) * inverse * raw
    rho[...] = density
    slope = (40.0 / 3.0 * NORM / CELL) * inverse * energy[...] / density
    for g in range(CPD // 8):
        coef[g] = slope[g * 8 : g * 8 + 8]
    mine[...] = slope
    for b in range(8):
        offered[b : b + 1, :] = mine[pl.ds(boundary[b], 1), :]
    here = group_of(z, x)
    coef[here] = offered[...]
    back = peer_copies(lambda group: (offered, coef.at[here]), sems[6:8])
    back += face_copies(
        (coef.at[0], coef.at[GROUPS - 1]), (coef.at[CPD // 8 - 1], coef.at[GROUPS - 2]), sems[4:6]
    )
    start(back)
    leave(copies)
    arrive(back)
    leave(back)


def settle_kernel(boundary, partial, accel, arrived, faces, own, near, *sems):
    local = [pltpu.make_async_copy(partial.at[pl.ds(0, CPD // 8)], own, near.at[0])]
    start(local)
    barrier(ALL_STEPS)
    total, copies = sum_back(partial, arrived, faces, sems[0:2], sems[2:4], near.at[1])
    leave_local(local)
    for c in range(3):
        kept = jnp.concatenate([own[g, c] for g in range(CPD // 8)], axis=0)
        accel[c] = settle(kept, total[c], faces[0, c], faces[1, c], boundary)
    leave(copies)


LEFT_SCRATCH = ((CPD, 32, CELL), (CPD, CELL, DEPTH), (CELL, CELL))


def comm_call(kernel, collective, out_shape, scratch, n_near, n_sems, operands, more=None):
    return pl.pallas_call(
        kernel,
        out_shape=out_shape,
        in_specs=[SMEM] + [ANY] * (len(operands) - 1) + [VMEM] * len(more or ()),
        out_specs=(VMEM, ANY, ANY, ANY) if more else jax.tree.map(lambda _: VMEM, out_shape),
        scratch_shapes=[pltpu.VMEM(dims, F32) for dims in scratch]
        + [pltpu.VMEM(dims, BF) for dims in (LEFT_SCRATCH if more else ())]
        + [pltpu.SemaphoreType.DMA((n_near,))]
        + [pltpu.SemaphoreType.DMA((n,)) for n in n_sems for _ in (0, 1)],
        compiler_params=pltpu.CompilerParams(collective_id=collective, has_side_effects=True),
        name=kernel.__name__,
    )(*operands, *(more or ()))


def per_device(positions, smoothing, energy, active, boundary, wanted, cell_pairs, pair_count):
    offers = boundary[0]
    pairs = cell_pairs.transpose(2, 0, 1)
    taken = wanted[0].T
    shape = lambda *dims: jax.ShapeDtypeStruct(dims, F32)
    rows = (8, CELL)
    view, *own = comm_call(
        gather_kernel, 0,
        (
            shape(GROUPS, 4, *rows),
            jax.ShapeDtypeStruct((CPD, CELL, DEPTH), BF),
            shape(CPD, *rows),
            shape(CPD, CELL, CELL),
        ),
        [(4, *rows), (3, CPD, CELL), (CPD, CELL), (CPD // 8, 4, *rows), (CPD, *rows),
         (CPD, CELL, CELL)], 5,
        (2, N_Z, N_Z * N_X),
        (offers, positions.transpose(1, 0, 2), smoothing),
        tables(),
    )
    partial = density_call(pairs, taken, pair_count, view, own, 32, 128)
    rho, coef = comm_call(
        factor_kernel, 1, (shape(CPD, CELL), shape(GROUPS, *rows)),
        [(N_Z * N_X, *rows), (2, *rows), rows, (CPD, CELL), (CPD // 8, *rows), (CPD, CELL), (CPD, CELL)],
        4, (2, N_Z * N_X, 2, N_Z * N_X),
        (offers, partial.reshape(GROUPS, *rows), smoothing, energy),
    )
    force, density = force_call(pairs, taken, pair_count, view, coef, rho, active, own, 32, 128)
    accel = comm_call(
        settle_kernel, 2, shape(3, CPD, CELL),
        [(N_Z * N_X, 3, *rows), (2, 3, *rows), (CPD // 8, 3, *rows)],
        2, (2, N_Z * N_X),
        (offers, force),
    )
    live = jnp.arange(CELL, dtype=jnp.int32)[None, :] < active[:, None]
    return density, jnp.where(live[:, None, :], accel.transpose(1, 0, 2), 0.0)


def solution(mesh):
    in_specs = (
        P(("slab", "dom"), None, None),
        P(("slab", "dom"), None),
        P(("slab", "dom"), None),
        P(("slab", "dom")),
        P(("slab", "dom"), None),
        P(("slab", "dom"), None, None),
        P(("slab", "dom"), None, None),
        P(("slab", "dom")),
    )
    out_specs = (P(("slab", "dom"), None), P(("slab", "dom"), None, None))
    return jax.shard_map(
        per_device, mesh=mesh, in_specs=in_specs, out_specs=out_specs, check_vma=False
    )
```

```python
import functools
import jax
import jax.numpy as jnp
import numpy as np
from jax import lax
from jax.experimental import pallas as pl
from jax.experimental.pallas import tpu as pltpu
from jax.sharding import PartitionSpec as P

CELL, CPD, NVIEW, GROUPS, PAIRS = 128, 32, 304, 38, 448
NORM = 21.0 / (2.0 * 3.141592653589793)
BF = jnp.bfloat16
F32 = jnp.float32
TINY = 1e-30
N_Z, N_X, N_SLAB = 8, 4, 8
MESH = pl.DeviceIdType.MESH
DEPTH = 80
NT = (((1,), (1,)), ((), ()))


def tables():
    sel = np.zeros((DEPTH, 32), np.float32)
    first, second, third, one = 0, 8, 24, 4
    for c in range(3):
        for part, base in ((first, 0), (second, 16), (third, 32)):
            sel[base + c, part + c] = -0.5
            sel[base + 5 + c, part + c] = -0.5
        sel[8 + c, first + c] = -0.5
        sel[24 + c, second + c] = -0.5
        sel[40 + c, first + c] = -0.5
        for base in (48, 56, 72):
            sel[base + c, one] = 1.0
    sel[3, one] = sel[11, one] = sel[12, one] = sel[43, one] = 1.0
    sel[4, first + 3] = sel[20, second + 3] = sel[36, third + 3] = 1.0
    return (jnp.asarray(sel, BF),)


def build_constants(shift, scale):
    row = lax.broadcasted_iota(jnp.int32, (8, CELL), 0)
    none = jnp.zeros((8, CELL), F32)
    for d in range(28):
        offset = (d // 9 - 1, d // 3 % 3 - 1, d % 3 - 1) if d < 27 else (0, 0, 0)
        length = sum(o * o for o in offset) if d < 27 else 16384
        moved, turned = none, none
        for c, o in enumerate(offset):
            if o:
                moved = jnp.where(row == 5 + c, -2.0 * o, moved)
                turned = jnp.where(row == c, -1.0 * o, turned)
        far = jnp.where(row == 4, 1.0 * length, none)
        shift[d] = jnp.concatenate([moved, far, moved, none], axis=0).astype(BF)
        scale[d] = jnp.concatenate([turned, turned, none, turned], axis=0).astype(BF)


def build_eye(eye):
    down = lax.broadcasted_iota(jnp.int32, (CELL, CELL), 0)
    across = lax.broadcasted_iota(jnp.int32, (CELL, CELL), 1)
    eye[...] = jnp.where(down == across, 1.0, 0.0).astype(BF)


def view_row(view, c, v):
    return view[v // 8, c, pl.ds(lax.rem(v, 8), 1), :]


def spread_columns(planes, put):
    turned = jnp.concatenate(planes, axis=0).T

    def some(g, turned):
        for k in range(8):
            for c in range(4):
                column = turned[:, c * CPD + k : c * CPD + k + 1]
                put(g * 8 + k, c, jnp.broadcast_to(column, (CELL, CELL)))
        return pltpu.roll(turned, CELL - 8, 1)

    lax.fori_loop(0, CPD // 8, some, turned)


def row_sums(load):
    lane = lax.broadcasted_iota(jnp.int32, (CELL, CELL), 1)

    def some(g, table):
        for k in range(16):
            u = g * 16 + k
            table = jnp.where(lane == u, jnp.sum(load(u), axis=1, keepdims=True), table)
        return table

    return lax.fori_loop(0, CPD // 16, some, jnp.zeros((CELL, CELL), F32)).T[0:CPD]


def own_plane(ref, *at):
    return jnp.concatenate([ref[(g, *at)] for g in range(CPD // 8)], axis=0)


def build_left(vv, sel, eye, at):
    def some(g, _):
        for k in range(16):
            u = g * 16 + k
            picked = jnp.dot(sel[...], vv[u], preferred_element_type=F32).astype(BF)
            cols = lax.dot_general(eye[...], picked, NT, preferred_element_type=F32)
            at[u] = cols.astype(BF)
        return 0

    lax.fori_loop(0, CPD // 16, some, 0)


def sweep(total, place, fill, use, buffers):
    half = len(buffers) // 2
    sides = buffers[:half], buffers[half:]

    def some(i, _):
        for side in (0, 1):
            for s in range(half):
                p = (2 * i + side) * half + s
                fill(sides[1 - side][s], place(p + half))
                use(place(p), sides[side][s])
        return 0

    for s in range(half):
        fill(sides[0][s], place(s))
    lax.fori_loop(0, pl.cdiv(total, 2 * half), some, 0)


def build_cell_tables(view, vv, groups=GROUPS):
    row = lax.broadcasted_iota(jnp.int32, (8, CELL), 0)

    def one_cell(g, k):
        x, y, z = (
            jnp.broadcast_to(view[g, c, pl.ds(k, 1), :], (8, CELL)) - 0.5 for c in range(3)
        )
        n = x * x + y * y + z * z
        w = jnp.where(row == 3, n, jnp.where(row == 4, 1.0, 0.0))
        w = jnp.where(row == 0, -2.0 * x, w)
        w = jnp.where(row == 1, -2.0 * y, w)
        w = jnp.where(row == 2, -2.0 * z, w)
        t1 = w.astype(BF).astype(F32)
        r1 = w - t1
        t2 = r1.astype(BF).astype(F32)
        t3 = r1 - t2
        return jnp.concatenate([t1, t2, t1, t3], axis=0).astype(BF)

    def two_groups(i, _):
        for k in range(16):
            g = i * 2 + k // 8
            vv[g * 8 + k % 8] = one_cell(g, k % 8)
        return 0

    lax.fori_loop(0, groups // 2, two_groups, 0)


def right_operand(vv, shift, scale, v, d):
    cell = vv[v]
    moved = cell + shift[d]
    turned = cell * scale[d]
    return jnp.concatenate([moved[:16], moved[:16], moved[16:], turned], axis=0)


def dist2(at, vv, shift, scale, u, v, d):
    return jnp.dot(
        at[u], right_operand(vv, shift, scale, v, d), preferred_element_type=F32
    )


def root(r2):
    r2 = jnp.maximum(r2, TINY)
    return r2 * lax.rsqrt(r2)


def fold_rows(w):
    return jnp.sum(w.reshape(-1, 8, CELL), axis=0)


def scalars(pairs, wanted, count, p):
    p = jnp.minimum(p, PAIRS - 1) if not isinstance(p, int) else p
    u, v = pairs[0, 0, p], pairs[1, 0, p]
    d = jnp.where(p < count, pairs[2, 0, p], 27)
    slot = jnp.clip(v - CPD, 0, 255)
    q = slot >> 3
    offered = CPD + (q & 3) * 64 + (q >> 2) * 8 + wanted[slot & 7, q]
    v = jnp.where((v >= CPD) & (v < CPD + 256), offered, v)
    return u, v, d


def self_densities(view, vv, at, sums):
    def some(g, _):
        for k in range(8):
            u = g * 8 + k
            cell = vv[u]
            right = jnp.concatenate([cell[:16], cell[:16], cell[16:]], axis=0)
            r = root(jnp.dot(at[u, :, 0:48], right, preferred_element_type=F32))
            h = jnp.broadcast_to(view[g, 3, k : k + 1, :], (CELL, CELL))
            f = jnp.maximum(h - r, 0.0)
            f2 = f * f
            sums[u] = fold_rows(f2 * f2 * (1.25 * h - f))
        return 0

    lax.fori_loop(0, CPD // 8, some, 0)


def density_kernel(
    unroll, rows,
    pairs, wanted, count, view_in, at_in, self_in, hb_in, out,
    shift, scale, vv, at, hb, hq, acc_l, acc_r, view, came, *buffers,
):
    coming = pltpu.make_async_copy(view_in, view, came.at[0])
    coming.start()
    handed = [
        pltpu.make_async_copy(at_in, at, came.at[1]),
        pltpu.make_async_copy(self_in, acc_r.at[pl.ds(0, CPD)], came.at[2]),
        pltpu.make_async_copy(hb_in, hb, came.at[3]),
    ]
    for copy in handed:
        copy.start()
    build_constants(shift, scale)

    def clear(g, _):
        acc_r[pl.ds(g * 8, 8)] = jnp.zeros((8, 8, CELL), F32)
        return 0

    lax.fori_loop(CPD // 8, GROUPS, clear, 0)

    def clear_left(g, _):
        acc_l[pl.ds(g * 4, 4)] = jnp.zeros((4, CELL, CELL), F32)
        return 0

    lax.fori_loop(0, CPD // 4, clear_left, 0)
    coming.wait()
    build_cell_tables(view, vv)
    for copy in handed:
        copy.wait()

    def prepare(g, _):
        hq[pl.ds(g * 4, 4)] = 1.25 * hb[pl.ds(g * 4, 4)]
        return 0

    lax.fori_loop(0, CPD // 4, prepare, 0)

    d2 = functools.partial(dist2, at, vv, shift, scale)
    chunks = range(CELL // rows)

    def fill(buffer, where):
        buffer[...] = d2(*where)

    n = count[0]
    place = functools.partial(scalars, pairs, wanted, n)

    def tile(where, r2):
        u, v, _ = where
        h_r = jnp.broadcast_to(view_row(view, 3, v), (rows, CELL))
        q_r = 1.25 * h_r
        total = acc_r[v]
        for c in chunks:
            at_rows = pl.ds(c * rows, rows)
            r = root(r2[c * rows : c * rows + rows, :])
            f = jnp.maximum(hb[u, at_rows, :] - r, 0.0)
            f2 = f * f
            acc_l[u, at_rows, :] += f2 * f2 * (hq[u, at_rows, :] - f)
            f = jnp.maximum(h_r - r, 0.0)
            f2 = f * f
            total += fold_rows(f2 * f2 * (q_r - f))
        acc_r[v] = total

    sweep(n, place, fill, tile, buffers)

    def finish(g, _):
        for h in range(2):
            at_rows = pl.ds((g * 2 + h) * 8, 8)
            out[at_rows, :] = jnp.sum(acc_r[at_rows], axis=1)
        return 0

    lax.fori_loop(0, GROUPS // 2, finish, 0)
    out[0:CPD, :] += row_sums(lambda u: acc_l[u])


def force_kernel(
    unroll, rows,
    pairs, wanted, count, active, view_in, coef_in, rho_in, at_in, hb_in, out, density,
    shift, scale, vv, at, hb, cb, xb, acc_l, acc_r, view, coef, rho, came, *buffers,
):
    coming = [
        pltpu.make_async_copy(src, dst, came.at[i])
        for i, (src, dst) in enumerate(((view_in, view), (coef_in, coef), (rho_in, rho)))
    ]
    handed = [
        pltpu.make_async_copy(at_in, at, came.at[3]),
        pltpu.make_async_copy(hb_in, hb, came.at[4]),
    ]
    for copy in coming + handed:
        copy.start()
    build_constants(shift, scale)

    def clear(g, _):
        for c in range(4):
            acc_r[c, pl.ds(g * 8, 8)] = jnp.zeros((8, 8, CELL), F32)
        return 0

    lax.fori_loop(0, GROUPS, clear, 0)
    acc_l[...] = jnp.zeros(acc_l.shape, F32)
    for copy in coming:
        copy.wait()
    row = lax.broadcasted_iota(jnp.int32, (CPD, CELL), 0)
    live = jnp.zeros((CPD, CELL), jnp.int32)
    for u in range(CPD):
        live = jnp.where(row == u, active[u], live)
    lane = lax.broadcasted_iota(jnp.int32, (CPD, CELL), 1)
    density[...] = jnp.where(lane < live, rho[...], 0.0)
    build_cell_tables(view, vv)


    def put(u, c, column):
        if c == 3:
            cb[u] = column
        else:
            xb[u, c] = column

    spread_columns([own_plane(view, c) - 0.5 for c in range(3)] + [own_plane(coef)], put)
    for copy in handed:
        copy.wait()
    d2 = functools.partial(dist2, at, vv, shift, scale)
    chunks = range(CELL // rows)

    def tile(both, where, r2):
        u, v, d = where
        h_r = jnp.broadcast_to(view_row(view, 3, v), (rows, CELL))
        c_r = jnp.broadcast_to(coef[v // 8, pl.ds(lax.rem(v, 8), 1), :], (rows, CELL))
        total = [jnp.zeros((8, CELL), F32)] * 4
        tops, rests = [], []
        for k in chunks:
            at_rows = pl.ds(k * rows, rows)
            r = root(r2[k * rows : k * rows + rows, :])
            f = jnp.maximum(hb[u, at_rows, :] - r, 0.0)
            s = f * f * (f * cb[u, at_rows, :])
            f = jnp.maximum(h_r - r, 0.0)
            s += f * f * (f * c_r)
            for c in range(3):
                total[c] += fold_rows(s * xb[u, c, at_rows, :])
            total[3] += fold_rows(s)
            if both:
                top = s.astype(BF)
                tops.append(top)
                rests.append((s - top.astype(F32)).astype(BF))
        if both:
            right = vv[v, 0:16, :] + shift[d, 0:16, :]
            acc_l[u] += lax.dot_general(
                jnp.concatenate([right, right], axis=1),
                jnp.concatenate(
                    [jnp.concatenate(tops, axis=0), jnp.concatenate(rests, axis=0)], axis=1
                ),
                NT,
                preferred_element_type=F32,
            )
        offset = (d // 9 - 1, lax.rem(d // 3, 3) - 1, lax.rem(d, 3) - 1)
        for c in range(3):
            acc_r[c, v] += total[c] - offset[c].astype(F32) * total[3]
        acc_r[3, v] += total[3]

    def fill(buffer, where):
        buffer[...] = d2(*where)

    def self_place(p):
        u = jnp.minimum(p, CPD - 1)
        return u, u, jnp.int32(13)

    sweep(CPD, self_place, fill, functools.partial(tile, False), buffers[:CPD])

    n = count[0]
    place = functools.partial(scalars, pairs, wanted, n)

    sweep(n, place, fill, functools.partial(tile, True), buffers)

    def finish(g, _):
        whole = jnp.sum(acc_r[3, pl.ds(g * 8, 8)], axis=1)
        for c in range(3):
            out[g, c] = (view[g, c] - 0.5) * whole - jnp.sum(acc_r[c, pl.ds(g * 8, 8)], axis=1)
        return 0

    lax.fori_loop(0, GROUPS, finish, 0)
    for g in range(CPD // 8):
        rows_of = lambda r: jnp.concatenate(
            [acc_l[g * 8 + k, r : r + 1, :] for k in range(8)], axis=0
        )
        whole = rows_of(4)
        for c in range(3):
            moved = rows_of(c) + rows_of(8 + c) + rows_of(5 + c)
            out[g, c] += (view[g, c] - 0.5) * whole + 0.5 * moved


SMEM = pl.BlockSpec(memory_space=pltpu.SMEM)
VMEM = pl.BlockSpec(memory_space=pltpu.VMEM)
ANY = pl.BlockSpec(memory_space=pl.ANY)


def density_call(pairs, wanted, count, view, own, unroll=2, rows=64):
    return pl.pallas_call(
        functools.partial(density_kernel, unroll, rows),
        out_shape=jax.ShapeDtypeStruct((NVIEW, CELL), F32),
        in_specs=[SMEM] * 3 + [ANY] * 4,
        out_specs=VMEM,
        scratch_shapes=[
            pltpu.VMEM((28, 32, CELL), BF),
            pltpu.VMEM((28, 32, CELL), BF),
            pltpu.VMEM((NVIEW, 32, CELL), BF),
            pltpu.VMEM((CPD, CELL, DEPTH), BF),
            pltpu.VMEM((CPD, CELL, CELL), F32),
            pltpu.VMEM((CPD, CELL, CELL), F32),
            pltpu.VMEM((CPD, CELL, CELL), F32),
            pltpu.VMEM((NVIEW, 8, CELL), F32),
            pltpu.VMEM((GROUPS, 4, 8, CELL), F32),
            pltpu.SemaphoreType.DMA((4,)),
        ]
        + [pltpu.VMEM((CELL, CELL), F32)] * unroll,
        compiler_params=pltpu.CompilerParams(vmem_limit_bytes=62 << 20),
        name="density_pairs",
    )(pairs, wanted, count, view, *own)


def force_call(pairs, wanted, count, view, coef, rho, active, own, unroll=2, rows=64):
    return pl.pallas_call(
        functools.partial(force_kernel, unroll, rows),
        out_shape=(
            jax.ShapeDtypeStruct((GROUPS, 3, 8, CELL), F32),
            jax.ShapeDtypeStruct((CPD, CELL), F32),
        ),
        in_specs=[SMEM] * 4 + [ANY] * 5,
        out_specs=(VMEM, VMEM),
        scratch_shapes=[
            pltpu.VMEM((28, 32, CELL), BF),
            pltpu.VMEM((28, 32, CELL), BF),
            pltpu.VMEM((NVIEW, 32, CELL), BF),
            pltpu.VMEM((CPD, CELL, DEPTH), BF),
            pltpu.VMEM((CPD, CELL, CELL), F32),
            pltpu.VMEM((CPD, CELL, CELL), F32),
            pltpu.VMEM((CPD, 3, CELL, CELL), F32),
            pltpu.VMEM((CPD, 16, CELL), F32),
            pltpu.VMEM((4, NVIEW, 8, CELL), F32),
            pltpu.VMEM((GROUPS, 4, 8, CELL), F32),
            pltpu.VMEM((GROUPS, 8, CELL), F32),
            pltpu.VMEM((CPD, CELL), F32),
            pltpu.SemaphoreType.DMA((5,)),
        ]
        + [pltpu.VMEM((CELL, CELL), F32)] * unroll,
        compiler_params=pltpu.CompilerParams(vmem_limit_bytes=62 << 20),
        name="force_pairs",
    )(pairs, wanted, count, active, view, coef, rho, own[0], own[2])


def spot():
    t = lax.axis_index("dom")
    return t // N_X, lax.rem(t, N_X), lax.axis_index("slab")


def group_of(z, x):
    return CPD // 8 + x * N_Z + z


def barrier(steps, meanwhile=lambda: None):
    z, x, s = spot()
    sem = pltpu.get_barrier_semaphore()
    peers = [{"dom": peer_at(z + i, x + j)} for i, j in steps]
    peers += [{"slab": (s + k) & (N_SLAB - 1)} for k in (1, N_SLAB - 1)]
    for peer in peers:
        pl.semaphore_signal(sem, inc=1, device_id=peer, device_id_type=MESH)
    meanwhile()
    pl.semaphore_wait(sem, len(peers))


def peer_at(z, x):
    return (z & (N_Z - 1)) * N_X + (x & (N_X - 1))


def far_first(steps):
    return sorted(steps, key=lambda at: -min(at[0], N_Z - at[0]) - min(at[1], N_X - at[1]))


ALL_STEPS = far_first((i, j) for i in range(N_Z) for j in range(N_X) if i or j)
AXIS_STEPS = far_first((i, j) for i, j in ALL_STEPS if i == 0 or j == 0)


def copy_to(src, dst, sems, k, peer):
    return pltpu.make_async_remote_copy(
        src_ref=src, dst_ref=dst, send_sem=sems[0].at[k], recv_sem=sems[1].at[k],
        device_id=peer, device_id_type=MESH,
    )


def z_copies(refs, sems):
    z, x, _ = spot()
    out = []
    for k in (4, 3, 5, 2, 6, 1, 7):
        to = (z + k) & (N_Z - 1)
        out.append((k, copy_to(*refs(to), sems, k, {"dom": to * N_X + x})))
    return dict(out)


def x_copies(refs, sems, base=0):
    z, x, _ = spot()
    out = []
    for k in (2, 1, 3):
        to = (x + k) & (N_X - 1)
        out.append(copy_to(*refs(to), sems, base + k, {"dom": z * N_X + to}))
    return out


def peer_copies(refs, sems):
    z, x, _ = spot()
    out = []
    for i, j in ALL_STEPS:
        group = group_of((z + i) & (N_Z - 1), (x + j) & (N_X - 1))
        out.append(
            copy_to(*refs(group), sems, i * N_X + j, {"dom": peer_at(z + i, x + j)})
        )
    return out


def face_copies(lower, upper, sems):
    s = lax.axis_index("slab")
    return [
        copy_to(*lower, sems, 0, {"slab": (s + N_SLAB - 1) & (N_SLAB - 1)}),
        copy_to(*upper, sems, 1, {"slab": (s + 1) & (N_SLAB - 1)}),
    ]


def start(copies):
    for copy in copies:
        copy.start()


def arrive(copies):
    for copy in copies:
        copy.wait_recv()


def leave(copies):
    for copy in copies:
        copy.wait_send()


def leave_local(copies):
    for copy in copies:
        copy.wait()


def pack(boundary, positions, smoothing, view, mine, offered, here, local):
    leave_local(local)
    for g in range(CPD // 8):
        for c in range(3):
            view[g, c] = positions[c, g * 8 : g * 8 + 8, :]
            mine[g, c] = positions[c, g * 8 : g * 8 + 8, :]
        view[g, 3] = smoothing[g * 8 : g * 8 + 8, :]
        mine[g, 3] = smoothing[g * 8 : g * 8 + 8, :]
    for b in range(8):
        cell = boundary[b]
        for c in range(3):
            offered[c, b : b + 1, :] = positions[c, pl.ds(cell, 1), :]
        offered[3, b : b + 1, :] = smoothing[pl.ds(cell, 1), :]
    view[here] = offered[...]


def gather_kernel(
    boundary, positions_in, smoothing_in, sel, view, at_out, self_out, hb_out,
    offered, positions, smoothing, mine, sums, hb, vv, at, eye, near, *sems,
):
    z, x, _ = spot()
    local = [
        pltpu.make_async_copy(positions_in, positions, near.at[0]),
        pltpu.make_async_copy(smoothing_in, smoothing, near.at[1]),
    ]
    start(local)
    here = group_of(z, x)
    barrier(AXIS_STEPS, lambda: pack(boundary, positions, smoothing, view, mine, offered, here, local))
    face_sems, z_sems, x_sems = sems[:2], sems[2:4], sems[4:6]
    along_z = z_copies(lambda to: (offered, view.at[here]), z_sems)
    faces = face_copies(
        (view.at[0], view.at[GROUPS - 1]), (view.at[CPD // 8 - 1], view.at[GROUPS - 2]), face_sems
    )
    start(along_z.values())
    along_x = x_copies(lambda to: (offered, view.at[here]), x_sems)
    start(along_x)
    start(faces)
    for k in (1, 7, 2, 6, 3, 5, 4):
        along_z[k].wait_recv()
        block = view.at[group_of((z - k) & (N_Z - 1), x)]
        onward = x_copies(lambda to: (block, block), x_sems, k * N_X)
        start(onward)
        along_x += onward
    build_eye(eye)
    build_cell_tables(mine, vv, CPD // 8)
    build_left(vv, sel, eye, at)
    self_densities(mine, vv, at, sums)

    def put(u, c, column):
        if c == 0:
            hb[u] = column

    spread_columns([own_plane(mine, 3)] * 4, put)
    handed = [
        pltpu.make_async_copy(at, at_out, near.at[2]),
        pltpu.make_async_copy(sums, self_out, near.at[3]),
        pltpu.make_async_copy(hb, hb_out, near.at[4]),
    ]
    start(handed)
    arrive(along_x + faces)
    leave(list(along_z.values()) + along_x + faces)
    leave_local(handed)


def settle(own, arrived, lower, upper, boundary):
    row = lax.broadcasted_iota(jnp.int32, (CPD, CELL), 0)
    for b in range(8):
        own += jnp.where(row == boundary[b], jnp.broadcast_to(arrived[b : b + 1], own.shape), 0.0)
    return jnp.concatenate([own[:8] + lower, own[8:24], own[24:] + upper], axis=0)


def sum_back(partial, arrived, faces, face_sems, sems, near):
    z, x, _ = spot()
    here = group_of(z, x)
    copies = peer_copies(lambda group: (partial.at[group], arrived.at[here - CPD // 8]), sems)
    copies += face_copies(
        (partial.at[GROUPS - 2], faces.at[1]), (partial.at[GROUPS - 1], faces.at[0]), face_sems
    )
    start(copies)
    mine = pltpu.make_async_copy(partial.at[here], arrived.at[here - CPD // 8], near)
    mine.start()
    mine.wait()
    arrive(copies)
    total = arrived[0]
    for k in range(1, N_Z * N_X):
        total += arrived[k]
    return total, copies


def factor_kernel(
    boundary, partial, smoothing_in, energy_in, rho, coef,
    arrived, faces, offered, mine, own, smoothing, energy, near, *sems,
):
    z, x, _ = spot()
    local = [
        pltpu.make_async_copy(src, dst, near.at[i])
        for i, (src, dst) in enumerate(
            ((partial.at[pl.ds(0, CPD // 8)], own), (smoothing_in, smoothing), (energy_in, energy))
        )
    ]
    start(local)
    barrier(ALL_STEPS)
    total, copies = sum_back(partial, arrived, faces, sems[0:2], sems[2:4], near.at[3])
    leave_local(local)
    h2 = smoothing[...] * smoothing[...]
    h4 = h2 * h2
    inverse = 1.0 / (h4 * h4)
    raw = settle(own[...].reshape(CPD, CELL), total, faces[0], faces[1], boundary)
    density = (4.0 * NORM / CELL) * inverse * raw
    rho[...] = density
    slope = (40.0 / 3.0 * NORM / CELL) * inverse * energy[...] / density
    for g in range(CPD // 8):
        coef[g] = slope[g * 8 : g * 8 + 8]
    mine[...] = slope
    for b in range(8):
        offered[b : b + 1, :] = mine[pl.ds(boundary[b], 1), :]
    here = group_of(z, x)
    coef[here] = offered[...]
    back = peer_copies(lambda group: (offered, coef.at[here]), sems[6:8])
    back += face_copies(
        (coef.at[0], coef.at[GROUPS - 1]), (coef.at[CPD // 8 - 1], coef.at[GROUPS - 2]), sems[4:6]
    )
    start(back)
    leave(copies)
    arrive(back)
    leave(back)


def settle_kernel(boundary, partial, accel, arrived, faces, own, near, *sems):
    local = [pltpu.make_async_copy(partial.at[pl.ds(0, CPD // 8)], own, near.at[0])]
    start(local)
    barrier(ALL_STEPS)
    total, copies = sum_back(partial, arrived, faces, sems[0:2], sems[2:4], near.at[1])
    leave_local(local)
    for c in range(3):
        kept = jnp.concatenate([own[g, c] for g in range(CPD // 8)], axis=0)
        accel[c] = settle(kept, total[c], faces[0, c], faces[1, c], boundary)
    leave(copies)


LEFT_SCRATCH = ((CPD, 32, CELL), (CPD, CELL, DEPTH), (CELL, CELL))


def comm_call(kernel, collective, out_shape, scratch, n_near, n_sems, operands, more=None):
    return pl.pallas_call(
        kernel,
        out_shape=out_shape,
        in_specs=[SMEM] + [ANY] * (len(operands) - 1) + [VMEM] * len(more or ()),
        out_specs=(VMEM, ANY, ANY, ANY) if more else jax.tree.map(lambda _: VMEM, out_shape),
        scratch_shapes=[pltpu.VMEM(dims, F32) for dims in scratch]
        + [pltpu.VMEM(dims, BF) for dims in (LEFT_SCRATCH if more else ())]
        + [pltpu.SemaphoreType.DMA((n_near,))]
        + [pltpu.SemaphoreType.DMA((n,)) for n in n_sems for _ in (0, 1)],
        compiler_params=pltpu.CompilerParams(collective_id=collective, has_side_effects=True),
        name=kernel.__name__,
    )(*operands, *(more or ()))


def per_device(positions, smoothing, energy, active, boundary, wanted, cell_pairs, pair_count):
    offers = boundary[0]
    pairs = cell_pairs.transpose(2, 0, 1)
    taken = wanted[0].T
    shape = lambda *dims: jax.ShapeDtypeStruct(dims, F32)
    rows = (8, CELL)
    view, *own = comm_call(
        gather_kernel, 0,
        (
            shape(GROUPS, 4, *rows),
            jax.ShapeDtypeStruct((CPD, CELL, DEPTH), BF),
            shape(CPD, *rows),
            shape(CPD, CELL, CELL),
        ),
        [(4, *rows), (3, CPD, CELL), (CPD, CELL), (CPD // 8, 4, *rows), (CPD, *rows),
         (CPD, CELL, CELL)], 5,
        (2, N_Z, N_Z * N_X),
        (offers, positions.transpose(1, 0, 2), smoothing),
        tables(),
    )
    partial = density_call(pairs, taken, pair_count, view, own, 32, 128)
    rho, coef = comm_call(
        factor_kernel, 1, (shape(CPD, CELL), shape(GROUPS, *rows)),
        [(N_Z * N_X, *rows), (2, *rows), rows, (CPD, CELL), (CPD // 8, *rows), (CPD, CELL), (CPD, CELL)],
        4, (2, N_Z * N_X, 2, N_Z * N_X),
        (offers, partial.reshape(GROUPS, *rows), smoothing, energy),
    )
    force, density = force_call(pairs, taken, pair_count, view, coef, rho, active, own, 32, 128)
    accel = comm_call(
        settle_kernel, 2, shape(3, CPD, CELL),
        [(N_Z * N_X, 3, *rows), (2, 3, *rows), (CPD // 8, 3, *rows)],
        2, (2, N_Z * N_X),
        (offers, force),
    )
    live = jnp.arange(CELL, dtype=jnp.int32)[None, :] < active[:, None]
    return density, jnp.where(live[:, None, :], accel.transpose(1, 0, 2), 0.0)


def solution(mesh):
    in_specs = (
        P(("slab", "dom"), None, None),
        P(("slab", "dom"), None),
        P(("slab", "dom"), None),
        P(("slab", "dom")),
        P(("slab", "dom"), None),
        P(("slab", "dom"), None, None),
        P(("slab", "dom"), None, None),
        P(("slab", "dom")),
    )
    out_specs = (P(("slab", "dom"), None), P(("slab", "dom"), None, None))
    return jax.shard_map(
        per_device, mesh=mesh, in_specs=in_specs, out_specs=out_specs, check_vma=False
    )
```
